32 devices in a mesh: dp: 8 (over z, x), tensor: 4 (over y, core).
Axes of the slice: x: 2, y: 2, z: 4, core: 2. Of those that a mesh axis runs over, the one named last changes fastest.
Arguments:
- tokens: bfloat16 [16384, 1024], P(('dp', 'tensor')), may hold values from -6 to 6
- cotangent: bfloat16 [16384, 1024], P(('dp', 'tensor')), may hold values from -6 to 6
- attention_gain: float32 [1024], replicated, may hold values from 0.5 to 1.5
- feedforward_gain: float32 [1024], replicated, may hold values from 0.5 to 1.5
- query_key_value_matrix: bfloat16 [3, 1024, 1024], P(None, 'dp', 'tensor'), may hold values from -0.1875 to 0.1875
- output_matrix: bfloat16 [1024, 1024], P('tensor', 'dp'), may hold values from -0.5 to 0.5
- feedforward_matrix: bfloat16 [2, 1024, 2816], P(None, 'dp', 'tensor'), may hold values from -0.1875 to 0.1875
- down_matrix: bfloat16 [2816, 1024], P('tensor', 'dp'), may hold values from -0.109375 to 0.109375
- memory_retention: float32 [8], replicated, may hold values from 0.3 to 0.98
- memory_step_size: float32 [8], replicated, may hold values from 0.2 to 0.9
- sequence_length: int32 [24], replicated, may hold values from 64 to 1920, as said below
- sequence_permutation: int32 [24], replicated, may hold values from 0 to 23, as said below
- sequence_adapter: int32 [24], replicated, may hold values from 0 to 7
- head_span_window: int32 [8], replicated, may hold values from 256 to 1024, as said below
- query_key_value_lower: bfloat16 [3, 1024, 128], P(None, ('dp', 'tensor')), may hold values from -0.1875 to 0.1875
- query_key_value_upper: bfloat16 [3, 128, 1024], P(None, None, ('dp', 'tensor')), may hold values from -0.75 to 0.75
- output_adapter_lower: bfloat16 [1024, 128], P(('dp', 'tensor')), may hold values from -0.1875 to 0.1875
- output_adapter_upper: bfloat16 [128, 1024], P(None, ('dp', 'tensor')), may hold values from -0.75 to 0.75
- feedforward_adapter_lower: bfloat16 [2, 1024, 128], P(None, ('dp', 'tensor')), may hold values from -0.1875 to 0.1875
- feedforward_adapter_upper: bfloat16 [2, 128, 2816], P(None, None, ('dp', 'tensor')), may hold values from -0.75 to 0.75
- down_adapter_lower: bfloat16 [2816, 128], P(('dp', 'tensor')), may hold values from -0.109375 to 0.109375
- down_adapter_upper: bfloat16 [128, 1024], P(None, ('dp', 'tensor')), may hold values from -0.75 to 0.75
Outputs:
- mixed: bfloat16 [16384, 1024], P(('dp', 'tensor'))
- token_grad: bfloat16 [16384, 1024], P(('dp', 'tensor'))
- qkv_lora_a_grad: float32 [3, 1024, 128], P(None, ('dp', 'tensor'))
- qkv_lora_b_grad: float32 [3, 128, 1024], P(None, None, ('dp', 'tensor'))
- out_lora_a_grad: float32 [1024, 128], P(('dp', 'tensor'))
- out_lora_b_grad: float32 [128, 1024], P(None, ('dp', 'tensor'))
- ffn_lora_a_grad: float32 [2, 1024, 128], P(None, ('dp', 'tensor'))
- ffn_lora_b_grad: float32 [2, 128, 2816], P(None, None, ('dp', 'tensor'))
- down_lora_a_grad: float32 [2816, 128], P(('dp', 'tensor'))
- down_lora_b_grad: float32 [128, 1024], P(None, ('dp', 'tensor'))
The draws below stay inside these ranges and needn't reach their ends.
Inputs may be any that keep to these rules, and one draw needn't show every extreme that they name: `sequence_length`: multiples of 64; the 3 sequences that sequence_permutation lists for a group sum to 2048. `sequence_permutation`: a permutation of the sequence numbers. `head_span_window`: multiples of 256.
All inputs are finite; a program needn't handle non-finite values.
Results may differ from the reference program's by a relative error of at most 0.02.
Values may be sent and summed in bfloat16 or wider, within the bound.
No kernel may reach another device: no remote copies, remote signals or barrier semaphores. Data moves between devices by JAX's collectives and lax.ppermute only.
A program may use at most 192 MiB of HBM per device.

```python
import jax
import jax.numpy as jnp
from jax import lax

MODEL_WIDTH = 1024
HEADS = 8
HEAD_DIM = 128
HIDDEN_UNITS = 2816
ADAPT = 8
ADAPTER_RANK = 16
STRETCH = 64
WIN_MAX = 1024
QBLK = 512
SEQ_G = 3
TOK_DEV = 512
ADAPTER_COLUMNS = 128
TOK_GROUP = 2048
TOKENS = 16384
SEQS = 24
N_DP = 8
N_TENSOR = 4


def seq_plan(key):
    groups_count = SEQS // SEQ_G
    units = TOK_GROUP // STRETCH
    short_most = max(1, units // 16)
    key_short, key_place, key_perm, key_pick = jax.random.split(key, 4)
    shorts = jax.random.randint(key_short, (groups_count, SEQ_G - 1), 1, short_most + 1)
    picked = jax.random.randint(key_pick, (), 0, groups_count)
    shorts = jnp.where(jnp.arange(groups_count)[:, None] == picked, 1, shorts)
    longest = units - jnp.sum(shorts, 1, keepdims=True)
    place = jax.random.randint(key_place, (groups_count, 1), 0, SEQ_G)
    slots = jnp.arange(SEQ_G, dtype=jnp.int32)[None, :]
    short_slot = jnp.clip(slots - (slots > place).astype(jnp.int32), 0, SEQ_G - 2)
    short_pick = jnp.take_along_axis(shorts, jnp.broadcast_to(short_slot, (groups_count, SEQ_G)), 1)
    stream_lengths = jnp.where(slots == place, longest, short_pick).reshape(-1) * STRETCH
    permuted = jax.random.permutation(key_perm, SEQS).astype(jnp.int32)
    lengths = jnp.zeros((SEQS,), jnp.int32).at[permuted].set(stream_lengths.astype(jnp.int32))
    return (lengths, permuted)


def draw_sequence_length(key, part):
    return seq_plan(key)[0]


def draw_sequence_permutation(key, part):
    return seq_plan(key)[1]


def draw_head_span_window(key, part):
    key = jax.random.fold_in(key, 7)
    key_level, key_widest, key_narrow = jax.random.split(key, 3)
    levels = jax.random.randint(key_level, (HEADS,), 1, 5)
    widest = jax.random.randint(key_widest, (), 0, HEADS)
    narrowest = (widest + 1 + jax.random.randint(key_narrow, (), 0, HEADS - 1)) % HEADS
    head_ids = jnp.arange(HEADS)
    levels = jnp.where(head_ids == widest, 4, levels)
    levels = jnp.where(head_ids == narrowest, 1, levels)
    return (levels * (WIN_MAX // 4)).astype(jnp.int32)


def with_ends(result, stream_key, low, high):
    shape = result.shape
    spot = [jax.random.randint(jax.random.fold_in(stream_key, axis), (), 0, shape[axis]) for axis in range(len(shape))]
    result = result.at[tuple(spot)].set(low)
    longest = shape.index(max(shape))
    spot[longest] = (spot[longest] + 1) % shape[longest]
    return result.at[tuple(spot)].set(high)


def block_scale(stream_key, shape, shards, smallest, high):
    def one(axis_at, parts):
        draws = jax.random.uniform(jax.random.fold_in(jax.random.fold_in(stream_key, 6), axis_at), (parts,), jnp.float32, smallest / len(shards), high / len(shards))
        return jnp.repeat(jnp.exp(draws), shape[axis_at] // parts).reshape((-1,) + (1,) * (len(shape) - axis_at - 1))

    factor_of = one(*shards[0])
    for cut in shards[1:]:
        factor_of = factor_of * one(*cut)
    return factor_of


def noise(stream_key, dims, scale, reach, pieces=(), kind=jnp.bfloat16):
    values = scale * jax.random.normal(stream_key, dims, jnp.float32)
    if pieces:
        values = values * block_scale(stream_key, dims, pieces, -0.22, 0.18)
    return jnp.clip(values, -reach, reach).astype(kind)


def setup_inputs(seed: int = 0) -> dict:
    splits = jax.random.split(jax.random.key(seed), 23)
    return {
        "tokens": noise(splits[0], (TOKENS, MODEL_WIDTH), 1.0, 6.0, ((0, 32),)),
        "cotangent": noise(splits[1], (TOKENS, MODEL_WIDTH), 1.0, 6.0, ((0, 32),)),
        "attention_gain": jnp.clip(1.0 + 0.1 * jax.random.normal(splits[2], (MODEL_WIDTH,), jnp.float32), 0.5, 1.5),
        "feedforward_gain": jnp.clip(1.0 + 0.1 * jax.random.normal(splits[3], (MODEL_WIDTH,), jnp.float32), 0.5, 1.5),
        "query_key_value_matrix": noise(splits[4], (3, MODEL_WIDTH, MODEL_WIDTH), MODEL_WIDTH ** -0.5, 0.1875, ((1, 8), (2, 4))),
        "output_matrix": noise(splits[5], (MODEL_WIDTH, MODEL_WIDTH), (MODEL_WIDTH // 8) ** -0.5, 0.5, ((0, 4), (1, 8))),
        "feedforward_matrix": noise(splits[6], (2, MODEL_WIDTH, HIDDEN_UNITS), MODEL_WIDTH ** -0.5, 0.1875, ((1, 8), (2, 4))),
        "down_matrix": noise(splits[7], (HIDDEN_UNITS, MODEL_WIDTH), HIDDEN_UNITS ** -0.5, 0.109375, ((0, 4), (1, 8))),
        "memory_retention": jnp.clip(jax.random.uniform(splits[8], (HEADS,), jnp.float32, 0.3, 0.98), 0.3, 0.98),
        "memory_step_size": jnp.clip(jax.random.uniform(splits[9], (HEADS,), jnp.float32, 0.2, 0.9), 0.2, 0.9),
        "sequence_length": draw_sequence_length(jax.random.fold_in(splits[22], 71), 0),
        "sequence_permutation": draw_sequence_permutation(jax.random.fold_in(splits[22], 71), 0),
        "sequence_adapter": with_ends(jax.random.randint(splits[12], (SEQS,), 0, ADAPT), jax.random.fold_in(splits[12], 1), 0, ADAPT - 1).astype(jnp.int32),
        "head_span_window": draw_head_span_window(jax.random.fold_in(splits[22], 71), 0),
        "query_key_value_lower": noise(splits[14], (3, MODEL_WIDTH, ADAPTER_COLUMNS), MODEL_WIDTH ** -0.5, 0.1875, ((1, 32),)),
        "query_key_value_upper": noise(splits[15], (3, ADAPTER_COLUMNS, MODEL_WIDTH), (4 * ADAPTER_RANK) ** -0.5, 0.75, ((2, 32),)),
        "output_adapter_lower": noise(splits[16], (MODEL_WIDTH, ADAPTER_COLUMNS), MODEL_WIDTH ** -0.5, 0.1875, ((0, 32),)),
        "output_adapter_upper": noise(splits[17], (ADAPTER_COLUMNS, MODEL_WIDTH), (4 * ADAPTER_RANK) ** -0.5, 0.75, ((1, 32),)),
        "feedforward_adapter_lower": noise(splits[18], (2, MODEL_WIDTH, ADAPTER_COLUMNS), MODEL_WIDTH ** -0.5, 0.1875, ((1, 32),)),
        "feedforward_adapter_upper": noise(splits[19], (2, ADAPTER_COLUMNS, HIDDEN_UNITS), (4 * ADAPTER_RANK) ** -0.5, 0.75, ((2, 32),)),
        "down_adapter_lower": noise(splits[20], (HIDDEN_UNITS, ADAPTER_COLUMNS), HIDDEN_UNITS ** -0.5, 0.109375, ((0, 32),)),
        "down_adapter_upper": noise(splits[21], (ADAPTER_COLUMNS, MODEL_WIDTH), (4 * ADAPTER_RANK) ** -0.5, 0.75, ((1, 32),)),
    }


@jax.custom_vjp
def lowered_value(v):
    return lax.optimization_barrier(v.astype(jnp.bfloat16)).astype(jnp.float32)

@jax.custom_vjp
def lowered_gradient(v):
    return v

def low_keep(v):
    return (lowered_value(v), None)

def low_pass(kept_values, grad):
    return (grad,)

def back_keep(v):
    return (v, None)

def back_low(kept_values, grad):
    return (lowered_value(grad),)
lowered_value.defvjp(low_keep, low_pass)
lowered_gradient.defvjp(back_keep, back_low)
highest = lax.Precision.HIGHEST
memory_gain = 32.0
epsilon = 1e-06

def matrix_product(left, right):
    return jnp.dot(left, right, precision=highest, preferred_element_type=jnp.float32)

def normalize(values, gain):
    return values * lax.rsqrt(lax.optimization_barrier(jnp.mean(values * values, -1, keepdims=True)) + epsilon) * gain

def pick_rows(lookup, wanted):
    hits = wanted[:, None] == jnp.arange(lookup.shape[0], dtype=jnp.int32)[None, :]
    return lax.optimization_barrier(jnp.sum(jnp.where(hits, lookup[None, :], 0), 1)).astype(jnp.int32)

def stream_layout(sequence_length, sequence_permutation, sequence_adapter, group_number, row_count):
    members = lax.dynamic_slice_in_dim(sequence_permutation, (group_number * SEQ_G).astype(jnp.int32), SEQ_G)
    member_length = pick_rows(sequence_length, members)
    member_adapter = pick_rows(sequence_adapter, members)
    begins = (jnp.cumsum(member_length) - member_length).astype(jnp.int32)
    positions = jnp.arange(row_count, dtype=jnp.int32)
    seq_index = (lax.optimization_barrier(jnp.sum((positions[:, None] >= begins[None, :]).astype(jnp.int32), 1)) - 1).astype(jnp.int32)
    return (seq_index, pick_rows(member_adapter, seq_index), pick_rows(begins, seq_index))

def adapter_mask(row_adapter):
    column_count = jnp.arange(ADAPTER_COLUMNS, dtype=jnp.int32)[None, :] // ADAPTER_RANK
    return (column_count == row_adapter[:, None]).astype(jnp.float32)

def to_streams(whole):
    slot_rows = TOK_DEV // N_DP
    shaped = whole.reshape(N_DP, N_TENSOR, N_DP, slot_rows, whole.shape[1])
    return jnp.transpose(shaped, (2, 1, 0, 3, 4)).reshape(N_DP, TOK_GROUP, whole.shape[1])

def from_streams(streams):
    slot_rows = TOK_DEV // N_DP
    shaped = streams.reshape(N_DP, N_TENSOR, N_DP, slot_rows, streams.shape[2])
    return jnp.transpose(shaped, (2, 1, 0, 3, 4)).reshape(TOKENS, streams.shape[2])

def widen_columns(input_rows, weight_matrix, adapter_lower, adapter_upper, expand_columns):
    latent_value = lowered_value(expand_columns * matrix_product(input_rows, adapter_lower))
    segment_width = adapter_upper.shape[1] // N_TENSOR
    segments = [matrix_product(lowered_gradient(latent_value), adapter_upper[:, member_sequence * segment_width:(member_sequence + 1) * segment_width]) for member_sequence in range(N_TENSOR)]
    return matrix_product(input_rows, weight_matrix) + jnp.concatenate(segments, 1)

def narrow_columns(input_rows, weight_matrix, adapter_lower, adapter_upper, expand_columns):
    segment_width = input_rows.shape[1] // N_TENSOR
    latent_value = jnp.zeros((input_rows.shape[0], adapter_lower.shape[1]), jnp.float32)
    for member_sequence in range(N_TENSOR):
        lower_precision = member_sequence * segment_width
        portion_latent = expand_columns * matrix_product(input_rows[:, lower_precision:lower_precision + segment_width], adapter_lower[lower_precision:lower_precision + segment_width])
        latent_value = latent_value + lowered_gradient(lowered_value(portion_latent))
    return matrix_product(input_rows, weight_matrix) + matrix_product(latent_value, adapter_upper)

def attention(queries, key_heads, value_heads, seq_index, windows):
    row_count, head_count, head_dim = queries.shape
    score_scale = head_dim ** (-0.5)
    key_span = QBLK + WIN_MAX
    padded_keys = jnp.pad(key_heads, ((WIN_MAX, 0), (0, 0), (0, 0)))
    padded_values = jnp.pad(value_heads, ((WIN_MAX, 0), (0, 0), (0, 0)))
    padded_seq = jnp.pad(seq_index, (WIN_MAX, 0), constant_values=-1)

    def block_out(number):
        first_row = number * QBLK
        query_block = lax.dynamic_slice_in_dim(queries, first_row, QBLK, 0)
        key_block = lax.dynamic_slice_in_dim(padded_keys, first_row, key_span, 0)
        value_block = lax.dynamic_slice_in_dim(padded_values, first_row, key_span, 0)
        distance = jnp.arange(QBLK, dtype=jnp.int32)[:, None] + WIN_MAX - jnp.arange(key_span, dtype=jnp.int32)[None, :]
        same_seq = lax.dynamic_slice_in_dim(seq_index, first_row, QBLK)[:, None] == lax.dynamic_slice_in_dim(padded_seq, first_row, key_span)[None, :]
        allowed = (distance >= 0)[None] & (distance[None] < windows[:, None, None]) & same_seq[None]
        scores = jnp.einsum('qhd,khd->hqk', query_block, key_block, precision=highest) * score_scale
        scores = jnp.where(allowed, lowered_gradient(scores), -1e+30)
        soft_weights = lowered_value(jax.nn.softmax(scores, -1))
        return jnp.einsum('hqk,khd->qhd', soft_weights, value_block, precision=highest)
    blocks = lax.map(jax.checkpoint(block_out), jnp.arange(row_count // QBLK, dtype=jnp.int32))
    return blocks.reshape(row_count, head_count, head_dim)

def memory_read(queries, key_heads, value_heads, decay_own, rate_own, stretch_first):
    row_count, head_count, head_dim = queries.shape
    query_unit = queries * lax.rsqrt(lax.optimization_barrier(jnp.sum(queries * queries, -1, keepdims=True)) + epsilon)
    key_unit = key_heads * lax.rsqrt(lax.optimization_barrier(jnp.sum(key_heads * key_heads, -1, keepdims=True)) + epsilon)
    stretches = row_count // STRETCH
    shaped = (stretches, STRETCH, head_count, head_dim)

    def advance(memory_state, input_rows):
        query_stretch, key_stretch, value_stretch, reset_flag = input_rows
        memory_state = jnp.where(reset_flag, jnp.zeros_like(memory_state), memory_state)
        read_out = jnp.einsum('thd,hde->the', query_stretch, memory_state, precision=highest)
        error_rows = jnp.einsum('thd,hde->the', key_stretch, memory_state, precision=highest) - value_stretch
        update = jnp.einsum('thd,the->hde', key_stretch, error_rows, precision=highest) / STRETCH
        memory_state = decay_own[:, None, None] * memory_state - rate_own[:, None, None] * update
        return (memory_state, read_out)
    initial = jnp.zeros((head_count, head_dim, head_dim), jnp.float32)
    final_state, reads = lax.scan(jax.checkpoint(advance), initial, (query_unit.reshape(shaped), key_unit.reshape(shaped), value_heads.reshape(shaped), stretch_first))
    return reads.reshape(row_count, head_count, head_dim)

def group_layer(stream, group_number, adapter_list, frozen):
    query_key_value_matrix, output_matrix, feedforward_matrix, down_matrix, attention_gain, feedforward_gain, memory_retention, memory_step_size, sequence_length, sequence_permutation, sequence_adapter, head_span_window = frozen
    qkv_a, qkv_b, out_a, out_b, ffn_a, ffn_b, down_a, down_b = adapter_list
    row_count = stream.shape[0]
    seq_index, row_adapter, row_begin = stream_layout(sequence_length, sequence_permutation, sequence_adapter, group_number, row_count)
    expand_columns = adapter_mask(row_adapter)
    stretch_first = row_begin.reshape(-1, STRETCH)[:, 0] == jnp.arange(row_count // STRETCH, dtype=jnp.int32) * STRETCH
    normed = lowered_value(normalize(stream, attention_gain))
    projected = [lowered_gradient(lowered_value(widen_columns(normed, query_key_value_matrix[member_sequence], qkv_a[member_sequence], qkv_b[member_sequence], expand_columns))) for member_sequence in range(3)]
    query_heads, key_heads, value_heads = [item.reshape(row_count, HEADS, HEAD_DIM) for item in projected]
    attended = attention(query_heads, key_heads, value_heads, seq_index, head_span_window)
    remembered = memory_read(query_heads, key_heads, value_heads, memory_retention, memory_step_size, stretch_first)
    heads = lowered_gradient(lowered_value(attended + memory_gain * remembered)).reshape(row_count, MODEL_WIDTH)
    hidden_one = stream + lowered_gradient(narrow_columns(heads, output_matrix, out_a, out_b, expand_columns))
    normed_two = lowered_value(normalize(hidden_one, feedforward_gain))
    gate_pre = lowered_gradient(widen_columns(normed_two, feedforward_matrix[0], ffn_a[0], ffn_b[0], expand_columns))
    up_pre = lowered_gradient(widen_columns(normed_two, feedforward_matrix[1], ffn_a[1], ffn_b[1], expand_columns))
    swiglu = lowered_value(jax.nn.silu(gate_pre) * up_pre)
    return hidden_one + lowered_gradient(narrow_columns(swiglu, down_matrix, down_a, down_b, expand_columns))

def forward_all(streams, adapter_list, frozen):

    def one_group(carried, input_rows):
        stream, group_number = input_rows
        return (carried, group_layer(stream, group_number, adapter_list, frozen))
    start_carry = jnp.zeros((), jnp.float32)
    final_carry, outputs = lax.scan(jax.checkpoint(one_group), start_carry, (streams, jnp.arange(N_DP, dtype=jnp.int32)))
    return outputs

def reference(tokens, cotangent, attention_gain, feedforward_gain, query_key_value_matrix, output_matrix, feedforward_matrix, down_matrix, memory_retention, memory_step_size, sequence_length, sequence_permutation, sequence_adapter, head_span_window, query_key_value_lower, query_key_value_upper, output_adapter_lower, output_adapter_upper, feedforward_adapter_lower, feedforward_adapter_upper, down_adapter_lower, down_adapter_upper):
    frozen = (query_key_value_matrix.astype(jnp.float32), output_matrix.astype(jnp.float32), feedforward_matrix.astype(jnp.float32), down_matrix.astype(jnp.float32), attention_gain, feedforward_gain, memory_retention, memory_step_size, sequence_length, sequence_permutation, sequence_adapter, head_span_window)
    adapter_list = (query_key_value_lower.astype(jnp.float32), query_key_value_upper.astype(jnp.float32), output_adapter_lower.astype(jnp.float32), output_adapter_upper.astype(jnp.float32), feedforward_adapter_lower.astype(jnp.float32), feedforward_adapter_upper.astype(jnp.float32), down_adapter_lower.astype(jnp.float32), down_adapter_upper.astype(jnp.float32))
    streams = to_streams(tokens.astype(jnp.float32))
    grad_streams = to_streams(cotangent.astype(jnp.float32))
    outputs, pullback = jax.vjp(lambda stream_all, adapter_all: forward_all(stream_all, adapter_all, frozen), streams, adapter_list)
    stream_grads, adapter_grads = pullback(grad_streams)
    mixed = from_streams(outputs).astype(jnp.bfloat16)
    token_grad = from_streams(stream_grads).astype(jnp.bfloat16)
    return (mixed, token_grad, adapter_grads[0], adapter_grads[1], adapter_grads[2], adapter_grads[3], adapter_grads[4], adapter_grads[5], adapter_grads[6], adapter_grads[7])
```

```python
import jax
import jax.numpy as jnp
from jax import lax
from jax.sharding import PartitionSpec as P

HEAD_DIM = 128
ADAPTER_RANK = 16
STRETCH = 64
WIN_MAX = 1024
QBLK = 512
SEQ_G = 3
ADAPTER_COLUMNS = 128


highest = lax.Precision.HIGHEST
memory_gain = 32.0
epsilon = 1e-06


def normalize(values, gain):
    return values * lax.rsqrt(jnp.mean(values * values, -1, keepdims=True) + epsilon) * gain


def pick_rows(lookup, wanted):
    hits = wanted[:, None] == jnp.arange(lookup.shape[0], dtype=jnp.int32)[None, :]
    return jnp.sum(jnp.where(hits, lookup[None, :], 0), 1)


def stream_layout(sequence_length, sequence_permutation, sequence_adapter, group_number, row_count):
    members = lax.dynamic_slice_in_dim(sequence_permutation, group_number * SEQ_G, SEQ_G)
    member_length = pick_rows(sequence_length, members)
    member_adapter = pick_rows(sequence_adapter, members)
    order = jnp.arange(SEQ_G, dtype=jnp.int32)
    begins = jnp.sum(jnp.where(order[None, :] < order[:, None], member_length[None, :], 0), 1)
    positions = jnp.arange(row_count, dtype=jnp.int32)
    seq_index = jnp.sum((positions[:, None] >= begins[None, :]).astype(jnp.int32), 1) - 1
    return (seq_index, pick_rows(member_adapter, seq_index), pick_rows(begins, seq_index))


def adapter_mask(row_adapter):
    column_count = jnp.arange(ADAPTER_COLUMNS, dtype=jnp.int32)[None, :] // ADAPTER_RANK
    return (column_count == row_adapter[:, None]).astype(jnp.float32)


def memory_read(queries, key_heads, value_heads, decay_own, rate_own, stretch_first):
    row_count, head_count, head_dim = queries.shape
    query_unit = queries * lax.rsqrt(jnp.sum(queries * queries, -1, keepdims=True) + epsilon)
    key_unit = key_heads * lax.rsqrt(jnp.sum(key_heads * key_heads, -1, keepdims=True) + epsilon)
    stretches = row_count // STRETCH
    shaped = (stretches, STRETCH, head_count, head_dim)

    def advance(memory_state, input_rows):
        query_stretch, key_stretch, value_stretch, reset_flag = input_rows
        memory_state = jnp.where(reset_flag, jnp.zeros_like(memory_state), memory_state)
        read_out = jnp.einsum("thd,hde->the", query_stretch, memory_state, precision=highest)
        error_rows = (
            jnp.einsum("thd,hde->the", key_stretch, memory_state, precision=highest) - value_stretch
        )
        update = jnp.einsum("thd,the->hde", key_stretch, error_rows, precision=highest) / STRETCH
        memory_state = decay_own[:, None, None] * memory_state - rate_own[:, None, None] * update
        return (memory_state, read_out)

    initial = jnp.zeros((head_count, head_dim, head_dim), jnp.float32)
    final_state, reads = lax.scan(
        jax.checkpoint(advance),
        initial,
        (
            query_unit.reshape(shaped),
            key_unit.reshape(shaped),
            value_heads.reshape(shaped),
            stretch_first,
        ),
    )
    return reads.reshape(row_count, head_count, head_dim)


def block_parts(queries, padded_keys, padded_values, seq_index, padded_seq, windows, number):
    key_span = QBLK + WIN_MAX
    first_row = number * QBLK
    query_block = lax.dynamic_slice_in_dim(queries, first_row, QBLK, 0)
    key_block = lax.dynamic_slice_in_dim(padded_keys, first_row, key_span, 0)
    value_block = lax.dynamic_slice_in_dim(padded_values, first_row, key_span, 0)
    distance = (
        jnp.arange(QBLK, dtype=jnp.int32)[:, None]
        + WIN_MAX
        - jnp.arange(key_span, dtype=jnp.int32)[None, :]
    )
    same_seq = (
        lax.dynamic_slice_in_dim(seq_index, first_row, QBLK)[:, None]
        == lax.dynamic_slice_in_dim(padded_seq, first_row, key_span)[None, :]
    )
    allowed = (distance >= 0)[None] & (distance[None] < windows[:, None, None]) & same_seq[None]
    score_scale = queries.shape[2] ** (-0.5)
    scores = (
        jnp.einsum("qhd,khd->hqk", query_block, key_block, preferred_element_type=jnp.float32)
        * score_scale
    )
    return (query_block, key_block, value_block, jnp.where(allowed, scores, -1e30))


def padded_inputs(key_heads, value_heads, seq_index):
    padded_keys = jnp.pad(key_heads, ((WIN_MAX, 0), (0, 0), (0, 0)))
    padded_values = jnp.pad(value_heads, ((WIN_MAX, 0), (0, 0), (0, 0)))
    padded_seq = jnp.pad(seq_index, (WIN_MAX, 0), constant_values=-1)
    return (padded_keys, padded_values, padded_seq)


def attend_forward(queries, key_heads, value_heads, seq_index, windows):
    row_count, head_count, head_dim = queries.shape
    padded_keys, padded_values, padded_seq = padded_inputs(key_heads, value_heads, seq_index)

    def block_out(number):
        query_block, key_block, value_block, scores = block_parts(
            queries, padded_keys, padded_values, seq_index, padded_seq, windows, number
        )
        row_max = jnp.max(scores, -1, keepdims=True)
        exponent = jnp.exp(scores - row_max)
        row_total = jnp.sum(exponent, -1, keepdims=True)
        soft_weights = (exponent / row_total).astype(jnp.bfloat16)
        attended = jnp.einsum(
            "hqk,khd->qhd", soft_weights, value_block, preferred_element_type=jnp.float32
        )
        return (attended, row_max + jnp.log(row_total))

    outputs, log_totals = lax.map(block_out, jnp.arange(row_count // QBLK, dtype=jnp.int32))
    return (outputs.reshape(row_count, head_count, head_dim), log_totals)


def attend_backward(queries, key_heads, value_heads, seq_index, windows, log_totals, grad_heads):
    row_count, head_count, head_dim = queries.shape
    score_scale = head_dim ** (-0.5)
    key_span = QBLK + WIN_MAX
    padded_keys, padded_values, padded_seq = padded_inputs(key_heads, value_heads, seq_index)

    def accumulate(number, carried):
        grad_query, grad_key, grad_value = carried
        query_block, key_block, value_block, scores = block_parts(
            queries, padded_keys, padded_values, seq_index, padded_seq, windows, number
        )
        first_row = number * QBLK
        soft_weights = jnp.exp(scores - log_totals[number])
        grad_block = lax.dynamic_slice_in_dim(grad_heads, first_row, QBLK, 0)
        grad_soft = jnp.einsum(
            "qhd,khd->hqk", grad_block, value_block, preferred_element_type=jnp.float32
        )
        inner_sum = jnp.sum(soft_weights * grad_soft, -1, keepdims=True)
        grad_scores = (soft_weights * (grad_soft - inner_sum)).astype(jnp.bfloat16)
        block_query = (
            jnp.einsum("hqk,khd->qhd", grad_scores, key_block, preferred_element_type=jnp.float32)
            * score_scale
        )
        block_key = (
            jnp.einsum("hqk,qhd->khd", grad_scores, query_block, preferred_element_type=jnp.float32)
            * score_scale
        )
        block_value = jnp.einsum(
            "hqk,qhd->khd",
            soft_weights.astype(jnp.bfloat16),
            grad_block,
            preferred_element_type=jnp.float32,
        )
        grad_query = lax.dynamic_update_slice_in_dim(grad_query, block_query, first_row, 0)
        grad_key = lax.dynamic_update_slice_in_dim(
            grad_key,
            lax.dynamic_slice_in_dim(grad_key, first_row, key_span, 0) + block_key,
            first_row,
            0,
        )
        grad_value = lax.dynamic_update_slice_in_dim(
            grad_value,
            lax.dynamic_slice_in_dim(grad_value, first_row, key_span, 0) + block_value,
            first_row,
            0,
        )
        return (grad_query, grad_key, grad_value)

    padded_shape = (row_count + WIN_MAX, head_count, head_dim)
    initial = (
        jnp.zeros(queries.shape, jnp.float32),
        jnp.zeros(padded_shape, jnp.float32),
        jnp.zeros(padded_shape, jnp.float32),
    )
    results = lax.fori_loop(0, row_count // QBLK, accumulate, initial)
    return (results[0], results[1][WIN_MAX:], results[2][WIN_MAX:])


def gather_stream(values):
    return lax.all_gather(values, "tensor", axis=0, tiled=True)


def input_grads(row_term, quarter):
    return lax.psum_scatter(
        row_term(jnp.int32(0), quarter * lax.axis_size("tensor")).astype(jnp.bfloat16),
        "tensor",
        scatter_dimension=0,
        tiled=True,
    ).astype(jnp.float32)


def projection_inward(
    input_rows, weight_locals, adapter_lower, adapter_upper_local, expand_columns
):
    outputs = []
    latents = []
    for member_sequence in range(weight_locals.shape[0]):
        latent_value = (
            expand_columns
            * jnp.dot(
                input_rows, adapter_lower[member_sequence], preferred_element_type=jnp.float32
            )
        ).astype(jnp.bfloat16)
        outputs.append(
            jnp.dot(input_rows, weight_locals[member_sequence], preferred_element_type=jnp.float32)
            + jnp.dot(
                latent_value,
                adapter_upper_local[member_sequence],
                preferred_element_type=jnp.float32,
            )
        )
        latents.append(latent_value)
    return (outputs, latents)


def back_in(
    input_rows,
    gradient_list,
    weight_locals,
    adapter_lower,
    adapter_upper_local,
    latents,
    expand_columns,
    quarter,
    portion_index,
    portion_count,
):
    count_in = len(gradient_list)
    d_latents = [
        (
            expand_columns
            * jnp.dot(
                gradient_list[member_sequence],
                adapter_upper_local[member_sequence].T,
                preferred_element_type=jnp.float32,
            )
        ).astype(jnp.bfloat16)
        for member_sequence in range(count_in)
    ]

    def row_term(first_row, row_total):
        summed = jnp.zeros((row_total, input_rows.shape[1]), jnp.float32)
        for member_sequence in range(count_in):
            gradient_rows = gradient_list[member_sequence]
            latent_row_block = d_latents[member_sequence]
            summed = summed + jnp.dot(
                gradient_rows, weight_locals[member_sequence].T, preferred_element_type=jnp.float32
            )
            summed = summed + jnp.dot(
                latent_row_block,
                adapter_lower[member_sequence].T,
                preferred_element_type=jnp.float32,
            )
        return summed

    grad_inputs = input_grads(row_term, quarter)
    a_terms = jnp.stack(
        [
            jnp.dot(input_rows.T, d_latents[member_sequence], preferred_element_type=jnp.float32)
            for member_sequence in range(count_in)
        ]
    )
    b_own = jnp.stack(
        [
            jnp.dot(
                latents[member_sequence].T,
                gradient_list[member_sequence],
                preferred_element_type=jnp.float32,
            )
            for member_sequence in range(count_in)
        ]
    )
    local_width = b_own.shape[2]
    b_terms = lax.dynamic_update_slice_in_dim(
        jnp.zeros((count_in, b_own.shape[1], local_width * portion_count), jnp.float32),
        b_own,
        portion_index * local_width,
        2,
    )
    return (grad_inputs, a_terms, b_terms)


def projection_outward(
    activation_value,
    weight_local,
    adapter_lower_local,
    adapter_upper,
    expand_columns,
    portion_count,
):
    row_count = activation_value.shape[0]
    quarter = row_count // portion_count
    latent_value = (
        expand_columns
        * jnp.dot(activation_value, adapter_lower_local, preferred_element_type=jnp.float32)
    ).astype(jnp.bfloat16)

    def row_term(first_row, row_total):
        return jnp.dot(
            activation_value, weight_local, preferred_element_type=jnp.float32
        ) + jnp.dot(latent_value, adapter_upper, preferred_element_type=jnp.float32)

    result = lax.psum_scatter(
        row_term(jnp.int32(0), quarter * lax.axis_size("tensor")).astype(jnp.bfloat16),
        "tensor",
        scatter_dimension=0,
        tiled=True,
    ).astype(jnp.float32)
    return (result, (activation_value, latent_value))


def project_back(
    gradient_quarter,
    kept_values,
    weight_local,
    adapter_lower_local,
    adapter_upper,
    expand_columns,
    portion_index,
    portion_count,
):
    adapter_width = adapter_upper.shape[0]
    activation_value, latent_value = kept_values
    gradient_rows = lax.all_gather(
        gradient_quarter.astype(jnp.bfloat16), "tensor", axis=0, tiled=True
    )
    latent_gradient = (
        expand_columns * jnp.dot(gradient_rows, adapter_upper.T, preferred_element_type=jnp.float32)
    ).astype(jnp.bfloat16)
    d_activation = jnp.dot(
        gradient_rows, weight_local.T, preferred_element_type=jnp.float32
    ) + jnp.dot(latent_gradient, adapter_lower_local.T, preferred_element_type=jnp.float32)
    b_term = jnp.dot(latent_value.T, gradient_rows, preferred_element_type=jnp.float32)
    a_own = jnp.dot(activation_value.T, latent_gradient, preferred_element_type=jnp.float32)
    local_width = a_own.shape[0]
    a_term = lax.dynamic_update_slice_in_dim(
        jnp.zeros((local_width * portion_count, adapter_width), jnp.float32),
        a_own,
        portion_index * local_width,
        0,
    )
    return (d_activation, a_term, b_term)


def per_device(
    tokens,
    cotangent,
    attention_gain,
    feedforward_gain,
    query_key_value_matrix,
    output_matrix,
    feedforward_matrix,
    down_matrix,
    memory_retention,
    memory_step_size,
    sequence_length,
    sequence_permutation,
    sequence_adapter,
    head_span_window,
    query_key_value_lower,
    query_key_value_upper,
    output_adapter_lower,
    output_adapter_upper,
    feedforward_adapter_lower,
    feedforward_adapter_upper,
    down_adapter_lower,
    down_adapter_upper,
):
    groups_count = lax.axis_size("dp")
    portion_count = lax.axis_size("tensor")
    portion_index = lax.axis_index("tensor")
    group_index = lax.axis_index("dp")
    quarter, width = tokens.shape
    slot_rows = quarter // groups_count
    row_count = quarter * portion_count
    arrived_tokens, arrived_grads = (
        lax.all_to_all(
            tokens.reshape(groups_count, slot_rows, width),
            "dp",
            split_axis=0,
            concat_axis=0,
            tiled=True,
        ),
        lax.all_to_all(
            cotangent.reshape(groups_count, slot_rows, width),
            "dp",
            split_axis=0,
            concat_axis=0,
            tiled=True,
        ),
    )
    stream_in = arrived_tokens.reshape(quarter, width).astype(jnp.float32)
    grad_out = arrived_grads.reshape(quarter, width).astype(jnp.float32)
    qkv_local, out_local, ffn_local, down_local = (
        lax.all_gather(query_key_value_matrix, "dp", axis=1, tiled=True),
        lax.all_gather(output_matrix, "dp", axis=1, tiled=True),
        lax.all_gather(feedforward_matrix, "dp", axis=1, tiled=True),
        lax.all_gather(down_matrix, "dp", axis=1, tiled=True),
    )
    qkv_a, qkv_b, out_a, out_b, ffn_a, ffn_b, down_a, down_b = (
        lax.all_gather(query_key_value_lower, ("dp", "tensor"), axis=1, tiled=True),
        lax.all_gather(query_key_value_upper, ("dp", "tensor"), axis=2, tiled=True),
        lax.all_gather(output_adapter_lower, ("dp", "tensor"), axis=0, tiled=True),
        lax.all_gather(output_adapter_upper, ("dp", "tensor"), axis=1, tiled=True),
        lax.all_gather(feedforward_adapter_lower, ("dp", "tensor"), axis=1, tiled=True),
        lax.all_gather(feedforward_adapter_upper, ("dp", "tensor"), axis=2, tiled=True),
        lax.all_gather(down_adapter_lower, ("dp", "tensor"), axis=0, tiled=True),
        lax.all_gather(down_adapter_upper, ("dp", "tensor"), axis=1, tiled=True),
    )
    head_width = width // portion_count
    hidden_width = ffn_local.shape[2]
    head_local = head_width // HEAD_DIM
    qkv_b_own = lax.dynamic_slice_in_dim(qkv_b, portion_index * head_width, head_width, 2)
    out_a_own = lax.dynamic_slice_in_dim(out_a, portion_index * head_width, head_width, 0)
    ffn_b_own = lax.dynamic_slice_in_dim(ffn_b, portion_index * hidden_width, hidden_width, 2)
    down_a_own = lax.dynamic_slice_in_dim(down_a, portion_index * hidden_width, hidden_width, 0)
    windows = lax.dynamic_slice_in_dim(head_span_window, portion_index * head_local, head_local, 0)
    decay_own = lax.dynamic_slice_in_dim(
        memory_retention, portion_index * head_local, head_local, 0
    )
    rate_own = lax.dynamic_slice_in_dim(memory_step_size, portion_index * head_local, head_local, 0)
    seq_index, row_adapter, row_begin = stream_layout(
        sequence_length, sequence_permutation, sequence_adapter, group_index, row_count
    )
    expand_columns = adapter_mask(row_adapter)
    stretch_first = (
        row_begin.reshape(-1, STRETCH)[:, 0]
        == jnp.arange(row_count // STRETCH, dtype=jnp.int32) * STRETCH
    )
    normed = gather_stream(normalize(stream_in, attention_gain).astype(jnp.bfloat16))
    projected, qkv_latents = projection_inward(normed, qkv_local, qkv_a, qkv_b_own, expand_columns)
    query_heads, key_heads, value_heads = [
        item.astype(jnp.bfloat16).reshape(row_count, head_local, HEAD_DIM) for item in projected
    ]
    attended, log_totals = attend_forward(query_heads, key_heads, value_heads, seq_index, windows)

    def memory_part(query_float, key_float, value_float):
        return memory_read(query_float, key_float, value_float, decay_own, rate_own, stretch_first)

    remembered, memory_pull = jax.vjp(
        memory_part,
        query_heads.astype(jnp.float32),
        key_heads.astype(jnp.float32),
        value_heads.astype(jnp.float32),
    )
    heads_out = (
        (attended + memory_gain * remembered).reshape(row_count, head_width).astype(jnp.bfloat16)
    )
    attn_branch, out_kept = projection_outward(
        heads_out, out_local, out_a_own, out_b, expand_columns, portion_count
    )
    hidden_one = stream_in + attn_branch
    normed_two = gather_stream(normalize(hidden_one, feedforward_gain).astype(jnp.bfloat16))
    ffn_pre, ffn_latents = projection_inward(
        normed_two, ffn_local, ffn_a, ffn_b_own, expand_columns
    )

    def swiglu_part(gate_pre, up_pre):
        return jax.nn.silu(gate_pre) * up_pre

    swiglu_out, swiglu_pull = jax.vjp(swiglu_part, ffn_pre[0], ffn_pre[1])
    ffn_branch, down_kept = projection_outward(
        swiglu_out.astype(jnp.bfloat16),
        down_local,
        down_a_own,
        down_b,
        expand_columns,
        portion_count,
    )
    mixed_rows = (hidden_one + ffn_branch).astype(jnp.bfloat16)
    grad_swiglu, down_a_term, down_b_term = project_back(
        grad_out,
        down_kept,
        down_local,
        down_a_own,
        down_b,
        expand_columns,
        portion_index,
        portion_count,
    )
    grad_gate, grad_up = swiglu_pull(grad_swiglu)
    ffn_grad_list = [grad_gate.astype(jnp.bfloat16), grad_up.astype(jnp.bfloat16)]
    grad_normed_two, ffn_a_term, ffn_b_term = back_in(
        normed_two,
        ffn_grad_list,
        ffn_local,
        ffn_a,
        ffn_b_own,
        ffn_latents,
        expand_columns,
        quarter,
        portion_index,
        portion_count,
    )
    norm_value, norm_pull = jax.vjp(lambda values: normalize(values, feedforward_gain), hidden_one)
    grad_one = grad_out + norm_pull(grad_normed_two)[0]
    grad_heads, out_a_term, out_b_term = project_back(
        grad_one,
        out_kept,
        out_local,
        out_a_own,
        out_b,
        expand_columns,
        portion_index,
        portion_count,
    )
    grad_heads_low = grad_heads.astype(jnp.bfloat16).reshape(row_count, head_local, HEAD_DIM)
    memory_query, memory_key, memory_value = memory_pull(
        memory_gain * grad_heads_low.astype(jnp.float32)
    )
    attn_query, attn_key, attn_value = attend_backward(
        query_heads, key_heads, value_heads, seq_index, windows, log_totals, grad_heads_low
    )
    qkv_grad_list = [
        (attn_query + memory_query).reshape(row_count, head_width).astype(jnp.bfloat16),
        (attn_key + memory_key).reshape(row_count, head_width).astype(jnp.bfloat16),
        (attn_value + memory_value).reshape(row_count, head_width).astype(jnp.bfloat16),
    ]
    grad_normed, qkv_a_term, qkv_b_term = back_in(
        normed,
        qkv_grad_list,
        qkv_local,
        qkv_a,
        qkv_b_own,
        qkv_latents,
        expand_columns,
        quarter,
        portion_index,
        portion_count,
    )
    first_value, first_pull = jax.vjp(lambda values: normalize(values, attention_gain), stream_in)
    grad_input = (grad_one + first_pull(grad_normed)[0]).astype(jnp.bfloat16)
    mixed_back, grad_back = (
        lax.all_to_all(
            mixed_rows.reshape(groups_count, slot_rows, width),
            "dp",
            split_axis=0,
            concat_axis=0,
            tiled=True,
        ),
        lax.all_to_all(
            grad_input.reshape(groups_count, slot_rows, width),
            "dp",
            split_axis=0,
            concat_axis=0,
            tiled=True,
        ),
    )
    summed = (
        lax.psum_scatter(qkv_a_term, ("dp", "tensor"), scatter_dimension=1, tiled=True),
        lax.psum_scatter(qkv_b_term, ("dp", "tensor"), scatter_dimension=2, tiled=True),
        lax.psum_scatter(out_a_term, ("dp", "tensor"), scatter_dimension=0, tiled=True),
        lax.psum_scatter(out_b_term, ("dp", "tensor"), scatter_dimension=1, tiled=True),
        lax.psum_scatter(ffn_a_term, ("dp", "tensor"), scatter_dimension=1, tiled=True),
        lax.psum_scatter(ffn_b_term, ("dp", "tensor"), scatter_dimension=2, tiled=True),
        lax.psum_scatter(down_a_term, ("dp", "tensor"), scatter_dimension=0, tiled=True),
        lax.psum_scatter(down_b_term, ("dp", "tensor"), scatter_dimension=1, tiled=True),
    )
    return (
        mixed_back.reshape(quarter, width),
        grad_back.reshape(quarter, width),
        summed[0],
        summed[1],
        summed[2],
        summed[3],
        summed[4],
        summed[5],
        summed[6],
        summed[7],
    )


def solution(mesh):
    placed = (
        P(("dp", "tensor"), None),
        P(("dp", "tensor"), None),
        P(),
        P(),
        P(None, "dp", "tensor"),
        P("tensor", "dp"),
        P(None, "dp", "tensor"),
        P("tensor", "dp"),
        P(),
        P(),
        P(),
        P(),
        P(),
        P(),
        P(None, ("dp", "tensor"), None),
        P(None, None, ("dp", "tensor")),
        P(("dp", "tensor"), None),
        P(None, ("dp", "tensor")),
        P(None, ("dp", "tensor"), None),
        P(None, None, ("dp", "tensor")),
        P(("dp", "tensor"), None),
        P(None, ("dp", "tensor")),
    )
    return jax.shard_map(
        per_device,
        mesh=mesh,
        in_specs=placed,
        out_specs=(
            P(("dp", "tensor"), None),
            P(("dp", "tensor"), None),
            P(None, ("dp", "tensor"), None),
            P(None, None, ("dp", "tensor")),
            P(("dp", "tensor"), None),
            P(None, ("dp", "tensor")),
            P(None, ("dp", "tensor"), None),
            P(None, None, ("dp", "tensor")),
            P(("dp", "tensor"), None),
            P(None, ("dp", "tensor")),
        ),
        check_vma=False,
    )
```

```python
import functools

import jax
import jax.numpy as jnp
from jax import lax
from jax.experimental import pallas as pl
from jax.experimental.pallas import tpu as pltpu
from jax.sharding import PartitionSpec as P

HEAD_DIM = 128
ADAPTER_RANK = 16
STRETCH = 64
SEQ_G = 3
LANES = 128
BLOCK = 256
MEMORY_GAIN = 32.0
EPSILON = 1e-06
LOG2E = 1.4426950408889634
BF16 = jnp.bfloat16
F32 = jnp.float32
VMEM_LIMIT = 56 * 1024 * 1024


def nn(left, right):
    return jnp.dot(left, right, preferred_element_type=F32)


def nt(left, right, precision=None):
    return lax.dot_general(
        left, right, (((1,), (1,)), ((), ())), precision=precision, preferred_element_type=F32
    )


def tn(left, right):
    return lax.dot_general(left, right, (((0,), (0,)), ((), ())), preferred_element_type=F32)


def params(vmem=VMEM_LIMIT):
    return pltpu.CompilerParams(dimension_semantics=("arbitrary",), vmem_limit_bytes=vmem)


def cost(flops, moved):
    return pl.CostEstimate(flops=int(flops), bytes_accessed=int(moved), transcendentals=0)


def whole(*shape):
    return pl.BlockSpec(shape, lambda *_: (0,) * len(shape), pipeline_mode=pl.Buffered(1))


def adapter_select(meta, first_row, rows, copies):
    row = first_row + lax.broadcasted_iota(jnp.int32, (rows, 1), 0)
    adapter = jnp.where(row >= meta[1], meta[4], jnp.where(row >= meta[0], meta[3], meta[2]))
    column = lax.broadcasted_iota(jnp.int32, (rows, copies * LANES), 1)
    return (column % LANES) // ADAPTER_RANK == adapter


def keep_low(select, values):
    return jnp.where(select, values, 0.0).astype(BF16)


def qkv_kernel(meta, x0, x1, x2, x3, gain, weight, lower, upper_t, normed, qkv, latent, x_scr):
    step = pl.program_id(0)
    rows = x_scr.shape[0]
    for k, x_ref in enumerate((x0, x1, x2, x3)):

        @pl.when(step == k)
        def _():
            x_scr[...] = x_ref[...]

    values = x_scr[...].astype(F32)
    scale = lax.rsqrt(jnp.mean(values * values, -1, keepdims=True) + EPSILON)
    low = (values * scale * gain[...]).astype(BF16)
    normed[...] = low
    select = adapter_select(meta, (meta[7] ^ step) * rows, rows, 3)
    lat = keep_low(select, nn(low, lower[...]))
    latent[...] = lat
    for m in range(3):
        qkv[m] = (
            nn(low, weight[m]) + nt(lat[:, m * LANES : (m + 1) * LANES], upper_t[m])
        ).astype(BF16)


def project_qkv(meta, pieces, gain, weight, lower, upper_t):
    rows, width = pieces[0].shape
    own = weight.shape[2]
    total = rows * len(pieces)
    place = lambda step, meta: (meta[7] ^ step, 0)
    return pl.pallas_call(
        qkv_kernel,
        grid_spec=pltpu.PrefetchScalarGridSpec(
            num_scalar_prefetch=1,
            grid=(len(pieces),),
            in_specs=[whole(rows, width)] * 4
            + [
                whole(1, width),
                whole(*weight.shape),
                whole(*lower.shape),
                whole(*upper_t.shape),
            ],
            out_specs=[
                pl.BlockSpec((rows, width), place),
                pl.BlockSpec((3, rows, own), lambda step, meta: (0, meta[7] ^ step, 0)),
                pl.BlockSpec((rows, 3 * LANES), place),
            ],
            scratch_shapes=[pltpu.VMEM((rows, width), BF16)],
        ),
        out_shape=[
            jax.ShapeDtypeStruct((total, width), BF16),
            jax.ShapeDtypeStruct((3, total, own), BF16),
            jax.ShapeDtypeStruct((total, 3 * LANES), BF16),
        ],
        compiler_params=params(),
        cost_estimate=cost(2 * total * width * (3 * own + 600), 4 * total * width),
        name="project_qkv",
    )(meta, *pieces, gain, weight, lower, upper_t)


def span_variants(count, spans, run):
    for n, blocks in enumerate(spans):
        if n == 0:
            condition = count <= blocks
        else:
            condition = count == blocks
        pl.when(condition)(functools.partial(run, blocks * BLOCK))


def stretch_columns(low, total_stretches):
    stretch = lax.broadcasted_iota(jnp.int32, low.shape, 0) // STRETCH
    zero = jnp.zeros_like(low)
    return jnp.concatenate(
        [jnp.where(stretch == n, low, zero) for n in range(total_stretches)], 1
    )


def unit_rows(values):
    inverse = lax.rsqrt(jnp.sum(values * values, -1, keepdims=True) + EPSILON)
    return values * inverse, inverse


def mixer_forward_kernel(
    spans, meta, fmeta, qkv, heads, attended, log_total, states, state_scr
):
    block = pl.program_id(0)
    first_row = block * BLOCK
    start_two, start_three = meta[0], meta[1]
    row = first_row + lax.broadcasted_iota(jnp.int32, (BLOCK, 1), 0)
    begin = jnp.where(row >= start_three, start_three, jnp.where(row >= start_two, start_two, 0))
    first_begin = jnp.where(
        first_row >= start_three, start_three, jnp.where(first_row >= start_two, start_two, 0)
    )
    factor = HEAD_DIM ** (-0.5) * LOG2E
    stretches = BLOCK // STRETCH

    @pl.when(block == 0)
    def _():
        state_scr[...] = jnp.zeros_like(state_scr)

    for h in range(2):
        cols = slice(h * HEAD_DIM, (h + 1) * HEAD_DIM)
        window = meta[5 + h]
        low_key = jnp.maximum(row - window + 1, begin)
        first_key = jnp.maximum(first_row - window + 1, first_begin)
        count = block - first_key // BLOCK + 1

        def attend(span, cols=cols, low_key=low_key, h=h):
            start = pl.multiple_of(jnp.maximum(first_row + BLOCK - span, 0), BLOCK)
            query = qkv[0, pl.ds(pl.multiple_of(first_row, BLOCK), BLOCK), cols]
            key = qkv[1, pl.ds(start, span), cols]
            value = qkv[2, pl.ds(start, span), cols]
            score = nt(query, key)
            position = start + lax.broadcasted_iota(jnp.int32, (BLOCK, span), 1)
            score = jnp.where((position >= low_key) & (position <= row), score, -1e30)
            top = jnp.max(score, -1, keepdims=True)
            weight = jnp.exp2((score - top) * factor).astype(BF16)
            with_ones = jnp.concatenate([value, jnp.ones_like(value)], 1)
            both = nn(weight, with_ones)
            total = both[:, HEAD_DIM : HEAD_DIM + 1]
            attended[:, cols] = both[:, :HEAD_DIM] / both[:, HEAD_DIM:]
            logs = jnp.broadcast_to(top * factor + jnp.log2(total), (BLOCK, LANES))
            pick = jnp.where(lax.broadcasted_iota(jnp.int32, (8, LANES), 1) == 0, 1.0, 0.0)
            log_total[0, h : h + 1, :] = nt(pick, logs, lax.Precision.HIGHEST)[0:1]

        span_variants(count, spans, attend)

    for h in range(2):
        cols = slice(h * HEAD_DIM, (h + 1) * HEAD_DIM)
        here = pl.ds(pl.multiple_of(first_row, BLOCK), BLOCK)
        query_unit, _ = unit_rows(qkv[0, here, cols].astype(F32))
        key_unit, _ = unit_rows(qkv[1, here, cols].astype(F32))
        query_low = query_unit.astype(BF16)
        key_low = key_unit.astype(BF16)
        by_stretch = stretch_columns(key_low, stretches)
        retention, step_size = fmeta[h], fmeta[2 + h]
        gram = (nn(key_unit.T.astype(BF16), by_stretch) * step_size).astype(BF16)
        written = nn(qkv[2, here, cols].astype(F32).T.astype(BF16), by_stretch) * step_size
        state = state_scr[h]
        for n in range(stretches):
            row_at = first_row + n * STRETCH
            keep = jnp.where((row_at == start_two) | (row_at == start_three), 0.0, 1.0)
            state = state * keep
            low = state.astype(BF16)
            states[n, h] = low
            rows = slice(n * STRETCH, (n + 1) * STRETCH)
            lanes = slice(n * HEAD_DIM, (n + 1) * HEAD_DIM)
            read = nt(query_low[rows], low)
            heads[rows, cols] = (attended[rows, cols] + MEMORY_GAIN * read).astype(BF16)
            state = retention * state - nn(low, gram[:, lanes]) + written[:, lanes]
        state_scr[h] = state


def mixer_forward(meta, fmeta, qkv, spans):
    total, own = qkv.shape[1:]
    blocks = total // BLOCK
    stretches = BLOCK // STRETCH
    row_block = pl.BlockSpec((BLOCK, own), lambda b, *_: (b, 0))
    return pl.pallas_call(
        functools.partial(mixer_forward_kernel, spans),
        grid_spec=pltpu.PrefetchScalarGridSpec(
            num_scalar_prefetch=2,
            grid=(blocks,),
            in_specs=[whole(*qkv.shape)],
            out_specs=[
                row_block,
                row_block,
                pl.BlockSpec((1, 8, BLOCK), lambda b, *_: (b, 0, 0)),
                pl.BlockSpec(
                    (stretches, 2, HEAD_DIM, HEAD_DIM), lambda b, *_: (b, 0, 0, 0)
                ),
            ],
            scratch_shapes=[pltpu.VMEM((2, HEAD_DIM, HEAD_DIM), F32)],
        ),
        out_shape=[
            jax.ShapeDtypeStruct((total, own), BF16),
            jax.ShapeDtypeStruct((total, own), F32),
            jax.ShapeDtypeStruct((blocks, 8, BLOCK), F32),
            jax.ShapeDtypeStruct((blocks * stretches, 2, HEAD_DIM, HEAD_DIM), BF16),
        ],
        compiler_params=params(),
        cost_estimate=cost(4e9, 12e6),
        name="mixer_forward",
    )(meta, fmeta, qkv)


def mixer_backward_kernel(
    spans,
    blocks,
    meta,
    fmeta,
    qkv,
    grad_out,
    attended,
    log_total,
    states,
    grads,
    key_t,
    key_sum,
    value_sum,
    query_t,
    state_grad,
):
    block = blocks - 1 - pl.program_id(0)
    first_row = block * BLOCK
    start_two, start_three = meta[0], meta[1]
    row = first_row + lax.broadcasted_iota(jnp.int32, (1, BLOCK), 1)
    begin = jnp.where(row >= start_three, start_three, jnp.where(row >= start_two, start_two, 0))
    first_begin = jnp.where(
        first_row >= start_three, start_three, jnp.where(first_row >= start_two, start_two, 0)
    )
    scale = HEAD_DIM ** (-0.5)
    factor = scale * LOG2E
    stretches = BLOCK // STRETCH
    here = pl.ds(pl.multiple_of(first_row, BLOCK), BLOCK)

    @pl.when(pl.program_id(0) == 0)
    def _():
        key_sum[...] = jnp.zeros_like(key_sum)
        value_sum[...] = jnp.zeros_like(value_sum)
        state_grad[...] = jnp.zeros_like(state_grad)
        for h in range(2):
            for b in range(blocks):
                rows = slice(b * BLOCK, (b + 1) * BLOCK)
                key = qkv[1, rows, h * HEAD_DIM : (h + 1) * HEAD_DIM]
                key_t[h, :, rows] = key.astype(F32).T.astype(BF16)

    for h in range(2):
        cols = slice(h * HEAD_DIM, (h + 1) * HEAD_DIM)
        window = meta[5 + h]
        low_key = jnp.maximum(row - window + 1, begin)
        first_key = jnp.maximum(first_row - window + 1, first_begin)
        count = block - first_key // BLOCK + 1
        product = grad_out[:, cols].astype(F32) * attended[:, cols]
        inner = nt(jnp.ones((8, HEAD_DIM), F32), product, lax.Precision.HIGHEST)[0:1]
        logs = log_total[0, h : h + 1, :]

        def attend(span, cols=cols, low_key=low_key, h=h, inner=inner, logs=logs):
            start = pl.multiple_of(jnp.maximum(first_row + BLOCK - span, 0), BLOCK)
            there = pl.ds(start, span)
            query = qkv[0, here, cols]
            grad = grad_out[:, cols]
            score = nt(qkv[1, there, cols], query)
            position = start + lax.broadcasted_iota(jnp.int32, (span, BLOCK), 0)
            allowed = (position >= low_key) & (position <= row)
            weight = jnp.where(allowed, jnp.exp2(score * factor - logs), 0.0)
            grad_weight = nt(qkv[2, there, cols], grad)
            grad_score = (weight * (grad_weight - inner)).astype(BF16)
            value_sum[h, there, :] += nn(weight.astype(BF16), grad)
            key_sum[h, there, :] += nn(grad_score, query)
            query_t[h] = nn(key_t[h, :, there], grad_score)

        span_variants(count, spans, attend)

    for h in range(2):
        cols = slice(h * HEAD_DIM, (h + 1) * HEAD_DIM)
        query_unit, query_inverse = unit_rows(qkv[0, here, cols].astype(F32))
        key_unit, key_inverse = unit_rows(qkv[1, here, cols].astype(F32))
        value = qkv[2, here, cols].astype(F32)
        key_low = key_unit.astype(BF16)
        grad = grad_out[:, cols]
        retention, step_size = fmeta[h], fmeta[2 + h]
        gram = (
            nn(key_unit.T.astype(BF16), stretch_columns(key_low, stretches)) * step_size
        ).astype(BF16)
        read_grad = MEMORY_GAIN * nn(
            grad.astype(F32).T.astype(BF16),
            stretch_columns(query_unit.astype(BF16), stretches),
        )
        carried = state_grad[h]
        query_grads, key_grads, value_grads = [], [], []
        for n in reversed(range(stretches)):
            row_at = first_row + n * STRETCH
            keep = jnp.where((row_at == start_two) | (row_at == start_three), 0.0, 1.0)
            rows = slice(n * STRETCH, (n + 1) * STRETCH)
            lanes = slice(n * HEAD_DIM, (n + 1) * HEAD_DIM)
            carried_low = carried.astype(BF16)
            state = states[n, h]
            key_rows = key_low[rows]
            pulled = nt(key_rows, carried_low)
            error = nt(key_rows, state) - value[rows]
            value_grads.append(step_size * pulled)
            key_grads.append(
                -step_size
                * (nn(pulled.astype(BF16), state) + nn(error.astype(BF16), carried_low))
            )
            query_grads.append(MEMORY_GAIN * nn(grad[rows], state))
            carried = keep * (
                read_grad[:, lanes] + retention * carried - nn(carried_low, gram[:, lanes])
            )
        state_grad[h] = carried
        query_unit_grad = jnp.concatenate(query_grads[::-1], 0)
        key_unit_grad = jnp.concatenate(key_grads[::-1], 0)
        value_grad = jnp.concatenate(value_grads[::-1], 0)
        query_memory = query_inverse * (
            query_unit_grad
            - query_unit * jnp.sum(query_unit * query_unit_grad, -1, keepdims=True)
        )
        key_memory = key_inverse * (
            key_unit_grad - key_unit * jnp.sum(key_unit * key_unit_grad, -1, keepdims=True)
        )
        grads[0, :, cols] = (scale * query_t[h].T + query_memory).astype(BF16)
        grads[1, :, cols] = (scale * key_sum[h, here, :] + key_memory).astype(BF16)
        grads[2, :, cols] = (value_sum[h, here, :] + value_grad).astype(BF16)


def mixer_backward(meta, fmeta, qkv, grad_pieces, attended, log_total, states, spans):
    total, own = qkv.shape[1:]
    blocks = total // BLOCK
    stretches = BLOCK // STRETCH
    per_piece = grad_pieces.shape[1] // BLOCK

    def piece_at(step, meta, fmeta):
        block = blocks - 1 - step
        return ((block // per_piece) ^ meta[7], block % per_piece, 0)

    row_block = pl.BlockSpec((BLOCK, own), lambda s, *_: (blocks - 1 - s, 0))
    return pl.pallas_call(
        functools.partial(mixer_backward_kernel, spans, blocks),
        grid_spec=pltpu.PrefetchScalarGridSpec(
            num_scalar_prefetch=2,
            grid=(blocks,),
            in_specs=[
                whole(*qkv.shape),
                pl.BlockSpec((None, BLOCK, own), piece_at),
                row_block,
                pl.BlockSpec((1, 8, BLOCK), lambda s, *_: (blocks - 1 - s, 0, 0)),
                pl.BlockSpec(
                    (stretches, 2, HEAD_DIM, HEAD_DIM), lambda s, *_: (blocks - 1 - s, 0, 0, 0)
                ),
            ],
            out_specs=pl.BlockSpec((3, BLOCK, own), lambda s, *_: (0, blocks - 1 - s, 0)),
            scratch_shapes=[
                pltpu.VMEM((2, HEAD_DIM, total), BF16),
                pltpu.VMEM((2, total, HEAD_DIM), F32),
                pltpu.VMEM((2, total, HEAD_DIM), F32),
                pltpu.VMEM((2, HEAD_DIM, BLOCK), F32),
                pltpu.VMEM((2, HEAD_DIM, HEAD_DIM), F32),
            ],
        ),
        out_shape=jax.ShapeDtypeStruct(qkv.shape, BF16),
        compiler_params=params(),
        cost_estimate=cost(10e9, 16e6),
        name="mixer_backward",
    )(meta, fmeta, qkv, grad_pieces, attended, log_total, states)


def out_forward_kernel(meta, mine, other, weight_t, lower, upper_t, branch, latent):
    own = mine.shape[1]
    select = adapter_select(meta, meta[8], mine.shape[0], 1)
    lat = keep_low(select, nn(mine[...], lower[:own]) + nn(other[...], lower[own:]))
    latent[...] = lat
    branch[...] = (
        nt(mine[...], weight_t[:, :own])
        + nt(other[...], weight_t[:, own:])
        + nt(lat, upper_t[...])
    ).astype(BF16)


def out_forward(meta, mine, other, weight_t, lower, upper_t):
    rows, own = mine.shape
    width = weight_t.shape[0]
    return pl.pallas_call(
        out_forward_kernel,
        grid_spec=pltpu.PrefetchScalarGridSpec(
            num_scalar_prefetch=1,
            grid=(1,),
            in_specs=[
                whole(rows, own),
                whole(rows, own),
                whole(*weight_t.shape),
                whole(*lower.shape),
                whole(*upper_t.shape),
            ],
            out_specs=[whole(rows, width), whole(rows, LANES)],
        ),
        out_shape=[
            jax.ShapeDtypeStruct((rows, width), BF16),
            jax.ShapeDtypeStruct((rows, LANES), BF16),
        ],
        compiler_params=params(),
        cost_estimate=cost(2 * rows * width * 640, 5e6),
        name="out_forward",
    )(meta, mine, other, weight_t, lower, upper_t)


def out_backward_kernel(meta, grad, weight_t, lower, upper_t, mine, other, latent_grad):
    own = mine.shape[1]
    select = adapter_select(meta, meta[8], mine.shape[0], 1)
    lat = keep_low(select, nn(grad[...], upper_t[...]))
    latent_grad[...] = lat
    mine[...] = (nn(grad[...], weight_t[:, :own]) + nt(lat, lower[:own])).astype(BF16)
    other[...] = (nn(grad[...], weight_t[:, own:]) + nt(lat, lower[own:])).astype(BF16)


def out_backward(meta, grad, weight_t, lower, upper_t):
    rows, width = grad.shape
    own = weight_t.shape[1] // 2
    return pl.pallas_call(
        out_backward_kernel,
        grid_spec=pltpu.PrefetchScalarGridSpec(
            num_scalar_prefetch=1,
            grid=(1,),
            in_specs=[
                whole(rows, width),
                whole(*weight_t.shape),
                whole(*lower.shape),
                whole(*upper_t.shape),
            ],
            out_specs=[whole(rows, own), whole(rows, own), whole(rows, LANES)],
        ),
        out_shape=[
            jax.ShapeDtypeStruct((rows, own), BF16),
            jax.ShapeDtypeStruct((rows, own), BF16),
            jax.ShapeDtypeStruct((rows, LANES), BF16),
        ],
        compiler_params=params(),
        cost_estimate=cost(2 * rows * width * 640, 5e6),
        name="out_backward",
    )(meta, grad, weight_t, lower, upper_t)


def ffn_kernel(
    first,
    meta,
    x0,
    x1,
    g0,
    g1,
    weight,
    lower,
    upper_t,
    down_lower,
    down_upper_t,
    dx0,
    dx1,
    swiglu,
    gate_grad,
    up_grad,
    latent,
    latent_grad,
    down_latent_grad,
    x_scr,
    g_scr,
    dx_scr,
):
    step = pl.program_id(0)
    rows = x_scr.shape[0]
    halves = x0.shape[0] // rows
    piece, part = step // halves, step % halves
    at = pl.ds(pl.multiple_of(part * rows, rows), rows)
    for k, (x_ref, g_ref) in enumerate(((x0, g0), (x1, g1))):

        @pl.when(piece == k)
        def _():
            x_scr[...] = x_ref[at, :]
            g_scr[...] = g_ref[at, :]

    first_row = (meta[7] ^ (first + piece)) * (rows * halves) + part * rows
    select = adapter_select(meta, first_row, rows, 2)
    select_one = select[:, :LANES]
    x = x_scr[...]
    grad = g_scr[...]
    lat = keep_low(select, nn(x, lower[...]))
    latent[...] = lat
    gate = nn(x, weight[0]) + nt(lat[:, :LANES], upper_t[0])
    up = nn(x, weight[1]) + nt(lat[:, LANES:], upper_t[1])
    sigmoid = 1.0 / (1.0 + jnp.exp(-gate))
    silu = gate * sigmoid
    swiglu[...] = (silu * up).astype(BF16)
    down_lat = keep_low(select_one, nn(grad, down_upper_t[...]))
    down_latent_grad[...] = down_lat
    wide_grad = nn(grad, weight[2]) + nt(down_lat, down_lower[...])
    d_up = (wide_grad * silu).astype(BF16)
    d_gate = (wide_grad * up * (sigmoid * (1.0 + gate * (1.0 - sigmoid)))).astype(BF16)
    gate_grad[...] = d_gate
    up_grad[...] = d_up
    lat_grad = keep_low(
        select, jnp.concatenate([nn(d_gate, upper_t[0]), nn(d_up, upper_t[1])], 1)
    )
    latent_grad[...] = lat_grad
    dx_scr[...] = (
        nt(d_gate, weight[0]) + nt(d_up, weight[1]) + nt(lat_grad, lower[...])
    ).astype(BF16)
    for k, dx_ref in enumerate((dx0, dx1)):

        @pl.when(piece == k)
        def _():
            dx_ref[at, :] = dx_scr[...]


def ffn(meta, first, xs, grads, weight, lower, upper_t, down_lower, down_upper_t):
    rows, width = xs[0].shape
    hidden = weight.shape[2]
    total = 2 * rows
    grid = total // BLOCK
    block = lambda columns: pl.BlockSpec((BLOCK, columns), lambda s, *_: (s, 0))
    return pl.pallas_call(
        functools.partial(ffn_kernel, first),
        grid_spec=pltpu.PrefetchScalarGridSpec(
            num_scalar_prefetch=1,
            grid=(grid,),
            in_specs=[whole(rows, width)] * 4
            + [
                whole(*weight.shape),
                whole(*lower.shape),
                whole(*upper_t.shape),
                whole(*down_lower.shape),
                whole(*down_upper_t.shape),
            ],
            out_specs=[whole(rows, width)] * 2
            + [block(hidden)] * 3
            + [block(2 * LANES), block(2 * LANES), block(LANES)],
            scratch_shapes=[pltpu.VMEM((BLOCK, width), BF16)] * 3,
        ),
        out_shape=[jax.ShapeDtypeStruct((rows, width), BF16)] * 2
        + [jax.ShapeDtypeStruct((total, hidden), BF16)] * 3
        + [
            jax.ShapeDtypeStruct((total, 2 * LANES), BF16),
            jax.ShapeDtypeStruct((total, 2 * LANES), BF16),
            jax.ShapeDtypeStruct((total, LANES), BF16),
        ],
        compiler_params=params(),
        cost_estimate=cost(2 * total * width * hidden * 6.0, 14e6),
        name="ffn",
    )(meta, *xs, *grads, weight, lower, upper_t, down_lower, down_upper_t)


def down_kernel(meta, first, rows_each, sw, weight, lower, upper_t, y, latent):
    step = pl.program_id(0)
    rows = sw.shape[0]
    per = rows_each // rows
    first_row = (meta[7] ^ (first + step // per)) * rows_each + (step % per) * rows
    select = adapter_select(meta, first_row, rows, 1)
    lat = keep_low(select, nn(sw[...], lower[...]))
    latent[...] = lat
    y[...] = (nt(sw[...], weight[...]) + nt(lat, upper_t[...])).astype(BF16)


def down(meta, first, rows_each, sw, weight, lower, upper_t):
    total, hidden = sw.shape
    width = weight.shape[1]
    return pl.pallas_call(
        lambda meta, *refs: down_kernel(meta, first, rows_each, *refs),
        grid_spec=pltpu.PrefetchScalarGridSpec(
            num_scalar_prefetch=1,
            grid=(total // BLOCK,),
            in_specs=[
                pl.BlockSpec((BLOCK, hidden), lambda s, *_: (s, 0)),
                pl.BlockSpec((None, width, hidden), lambda s, *_: (2, 0, 0), pipeline_mode=pl.Buffered(1)),
                whole(*lower.shape),
                whole(*upper_t.shape),
            ],
            out_specs=[
                pl.BlockSpec((BLOCK, width), lambda s, *_: (s, 0)),
                pl.BlockSpec((BLOCK, LANES), lambda s, *_: (s, 0)),
            ],
        ),
        out_shape=[
            jax.ShapeDtypeStruct((total, width), BF16),
            jax.ShapeDtypeStruct((total, LANES), BF16),
        ],
        compiler_params=params(),
        cost_estimate=cost(2 * total * width * hidden * 1.3, 8e6),
        name="down",
    )(meta, sw, weight, lower, upper_t)


def pair_kernel(count, steps, *refs):
    lefts, rights = refs[:count], refs[count : 2 * count]
    outs, sums = refs[2 * count : 3 * count], refs[3 * count :]
    step = pl.program_id(0)
    for left, right, out, total in zip(lefts, rights, outs, sums):
        a, b = left.shape[1], right.shape[1]

        @pl.when(step == 0)
        def _():
            total[...] = jnp.zeros_like(total)

        total[:, :b] += tn(left[...], right[...])

        @pl.when(step == steps - 1)
        def _():
            out[...] = total[...].T[:b].astype(BF16)


def pair_sums(pairs, rows=512):
    count = len(pairs)
    total = pairs[0][0].shape[0]
    rows = min(rows, total)
    steps = total // rows
    lefts, rights = [p[0] for p in pairs], [p[1] for p in pairs]
    flops = sum(2 * total * l.shape[1] * r.shape[1] for l, r in pairs)
    padded = lambda n: -(-n // LANES) * LANES
    return pl.pallas_call(
        functools.partial(pair_kernel, count, steps),
        grid=(steps,),
        in_specs=[pl.BlockSpec((rows, v.shape[1]), lambda s: (s, 0)) for v in lefts + rights],
        out_specs=[whole(r.shape[1], l.shape[1]) for l, r in pairs],
        out_shape=[jax.ShapeDtypeStruct((r.shape[1], l.shape[1]), BF16) for l, r in pairs],
        scratch_shapes=[pltpu.VMEM((l.shape[1], padded(r.shape[1])), F32) for l, r in pairs],
        compiler_params=params(),
        cost_estimate=cost(flops * 2, 10e6),
        name="pair_sums",
    )(*lefts, *rights)


def qkv_backward_kernel(meta, first, grads, weight, lower, upper_t, dx):
    step = pl.program_id(0)
    rows = dx.shape[0]
    halves = 2
    first_row = (meta[7] ^ first) * (halves * rows) + step * rows
    select = adapter_select(meta, first_row, rows, 3)
    lat = keep_low(
        select, jnp.concatenate([nn(grads[m], upper_t[m]) for m in range(3)], 1)
    )
    total = nt(lat, lower[...])
    for m in range(3):
        total += nt(grads[m], weight[m])
    dx[...] = total.astype(BF16)


def qkv_backward(meta, first, rows, grads, weight, lower, upper_t):
    own = grads.shape[2]
    width = lower.shape[0]
    part = rows // 2
    return pl.pallas_call(
        lambda meta, *refs: qkv_backward_kernel(meta, first, *refs),
        grid_spec=pltpu.PrefetchScalarGridSpec(
            num_scalar_prefetch=1,
            grid=(2,),
            in_specs=[
                pl.BlockSpec((3, part, own), lambda s, meta: (0, (meta[7] ^ first) * 2 + s, 0)),
                whole(*weight.shape),
                whole(*lower.shape),
                whole(*upper_t.shape),
            ],
            out_specs=pl.BlockSpec((part, width), lambda s, *_: (s, 0)),
        ),
        out_shape=jax.ShapeDtypeStruct((rows, width), BF16),
        compiler_params=params(),
        cost_estimate=cost(2 * rows * width * 1250, 5e6),
        name="qkv_backward",
    )(meta, grads, weight, lower, upper_t)


def qkv_pairs_kernel(steps, meta, normed, latent, grads, upper_t, lower_out, upper_out, low_sum, up_sum):
    step = pl.program_id(0)
    rows = normed.shape[0]
    select = adapter_select(meta, step * rows, rows, 3)
    lat = keep_low(
        select, jnp.concatenate([nn(grads[m], upper_t[m]) for m in range(3)], 1)
    )

    @pl.when(step == 0)
    def _():
        low_sum[...] = jnp.zeros_like(low_sum)
        up_sum[...] = jnp.zeros_like(up_sum)

    low_sum[...] += tn(lat, normed[...])
    for m in range(3):
        up_sum[m] += tn(latent[:, m * LANES : (m + 1) * LANES], grads[m])

    @pl.when(step == steps - 1)
    def _():
        lower_out[...] = low_sum[...].T.astype(BF16)
        for m in range(3):
            upper_out[m] = up_sum[m].T.astype(BF16)


def qkv_pairs(meta, normed, latent, grads, upper_t):
    total, width = normed.shape
    own = grads.shape[2]
    rows = 512
    steps = total // rows
    return pl.pallas_call(
        functools.partial(qkv_pairs_kernel, steps),
        grid_spec=pltpu.PrefetchScalarGridSpec(
            num_scalar_prefetch=1,
            grid=(steps,),
            in_specs=[
                pl.BlockSpec((rows, width), lambda s, *_: (s, 0)),
                pl.BlockSpec((rows, 3 * LANES), lambda s, *_: (s, 0)),
                pl.BlockSpec((3, rows, own), lambda s, *_: (0, s, 0)),
                whole(*upper_t.shape),
            ],
            out_specs=[whole(width, 3 * LANES), whole(3, own, LANES)],
            scratch_shapes=[
                pltpu.VMEM((3 * LANES, width), F32),
                pltpu.VMEM((3, LANES, own), F32),
            ],
        ),
        out_shape=[
            jax.ShapeDtypeStruct((width, 3 * LANES), BF16),
            jax.ShapeDtypeStruct((3, own, LANES), BF16),
        ],
        compiler_params=params(),
        cost_estimate=cost(2 * total * width * 3 * LANES * 2, 10e6),
        name="qkv_pairs",
    )(meta, normed, latent, grads, upper_t)


def swap(values, bit):
    size = lax.axis_size("tensor")
    return lax.ppermute(values, "tensor", [(i, i ^ bit) for i in range(size)])


def swap_dp(values, bits):
    size = lax.axis_size("dp")
    return lax.ppermute(values, "dp", [(i, i ^ bits) for i in range(size)])


def gather_tensor(values):
    far = swap(values, 2)
    return [values, swap(values, 1), far, swap(far, 1)]


def tensor_order(pieces, place):
    stacked = jnp.stack(pieces)
    for bit in (1, 2):
        moved = stacked.reshape((2, 2) + pieces[0].shape)[:, ::-1] if bit == 1 else (
            stacked.reshape((2, 2) + pieces[0].shape)[::-1]
        )
        stacked = jnp.where((place & bit) != 0, moved.reshape(stacked.shape), stacked)
    return stacked


def gather_dp(values):
    size = lax.axis_size("dp")
    if size != 8:
        return lax.all_gather(values, "dp", axis=0, tiled=False)
    place = lax.axis_index("dp")
    near = [values] + [swap_dp(values, 2 * k) for k in (1, 2, 3)]
    result = jnp.zeros((size,) + values.shape, values.dtype)
    for k, piece in enumerate(near):
        result = lax.dynamic_update_index_in_dim(result, piece, place ^ (2 * k), 0)
        result = lax.dynamic_update_index_in_dim(result, swap_dp(piece, 1), place ^ (2 * k + 1), 0)
    return result


def exchange_dp(values):
    return lax.all_to_all(values, "dp", split_axis=0, concat_axis=0, tiled=True)


def norm_gradient(values, gain, grad):
    inverse = lax.rsqrt(jnp.mean(values * values, -1, keepdims=True) + EPSILON)
    scaled = gain * grad
    return inverse * scaled - values * (
        inverse * inverse * inverse * jnp.mean(scaled * values, -1, keepdims=True)
    )


def after(values, *earlier):
    return lax.optimization_barrier((values,) + earlier)[0]


def per_device(
    tokens,
    cotangent,
    attention_gain,
    feedforward_gain,
    query_key_value_matrix,
    output_matrix,
    feedforward_matrix,
    down_matrix,
    memory_retention,
    memory_step_size,
    sequence_length,
    sequence_permutation,
    sequence_adapter,
    head_span_window,
    query_key_value_lower,
    query_key_value_upper,
    output_adapter_lower,
    output_adapter_upper,
    feedforward_adapter_lower,
    feedforward_adapter_upper,
    down_adapter_lower,
    down_adapter_upper,
):
    groups = lax.axis_size("dp")
    group = lax.axis_index("dp")
    place = lax.axis_index("tensor")
    quarter, width = tokens.shape
    slot = quarter // groups
    heads_own = query_key_value_matrix.shape[2]
    hidden = feedforward_matrix.shape[2]

    members = lax.dynamic_slice_in_dim(sequence_permutation, group * SEQ_G, SEQ_G)
    hits = members[:, None] == jnp.arange(sequence_length.shape[0], dtype=jnp.int32)[None, :]
    lengths = jnp.sum(jnp.where(hits, sequence_length[None, :], 0), 1)
    adapters = jnp.sum(jnp.where(hits, sequence_adapter[None, :], 0), 1)
    head_at = place * 2
    windows = lax.dynamic_slice_in_dim(head_span_window, head_at, 2)
    meta = jnp.concatenate(
        [
            jnp.stack([lengths[0], lengths[0] + lengths[1]]),
            adapters,
            windows,
            jnp.stack([place, jnp.int32(0)]),
        ]
    ).astype(jnp.int32)
    at_piece = lambda k: meta.at[8].set((place ^ k) * quarter)
    fmeta = jnp.concatenate(
        [
            lax.dynamic_slice_in_dim(memory_retention, head_at, 2),
            lax.dynamic_slice_in_dim(memory_step_size, head_at, 2) / STRETCH,
        ]
    )
    spans = (2, 3, 4, 5)

    arrived = exchange_dp(tokens.reshape(groups, slot, width)).reshape(quarter, width)
    token_pieces = gather_tensor(arrived)

    def own_upper(values):
        return jnp.swapaxes(values, -1, -2)

    axes = ("dp", "tensor")
    tensors = lax.axis_size("tensor")
    to_user = [(j, (j % groups) * tensors + j // groups) for j in range(groups * tensors)]
    to_owner = [(b, a) for a, b in to_user]

    def flat(parts):
        return jnp.concatenate([v.reshape(-1, LANES) for v in parts], 0)

    def unflat(values, shapes):
        out, at = [], 0
        for shape in shapes:
            size = 1
            for n in shape[:-1]:
                size *= n
            out.append(lax.slice_in_dim(values, at, at + size, axis=values.ndim - 2).reshape(values.shape[:-2] + shape))
            at += size
        return out

    share = query_key_value_lower.shape[1]
    up_share = feedforward_adapter_upper.shape[2]
    qkv_upper_own = lax.ppermute(own_upper(query_key_value_upper), axes, to_user)
    qkv_lower_all = tensor_order(gather_tensor(query_key_value_lower), place)
    qkv_lower_all = jnp.swapaxes(qkv_lower_all, 0, 1).reshape(3, tensors * share, LANES)
    qkv_pack = gather_dp(flat([qkv_lower_all, qkv_upper_own]))
    qkv_a, qkv_b = unflat(qkv_pack, [(3, tensors * share, LANES), (3, share, LANES)])
    qkv_a = jnp.moveaxis(qkv_a, 1, 2).reshape(width, 3 * LANES)
    qkv_b = jnp.moveaxis(qkv_b, 0, 1).reshape(3, heads_own, LANES)
    qkv_w = jnp.moveaxis(gather_dp(query_key_value_matrix), 0, 1).reshape(3, width, heads_own)

    cot_arrived = exchange_dp(
        after(cotangent, token_pieces[3]).reshape(groups, slot, width)
    ).reshape(quarter, width)
    grad_pieces = gather_tensor(cot_arrived)
    out_t = output_matrix.T
    ffn_pack = jnp.concatenate([feedforward_matrix, down_matrix.T[None]], 0)
    ffn_w = jnp.moveaxis(lax.all_gather(ffn_pack, "dp", axis=0, tiled=False), 0, 1).reshape(3, width, hidden)
    out_pair = jnp.concatenate([out_t, swap(out_t, 2)], 1)
    out_w = gather_dp(out_pair).reshape(width, 2 * heads_own)
    full_shapes = [(2, share, LANES), (share, LANES), (share, LANES)]
    full = tensor_order(
        gather_tensor(
            flat([feedforward_adapter_lower, output_adapter_upper.T, down_adapter_upper.T])
        ),
        place,
    )
    ffn_a, out_b, down_b = unflat(full, full_shapes)
    user = lax.ppermute(
        flat([own_upper(feedforward_adapter_upper), down_adapter_lower, output_adapter_lower]),
        axes,
        to_user,
    )
    ffn_b, down_a, out_a = unflat(user, [(2, up_share, LANES), (up_share, LANES), (share, LANES)])
    late_shapes = [
        (2, tensors * share, LANES),
        (tensors * share, LANES),
        (tensors * share, LANES),
        (2, up_share, LANES),
        (up_share, LANES),
        (share, LANES),
        (share, LANES),
    ]
    late = lax.all_gather(
        flat([jnp.swapaxes(ffn_a, 0, 1), out_b, down_b, ffn_b, down_a, out_a, swap(out_a, 2)]),
        "dp",
        axis=0,
        tiled=False,
    )
    ffn_a, out_b, down_b, ffn_b, down_a, out_a, out_a_far = unflat(late, late_shapes)
    ffn_a = jnp.moveaxis(ffn_a, 1, 2).reshape(width, 2 * LANES)
    out_b = out_b.reshape(width, LANES)
    down_b = down_b.reshape(width, LANES)
    ffn_b = jnp.moveaxis(ffn_b, 0, 1).reshape(2, hidden, LANES)
    down_a = down_a.reshape(hidden, LANES)
    out_a = jnp.concatenate([out_a.reshape(heads_own, LANES), out_a_far.reshape(heads_own, LANES)], 0)

    gain_one = attention_gain.reshape(1, width)
    gain_two = feedforward_gain.reshape(1, width)
    normed, qkv, qkv_latent = project_qkv(meta, token_pieces, gain_one, qkv_w, qkv_a, qkv_b)
    heads, attended, log_total, states = mixer_forward(meta, fmeta, qkv, spans)
    half = 2 * quarter
    chip = place // 2
    heads_far = swap(lax.dynamic_slice_in_dim(heads, (1 - chip) * half, half, 0), 2)
    rows_of = lambda values, k: lax.dynamic_slice_in_dim(values, (place ^ k) * quarter, quarter, 0)
    rows_far = lambda k: lax.dynamic_slice_in_dim(heads_far, ((place ^ k) % 2) * quarter, quarter, 0)
    heads_mine = [rows_of(heads, k) for k in (0, 1)]
    heads_other = [rows_far(k) for k in (0, 1)]
    branch_mate, out_latent_mate = out_forward(at_piece(1), heads_mine[1], heads_other[1], out_w, out_a, out_b)
    branch_got = swap(branch_mate, 1)
    branch_own, out_latent_own = out_forward(at_piece(0), heads_mine[0], heads_other[0], out_w, out_a, out_b)
    stream = arrived.astype(F32)
    hidden_one = stream + (branch_own.astype(F32) + branch_got.astype(F32))
    normed_two = (
        hidden_one
        * lax.rsqrt(jnp.mean(hidden_one * hidden_one, -1, keepdims=True) + EPSILON)
        * gain_two
    ).astype(BF16)
    two = gather_tensor(normed_two)

    near = ffn(meta, 0, two[:2], grad_pieces[:2], ffn_w, ffn_a, ffn_b, down_a, down_b)
    far = ffn(meta, 2, two[2:], grad_pieces[2:], ffn_w, ffn_a, ffn_b, down_a, down_b)

    def scatter(own, mate, far_mate, across):
        onward = (far_mate.astype(F32) + swap(across, 1).astype(F32)).astype(BF16)
        return own.astype(F32) + swap(mate, 1).astype(F32) + swap(onward, 2).astype(F32)

    grad_two = scatter(near[0], near[1], far[0], far[1])
    grad_out = cot_arrived.astype(F32)
    grad_one = grad_out + norm_gradient(hidden_one, gain_two, grad_two)
    grad_one_low = grad_one.astype(BF16)

    y_near, down_latent_near = down(meta, 0, quarter, near[2], ffn_w, down_a, down_b)
    y_far, down_latent_far = down(meta, 2, quarter, far[2], ffn_w, down_a, down_b)
    ffn_branch = scatter(y_near[:quarter], y_near[quarter:], y_far[:quarter], y_far[quarter:])
    mixed_rows = (hidden_one + ffn_branch).astype(BF16)
    mixed = exchange_dp(mixed_rows.reshape(groups, slot, width)).reshape(quarter, width)
    ffn_terms = []
    for part, down_latent, x, grad in (
        (near, down_latent_near, two[:2], grad_pieces[:2]),
        (far, down_latent_far, two[2:], grad_pieces[2:]),
    ):
        _, _, sw, d_gate, d_up, lat, lat_grad, down_lat_grad = part
        ffn_terms.append(
            pair_sums(
                [
                    (lat_grad, jnp.concatenate(x, 0)),
                    (lat[:, :LANES], d_gate),
                    (lat[:, LANES:], d_up),
                    (down_lat_grad, sw),
                    (down_latent, jnp.concatenate(grad, 0)),
                ]
            )
        )
    ffn_terms = [(a.astype(F32) + b.astype(F32)).astype(BF16) for a, b in zip(*ffn_terms)]

    grad_mate = swap(grad_one_low, 1)
    back_own = out_backward(at_piece(0), grad_one_low, out_w, out_a, out_b)
    back_mate = out_backward(at_piece(1), grad_mate, out_w, out_a, out_b)
    got_own, got_mate = swap(back_own[1], 2), swap(back_mate[1], 2)
    heads_grad = jnp.stack([back_own[0], back_mate[0], got_own, got_mate])
    qkv_grads = mixer_backward(meta, fmeta, qkv, heads_grad, attended, log_total, states, spans)
    out_terms = pair_sums(
        [
            (jnp.concatenate([back_own[2], back_mate[2]], 0), jnp.concatenate([jnp.concatenate([heads_mine[0], heads_other[0]], 1), jnp.concatenate([heads_mine[1], heads_other[1]], 1)], 0)),
            (jnp.concatenate([out_latent_own, out_latent_mate], 0), jnp.concatenate([grad_one_low, grad_mate], 0)),
        ]
    )

    terms = [qkv_backward(meta, k, quarter, qkv_grads, qkv_w, qkv_a, qkv_b) for k in (3, 2, 1, 0)][::-1]
    grad_normed = scatter(*terms)
    qkv_lower_term, qkv_upper_term = qkv_pairs(meta, normed, qkv_latent, qkv_grads, qkv_b)
    grad_input = (grad_one + norm_gradient(stream, gain_one, grad_normed)).astype(BF16)
    token_grad = exchange_dp(grad_input.reshape(groups, slot, width)).reshape(quarter, width)

    def reduce_terms(full_terms, own_terms, own_far):
        columns = sum(v.shape[1] for v in full_terms)
        wide = jnp.concatenate(full_terms, 1).reshape(groups, tensors, share, columns)
        by_rel = lambda k: lax.dynamic_index_in_dim(wide, place ^ k, 1, keepdims=False)
        wide = scatter(by_rel(0), by_rel(1), by_rel(2), by_rel(3)).astype(BF16)
        parts = [wide[:, :, i * LANES : (i + 1) * LANES] for i in range(columns // LANES)]
        if own_far is not None:
            mine, other = own_far
            own_terms = own_terms + [(mine.astype(F32) + swap(other, 2).astype(F32)).astype(BF16)]
        pack = jnp.concatenate(parts + own_terms, 1)
        summed = jnp.sum(exchange_dp(pack).astype(F32), 0)
        cut = share * len(parts)
        own = lax.ppermute(summed[cut:], axes, to_owner)
        return summed[:cut].reshape(len(parts), share, LANES), own

    ffn_full, ffn_own = reduce_terms(
        [ffn_terms[0], out_terms[1], ffn_terms[4]],
        [
            ffn_terms[1].reshape(groups, up_share, LANES),
            ffn_terms[2].reshape(groups, up_share, LANES),
            ffn_terms[3].reshape(groups, up_share, LANES),
        ],
        [v.reshape(groups, share, LANES) for v in (out_terms[0][:heads_own], out_terms[0][heads_own:])],
    )
    qkv_full, qkv_own = reduce_terms(
        [qkv_lower_term],
        [jnp.moveaxis(qkv_upper_term.reshape(3, groups, share, LANES), 1, 0).reshape(groups, 3 * share, LANES)],
        None,
    )
    ffn_own_parts = [ffn_own[i * up_share : (i + 1) * up_share] for i in range(3)]
    return (
        mixed,
        token_grad,
        qkv_full,
        jnp.swapaxes(qkv_own.reshape(3, share, LANES), 1, 2),
        ffn_own[3 * up_share :],
        ffn_full[2].T,
        ffn_full[:2],
        jnp.stack([ffn_own_parts[0].T, ffn_own_parts[1].T]),
        ffn_own_parts[2],
        ffn_full[3].T,
    )


def solution(mesh):
    both = ("dp", "tensor")
    rows = P(both, None)
    lower = P(None, both, None)
    upper = P(None, None, both)
    return jax.shard_map(
        per_device,
        mesh=mesh,
        in_specs=(
            rows,
            rows,
            P(),
            P(),
            P(None, "dp", "tensor"),
            P("tensor", "dp"),
            P(None, "dp", "tensor"),
            P("tensor", "dp"),
            P(),
            P(),
            P(),
            P(),
            P(),
            P(),
            lower,
            upper,
            rows,
            P(None, both),
            lower,
            upper,
            rows,
            P(None, both),
        ),
        out_specs=(
            rows,
            rows,
            lower,
            upper,
            rows,
            P(None, both),
            lower,
            upper,
            rows,
            P(None, both),
        ),
        check_vma=False,
    )
```

```python
import functools

import jax
import jax.numpy as jnp
from jax import lax
from jax.experimental import pallas as pl
from jax.experimental.pallas import tpu as pltpu
from jax.sharding import PartitionSpec as P

HEAD_DIM = 128
ADAPTER_RANK = 16
STRETCH = 64
SEQ_G = 3
LANES = 128
BLOCK = 256
MEMORY_GAIN = 32.0
EPSILON = 1e-06
LOG2E = 1.4426950408889634
BF16 = jnp.bfloat16
F32 = jnp.float32
SLABS = 8


def nn(left, right):
    return jnp.dot(left, right, preferred_element_type=F32)


def nt(left, right, precision=None):
    return lax.dot_general(
        left, right, (((1,), (1,)), ((), ())), precision=precision, preferred_element_type=F32
    )


def tn(left, right):
    return lax.dot_general(left, right, (((0,), (0,)), ((), ())), preferred_element_type=F32)


def params(mebibytes):
    return pltpu.CompilerParams(
        dimension_semantics=("arbitrary",), vmem_limit_bytes=mebibytes * 1024 * 1024
    )


def cost(flops, moved):
    return pl.CostEstimate(flops=int(flops), bytes_accessed=int(moved), transcendentals=0)


def whole(*shape):
    return pl.BlockSpec(shape, lambda *_: (0,) * len(shape), pipeline_mode=pl.Buffered(1))


def adapter_select(meta, first_row, rows, copies):
    row = first_row + lax.broadcasted_iota(jnp.int32, (rows, 1), 0)
    adapter = jnp.where(row >= meta[1], meta[4], jnp.where(row >= meta[0], meta[3], meta[2]))
    column = lax.broadcasted_iota(jnp.int32, (rows, copies * LANES), 1)
    return (column % LANES) // ADAPTER_RANK == adapter


def keep_low(select, values):
    return jnp.where(select, values, 0.0).astype(BF16)


def qkv_kernel(meta, *refs):
    pieces, slabs, mates = refs[:4], refs[4 : 4 + SLABS], refs[4 + SLABS : 7 + SLABS]
    gain, normed, qkv, latent, weight_out, lower_out, upper_out, x_scr = refs[7 + SLABS :]
    step = pl.program_id(0)
    rows = x_scr.shape[0]
    slab, share = LANES, LANES // 4
    halves = weight_out.shape[2] // LANES
    upper_at = halves * 3 * slab
    lower_at = upper_at + 3 * share

    @pl.when(step == 0)
    def _():
        for k, ref in enumerate(slabs):
            place = meta[8] ^ k
            wide = pl.ds(pl.multiple_of(place * slab, slab), slab)
            thin = pl.ds(pl.multiple_of(place * share, share), share)
            for m in range(3):
                for half in range(halves):
                    at = (half * 3 + m) * slab
                    weight_out[m, wide, half * LANES : (half + 1) * LANES] = ref[at : at + slab, :]
                upper_out[m, thin, :] = ref[upper_at + m * share : upper_at + (m + 1) * share, :]
                lanes = slice(m * LANES, (m + 1) * LANES)
                for mate in range(4):
                    to = pl.multiple_of(place * slab + (meta[7] ^ mate) * share, share)
                    if mate == 0:
                        part = ref[lower_at + m * share : lower_at + (m + 1) * share, :]
                    else:
                        part = mates[mate - 1][k, m * share : (m + 1) * share, :]
                    lower_out[pl.ds(to, share), lanes] = part

    for k, x_ref in enumerate(pieces):

        @pl.when(step == k)
        def _(x_ref=x_ref):
            x_scr[...] = x_ref[...]

    values = x_scr[...].astype(F32)
    scale = lax.rsqrt(jnp.mean(values * values, -1, keepdims=True) + EPSILON)
    low = (values * scale * gain[...]).astype(BF16)
    normed[...] = low
    select = adapter_select(meta, (meta[7] ^ step) * rows, rows, 3)
    lat = keep_low(select, nn(low, lower_out[...]))
    latent[...] = lat
    for m in range(3):
        qkv[m] = (
            nn(low, weight_out[m]) + nt(lat[:, m * LANES : (m + 1) * LANES], upper_out[m])
        ).astype(BF16)


def project_qkv(meta, pieces, gain, slabs, mates, own):
    rows, width = pieces[0].shape
    total = rows * 4
    place = lambda step, meta: (meta[7] ^ step, 0)
    return pl.pallas_call(
        qkv_kernel,
        grid_spec=pltpu.PrefetchScalarGridSpec(
            num_scalar_prefetch=1,
            grid=(4,),
            in_specs=[whole(*v.shape) for v in pieces + slabs + mates]
            + [whole(1, width)],
            out_specs=[
                pl.BlockSpec((rows, width), place),
                pl.BlockSpec((3, rows, own), lambda step, meta: (0, meta[7] ^ step, 0)),
                pl.BlockSpec((rows, 3 * LANES), place),
                whole(3, width, own),
                whole(width, 3 * LANES),
                whole(3, own, LANES),
            ],
            scratch_shapes=[pltpu.VMEM((rows, width), BF16)],
        ),
        out_shape=[
            jax.ShapeDtypeStruct((total, width), BF16),
            jax.ShapeDtypeStruct((3, total, own), BF16),
            jax.ShapeDtypeStruct((total, 3 * LANES), BF16),
            jax.ShapeDtypeStruct((3, width, own), BF16),
            jax.ShapeDtypeStruct((width, 3 * LANES), BF16),
            jax.ShapeDtypeStruct((3, own, LANES), BF16),
        ],
        compiler_params=params(20),
        cost_estimate=cost(2 * total * width * (3 * own + 600), 4 * total * width),
        name="project_qkv",
    )(meta, *pieces, *slabs, *mates, gain)


def span_variants(count, spans, run):
    for n, blocks in enumerate(spans):
        if n == 0:
            condition = count <= blocks
        else:
            condition = count == blocks
        pl.when(condition)(functools.partial(run, blocks * BLOCK))


def stretch_columns(low, total_stretches):
    stretch = lax.broadcasted_iota(jnp.int32, low.shape, 0) // STRETCH
    zero = jnp.zeros_like(low)
    return jnp.concatenate(
        [jnp.where(stretch == n, low, zero) for n in range(total_stretches)], 1
    )


def unit_rows(values):
    inverse = lax.rsqrt(jnp.sum(values * values, -1, keepdims=True) + EPSILON)
    return values * inverse, inverse


def attend_forward_kernel(spans, meta, qkv, attended, log_total):
    block = pl.program_id(0)
    first_row = block * BLOCK
    start_two, start_three = meta[0], meta[1]
    row = first_row + lax.broadcasted_iota(jnp.int32, (BLOCK, 1), 0)
    begin = jnp.where(row >= start_three, start_three, jnp.where(row >= start_two, start_two, 0))
    first_begin = jnp.where(
        first_row >= start_three, start_three, jnp.where(first_row >= start_two, start_two, 0)
    )
    factor = HEAD_DIM ** (-0.5) * LOG2E

    for h in range(2):
        cols = slice(h * HEAD_DIM, (h + 1) * HEAD_DIM)
        window = meta[5 + h]
        low_key = jnp.maximum(row - window + 1, begin)
        first_key = jnp.maximum(first_row - window + 1, first_begin)
        count = block - first_key // BLOCK + 1

        def attend(span, cols=cols, low_key=low_key, h=h):
            start = pl.multiple_of(jnp.maximum(first_row + BLOCK - span, 0), BLOCK)
            query = qkv[0, pl.ds(pl.multiple_of(first_row, BLOCK), BLOCK), cols]
            key = qkv[1, pl.ds(start, span), cols]
            value = qkv[2, pl.ds(start, span), cols]
            score = nt(query, key)
            position = start + lax.broadcasted_iota(jnp.int32, (BLOCK, span), 1)
            score = jnp.where((position >= low_key) & (position <= row), score, -1e30)
            top = jnp.max(score, -1, keepdims=True)
            weight = jnp.exp2((score - top) * factor).astype(BF16)
            with_ones = jnp.concatenate([value, jnp.ones_like(value)], 1)
            both = nn(weight, with_ones)
            total = both[:, HEAD_DIM : HEAD_DIM + 1]
            attended[:, cols] = both[:, :HEAD_DIM] / both[:, HEAD_DIM:]
            logs = jnp.broadcast_to(top * factor + jnp.log2(total), (BLOCK, LANES))
            pick = jnp.where(lax.broadcasted_iota(jnp.int32, (8, LANES), 1) == 0, 1.0, 0.0)
            log_total[0, h : h + 1, :] = nt(pick, logs, lax.Precision.HIGHEST)[0:1]

        span_variants(count, spans, attend)


def attend_forward(meta, qkv, spans):
    total, own = qkv.shape[1:]
    blocks = total // BLOCK
    return pl.pallas_call(
        functools.partial(attend_forward_kernel, spans),
        grid_spec=pltpu.PrefetchScalarGridSpec(
            num_scalar_prefetch=1,
            grid=(blocks,),
            in_specs=[whole(*qkv.shape)],
            out_specs=[
                pl.BlockSpec((BLOCK, own), lambda b, *_: (b, 0)),
                pl.BlockSpec((1, 8, BLOCK), lambda b, *_: (b, 0, 0)),
            ],
        ),
        out_shape=[
            jax.ShapeDtypeStruct((total, own), F32),
            jax.ShapeDtypeStruct((blocks, 8, BLOCK), F32),
        ],
        compiler_params=params(12),
        cost_estimate=cost(4e9, 12e6),
        name="attend_forward",
    )(meta, qkv)


def memory_forward_kernel(meta, fmeta, qkv, attended, near, far, states, heads, state_scr):
    block = pl.program_id(0)
    first_row = block * BLOCK
    start_two, start_three = meta[0], meta[1]
    stretches = BLOCK // STRETCH

    @pl.when(block == 0)
    def _():
        state_scr[...] = jnp.zeros_like(state_scr)

    for h in range(2):
        cols = slice(h * HEAD_DIM, (h + 1) * HEAD_DIM)
        here = pl.ds(pl.multiple_of(first_row, BLOCK), BLOCK)
        query_unit, _ = unit_rows(qkv[0, here, cols].astype(F32))
        key_unit, _ = unit_rows(qkv[1, here, cols].astype(F32))
        query_low = query_unit.astype(BF16)
        key_low = key_unit.astype(BF16)
        by_stretch = stretch_columns(key_low, stretches)
        retention, step_size = fmeta[h], fmeta[2 + h]
        gram = (nn(key_unit.T.astype(BF16), by_stretch) * step_size).astype(BF16)
        written = nn(qkv[2, here, cols].astype(F32).T.astype(BF16), by_stretch) * step_size
        state = state_scr[h]
        for n in range(stretches):
            row_at = first_row + n * STRETCH
            keep = jnp.where((row_at == start_two) | (row_at == start_three), 0.0, 1.0)
            state = state * keep
            low = state.astype(BF16)
            states[n, h] = low
            rows = slice(n * STRETCH, (n + 1) * STRETCH)
            lanes = slice(n * HEAD_DIM, (n + 1) * HEAD_DIM)
            read = nt(query_low[rows], low)
            heads[rows, cols] = (attended[rows, cols] + MEMORY_GAIN * read).astype(BF16)
            state = retention * state - nn(low, gram[:, lanes]) + written[:, lanes]
        state_scr[h] = state

    half_blocks = near.shape[0] // BLOCK
    at = pl.ds(pl.multiple_of((block % half_blocks) * BLOCK, BLOCK), BLOCK)
    own_chip = block // half_blocks == meta[7] // 2

    @pl.when(own_chip)
    def _():
        near[at, :] = heads[...]

    @pl.when(jnp.logical_not(own_chip))
    def _():
        far[at, :] = heads[...]


def memory_forward(meta, fmeta, qkv, attended):
    total, own = qkv.shape[1:]
    blocks = total // BLOCK
    stretches = BLOCK // STRETCH
    return pl.pallas_call(
        memory_forward_kernel,
        grid_spec=pltpu.PrefetchScalarGridSpec(
            num_scalar_prefetch=2,
            grid=(blocks,),
            in_specs=[whole(*qkv.shape), pl.BlockSpec((BLOCK, own), lambda b, *_: (b, 0))],
            out_specs=[
                whole(total // 2, own),
                whole(total // 2, own),
                pl.BlockSpec(
                    (stretches, 2, HEAD_DIM, HEAD_DIM), lambda b, *_: (b, 0, 0, 0)
                ),
            ],
            scratch_shapes=[
                pltpu.VMEM((BLOCK, own), BF16),
                pltpu.VMEM((2, HEAD_DIM, HEAD_DIM), F32),
            ],
        ),
        out_shape=[
            jax.ShapeDtypeStruct((total // 2, own), BF16),
            jax.ShapeDtypeStruct((total // 2, own), BF16),
            jax.ShapeDtypeStruct((blocks * stretches, 2, HEAD_DIM, HEAD_DIM), BF16),
        ],
        compiler_params=params(10),
        cost_estimate=cost(2e9, 8e6),
        name="memory_forward",
    )(meta, fmeta, qkv, attended)


def mixer_backward_kernel(
    spans,
    blocks,
    meta,
    fmeta,
    qkv,
    grad_near,
    grad_far,
    attended,
    log_total,
    states,
    grads,
    grad_out,
    key_t,
    key_sum,
    value_sum,
    query_t,
    state_grad,
):
    block = blocks - 1 - pl.program_id(0)
    first_row = block * BLOCK
    start_two, start_three = meta[0], meta[1]
    row = first_row + lax.broadcasted_iota(jnp.int32, (1, BLOCK), 1)
    begin = jnp.where(row >= start_three, start_three, jnp.where(row >= start_two, start_two, 0))
    first_begin = jnp.where(
        first_row >= start_three, start_three, jnp.where(first_row >= start_two, start_two, 0)
    )
    scale = HEAD_DIM ** (-0.5)
    factor = scale * LOG2E
    stretches = BLOCK // STRETCH
    here = pl.ds(pl.multiple_of(first_row, BLOCK), BLOCK)
    per_piece = grad_near.shape[0] // 2 // BLOCK
    piece = (block // per_piece) ^ meta[7]
    at = pl.ds(
        pl.multiple_of(((piece % 2) * per_piece + block % per_piece) * BLOCK, BLOCK), BLOCK
    )

    @pl.when(piece < 2)
    def _():
        grad_out[...] = grad_near[at, :]

    @pl.when(piece >= 2)
    def _():
        grad_out[...] = grad_far[at, :]

    @pl.when(pl.program_id(0) == 0)
    def _():
        key_sum[...] = jnp.zeros_like(key_sum)
        value_sum[...] = jnp.zeros_like(value_sum)
        state_grad[...] = jnp.zeros_like(state_grad)
        for h in range(2):
            for b in range(blocks):
                rows = slice(b * BLOCK, (b + 1) * BLOCK)
                key = qkv[1, rows, h * HEAD_DIM : (h + 1) * HEAD_DIM]
                key_t[h, :, rows] = key.astype(F32).T.astype(BF16)

    for h in range(2):
        cols = slice(h * HEAD_DIM, (h + 1) * HEAD_DIM)
        window = meta[5 + h]
        low_key = jnp.maximum(row - window + 1, begin)
        first_key = jnp.maximum(first_row - window + 1, first_begin)
        count = block - first_key // BLOCK + 1
        product = grad_out[:, cols].astype(F32) * attended[:, cols]
        inner = nt(jnp.ones((8, HEAD_DIM), F32), product, lax.Precision.HIGHEST)[0:1]
        logs = log_total[0, h : h + 1, :]

        def attend(span, cols=cols, low_key=low_key, h=h, inner=inner, logs=logs):
            start = pl.multiple_of(jnp.maximum(first_row + BLOCK - span, 0), BLOCK)
            there = pl.ds(start, span)
            query = qkv[0, here, cols]
            grad = grad_out[:, cols]
            score = nt(qkv[1, there, cols], query)
            position = start + lax.broadcasted_iota(jnp.int32, (span, BLOCK), 0)
            allowed = (position >= low_key) & (position <= row)
            weight = jnp.where(allowed, jnp.exp2(score * factor - logs), 0.0)
            grad_weight = nt(qkv[2, there, cols], grad)
            grad_score = (weight * (grad_weight - inner)).astype(BF16)
            value_sum[h, there, :] += nn(weight.astype(BF16), grad)
            key_sum[h, there, :] += nn(grad_score, query)
            query_t[h] = nn(key_t[h, :, there], grad_score)

        span_variants(count, spans, attend)

    for h in range(2):
        cols = slice(h * HEAD_DIM, (h + 1) * HEAD_DIM)
        query_unit, query_inverse = unit_rows(qkv[0, here, cols].astype(F32))
        key_unit, key_inverse = unit_rows(qkv[1, here, cols].astype(F32))
        value = qkv[2, here, cols].astype(F32)
        key_low = key_unit.astype(BF16)
        grad = grad_out[:, cols]
        retention, step_size = fmeta[h], fmeta[2 + h]
        gram = (
            nn(key_unit.T.astype(BF16), stretch_columns(key_low, stretches)) * step_size
        ).astype(BF16)
        read_grad = MEMORY_GAIN * nn(
            grad.astype(F32).T.astype(BF16),
            stretch_columns(query_unit.astype(BF16), stretches),
        )
        carried = state_grad[h]
        query_grads, key_grads, value_grads = [], [], []
        for n in reversed(range(stretches)):
            row_at = first_row + n * STRETCH
            keep = jnp.where((row_at == start_two) | (row_at == start_three), 0.0, 1.0)
            rows = slice(n * STRETCH, (n + 1) * STRETCH)
            lanes = slice(n * HEAD_DIM, (n + 1) * HEAD_DIM)
            carried_low = carried.astype(BF16)
            state = states[n, h]
            key_rows = key_low[rows]
            pulled = nt(key_rows, carried_low)
            error = nt(key_rows, state) - value[rows]
            value_grads.append(step_size * pulled)
            key_grads.append(
                -step_size
                * (nn(pulled.astype(BF16), state) + nn(error.astype(BF16), carried_low))
            )
            query_grads.append(MEMORY_GAIN * nn(grad[rows], state))
            carried = keep * (
                read_grad[:, lanes] + retention * carried - nn(carried_low, gram[:, lanes])
            )
        state_grad[h] = carried
        query_unit_grad = jnp.concatenate(query_grads[::-1], 0)
        key_unit_grad = jnp.concatenate(key_grads[::-1], 0)
        value_grad = jnp.concatenate(value_grads[::-1], 0)
        query_memory = query_inverse * (
            query_unit_grad
            - query_unit * jnp.sum(query_unit * query_unit_grad, -1, keepdims=True)
        )
        key_memory = key_inverse * (
            key_unit_grad - key_unit * jnp.sum(key_unit * key_unit_grad, -1, keepdims=True)
        )
        grads[0, :, cols] = (scale * query_t[h].T + query_memory).astype(BF16)
        grads[1, :, cols] = (scale * key_sum[h, here, :] + key_memory).astype(BF16)
        grads[2, :, cols] = (value_sum[h, here, :] + value_grad).astype(BF16)


def mixer_backward(meta, fmeta, qkv, grad_near, grad_far, attended, log_total, states, spans):
    total, own = qkv.shape[1:]
    blocks = total // BLOCK
    stretches = BLOCK // STRETCH
    row_block = pl.BlockSpec((BLOCK, own), lambda s, *_: (blocks - 1 - s, 0))
    return pl.pallas_call(
        functools.partial(mixer_backward_kernel, spans, blocks),
        grid_spec=pltpu.PrefetchScalarGridSpec(
            num_scalar_prefetch=2,
            grid=(blocks,),
            in_specs=[
                whole(*qkv.shape),
                whole(*grad_near.shape),
                whole(*grad_far.shape),
                row_block,
                pl.BlockSpec((1, 8, BLOCK), lambda s, *_: (blocks - 1 - s, 0, 0)),
                pl.BlockSpec(
                    (stretches, 2, HEAD_DIM, HEAD_DIM), lambda s, *_: (blocks - 1 - s, 0, 0, 0)
                ),
            ],
            out_specs=pl.BlockSpec((3, BLOCK, own), lambda s, *_: (0, blocks - 1 - s, 0)),
            scratch_shapes=[
                pltpu.VMEM((BLOCK, own), BF16),
                pltpu.VMEM((2, HEAD_DIM, total), BF16),
                pltpu.VMEM((2, total, HEAD_DIM), F32),
                pltpu.VMEM((2, total, HEAD_DIM), F32),
                pltpu.VMEM((2, HEAD_DIM, BLOCK), F32),
                pltpu.VMEM((2, HEAD_DIM, HEAD_DIM), F32),
            ],
        ),
        out_shape=jax.ShapeDtypeStruct(qkv.shape, BF16),
        compiler_params=params(20),
        cost_estimate=cost(10e9, 16e6),
        name="mixer_backward",
    )(meta, fmeta, qkv, grad_near, grad_far, attended, log_total, states)


def unpack_kernel(meta, pack, f0, f1, f2, f3, used, wide, down, out, lower, out_upper, down_upper, out_lower):
    hidden = down.shape[0]
    width = out.shape[1]
    heads = out.shape[0] // 2
    share = LANES // 4
    first_out, first_lower = 3 * hidden, 3 * hidden + 2 * heads + 4 * share
    for p in range(SLABS):
        lanes = slice(p * LANES, (p + 1) * LANES)
        wide[:, lanes] = pack[p, : 2 * hidden, :]
        down[:, lanes] = pack[p, 2 * hidden : 3 * hidden, :]
        out[:, lanes] = pack[p, first_out : first_out + 2 * heads, :]
        for n in range(2):
            at = first_lower + n * share
            to = n * heads + p * share
            out_lower[to : to + share, :] = pack[p, at : at + share, :]
        for k, ref in enumerate((f0, f1, f2, f3)):
            to = pl.ds(pl.multiple_of(p * LANES + (meta[7] ^ k) * share, share), share)
            lower[to, :LANES] = ref[p, :share, :]
            lower[to, LANES:] = ref[p, share : 2 * share, :]
            out_upper[to, :] = ref[p, 2 * share : 3 * share, :]
            down_upper[to, :] = ref[p, 3 * share :, :]
    wide[:hidden, width:] = used[0]
    wide[hidden:, width:] = used[1]
    down[:, width:] = used[2]


def unpack(meta, pack, fulls, used, hidden, heads):
    width = SLABS * LANES
    shapes = [
        (2 * hidden, width + LANES),
        (hidden, width + LANES),
        (2 * heads, width),
        (width, 2 * LANES),
        (width, LANES),
        (width, LANES),
        (2 * heads, LANES),
    ]
    return pl.pallas_call(
        unpack_kernel,
        grid_spec=pltpu.PrefetchScalarGridSpec(
            num_scalar_prefetch=1,
            grid=(1,),
            in_specs=[whole(*v.shape) for v in (pack, *fulls, used)],
            out_specs=[whole(*v) for v in shapes],
        ),
        out_shape=[jax.ShapeDtypeStruct(v, BF16) for v in shapes],
        compiler_params=params(20),
        cost_estimate=cost(1e6, 14e6),
        name="unpack",
    )(meta, pack, *fulls, used)


def out_forward_kernel(meta, near, far, weight, lower, upper_t, own, mate, latent, heads):
    rows, columns = own.shape[0], near.shape[1]
    for k, out in enumerate((own, mate)):
        at = pl.ds(pl.multiple_of(((meta[7] % 2) ^ k) * rows, rows), rows)
        both = jnp.concatenate([near[at, :], far[at, :]], 1)
        here = slice(k * rows, (k + 1) * rows)
        heads[here, :] = both
        select = adapter_select(meta, (meta[7] ^ k) * rows, rows, 1)
        lat = keep_low(select, nn(both, lower[...]))
        latent[here, :] = lat
        out[...] = (nn(both, weight[...]) + nt(lat, upper_t[...])).astype(BF16)


def out_forward(meta, near, far, weight, lower, upper_t):
    rows, columns = near.shape[0] // 2, near.shape[1]
    width = upper_t.shape[0]
    return pl.pallas_call(
        out_forward_kernel,
        grid_spec=pltpu.PrefetchScalarGridSpec(
            num_scalar_prefetch=1,
            grid=(1,),
            in_specs=[whole(*v.shape) for v in (near, far, weight, lower, upper_t)],
            out_specs=[
                whole(rows, width),
                whole(rows, width),
                whole(2 * rows, LANES),
                whole(2 * rows, 2 * columns),
            ],
        ),
        out_shape=[
            jax.ShapeDtypeStruct((rows, width), BF16),
            jax.ShapeDtypeStruct((rows, width), BF16),
            jax.ShapeDtypeStruct((2 * rows, LANES), BF16),
            jax.ShapeDtypeStruct((2 * rows, 2 * columns), BF16),
        ],
        compiler_params=params(14),
        cost_estimate=cost(4 * rows * width * 640, 8e6),
        name="out_forward",
    )(meta, near, far, weight, lower, upper_t)


def out_backward_kernel(meta, grad_own, grad_mate, weight, lower, upper_t, mine, other, latent):
    rows, columns = grad_own.shape[0], mine.shape[1]
    for k, grad in enumerate((grad_own, grad_mate)):
        here = slice(k * rows, (k + 1) * rows)
        select = adapter_select(meta, (meta[7] ^ k) * rows, rows, 1)
        lat = keep_low(select, nn(grad[...], upper_t[...]))
        latent[here, :] = lat
        both = (nt(grad[...], weight[...]) + nt(lat, lower[...])).astype(BF16)
        mine[here, :] = both[:, :columns]
        other[here, :] = both[:, columns:]


def out_backward(meta, grad_own, grad_mate, weight, lower, upper_t):
    rows, width = grad_own.shape
    columns = lower.shape[0] // 2
    return pl.pallas_call(
        out_backward_kernel,
        grid_spec=pltpu.PrefetchScalarGridSpec(
            num_scalar_prefetch=1,
            grid=(1,),
            in_specs=[whole(*v.shape) for v in (grad_own, grad_mate, weight, lower, upper_t)],
            out_specs=[
                whole(2 * rows, columns),
                whole(2 * rows, columns),
                whole(2 * rows, LANES),
            ],
        ),
        out_shape=[
            jax.ShapeDtypeStruct((2 * rows, columns), BF16),
            jax.ShapeDtypeStruct((2 * rows, columns), BF16),
            jax.ShapeDtypeStruct((2 * rows, LANES), BF16),
        ],
        compiler_params=params(14),
        cost_estimate=cost(4 * rows * width * 640, 8e6),
        name="out_backward",
    )(meta, grad_own, grad_mate, weight, lower, upper_t)


def spread_shares(meta, turned, out, lanes):
    share = LANES // 4
    for mate in range(4):
        for p in range(SLABS):
            at = pl.multiple_of(p * LANES + (meta[7] ^ mate) * share, share)
            out[mate, p * share : (p + 1) * share, lanes] = turned[pl.ds(at, share), :]


def out_pairs_kernel(meta, heads, latent_grad, latent, grad_own, grad_mate, lower_out, upper_out, turned):
    rows = grad_own.shape[0]
    lower_out[...] = tn(latent_grad[...], heads[...]).T.astype(BF16)
    turned[...] = (
        (tn(latent[:rows], grad_own[...]) + tn(latent[rows:], grad_mate[...])).T
    ).astype(BF16)
    spread_shares(meta, turned, upper_out, slice(None))


def out_pairs(meta, heads, latent_grad, latent, grad_own, grad_mate):
    rows, width = grad_own.shape
    columns = heads.shape[1]
    return pl.pallas_call(
        out_pairs_kernel,
        grid_spec=pltpu.PrefetchScalarGridSpec(
            num_scalar_prefetch=1,
            grid=(1,),
            in_specs=[whole(*v.shape) for v in (heads, latent_grad, latent, grad_own, grad_mate)],
            out_specs=[whole(columns, LANES), whole(4, width // 4, LANES)],
            scratch_shapes=[pltpu.VMEM((width, LANES), BF16)],
        ),
        out_shape=[
            jax.ShapeDtypeStruct((columns, LANES), BF16),
            jax.ShapeDtypeStruct((4, width // 4, LANES), BF16),
        ],
        compiler_params=params(12),
        cost_estimate=cost(4 * rows * LANES * (columns + width), 5e6),
        name="out_pairs",
    )(meta, heads, latent_grad, latent, grad_own, grad_mate)


def ffn_kernel(
    first,
    meta,
    x0,
    x1,
    g0,
    g1,
    weight,
    down_weight,
    lower,
    down_upper_t,
    dx0,
    dx1,
    swiglu,
    pre_grads,
    latent,
    latent_grad,
    down_latent_grad,
):
    step = pl.program_id(0)
    rows = swiglu.shape[0]
    parts = x0.shape[0] // rows
    width, hidden = x0.shape[1], swiglu.shape[1]

    for k, (x_ref, g_ref, dx_ref) in enumerate(((x0, g0, dx0), (x1, g1, dx1))):

        @pl.when(step // parts == k)
        def _(k=k, x_ref=x_ref, g_ref=g_ref, dx_ref=dx_ref):
            part = step % parts
            at = pl.ds(pl.multiple_of(part * rows, rows), rows)
            first_row = (meta[7] ^ (first + k)) * (rows * parts) + part * rows
            select = adapter_select(meta, first_row, rows, 2)
            x = x_ref[at, :]
            grad = g_ref[at, :]
            lat = keep_low(select, nn(x, lower[...]))
            latent[...] = lat
            gate = nt(jnp.concatenate([x, lat[:, :LANES]], 1), weight[:hidden])
            up = nt(jnp.concatenate([x, lat[:, LANES:]], 1), weight[hidden:])
            down_lat = keep_low(select[:, :LANES], nn(grad, down_upper_t[...]))
            down_latent_grad[...] = down_lat
            wide_grad = nt(jnp.concatenate([grad, down_lat], 1), down_weight[...])
            sigmoid = 1.0 / (1.0 + jnp.exp(-gate))
            silu = gate * sigmoid
            swiglu[...] = (silu * up).astype(BF16)
            d_up = (wide_grad * silu).astype(BF16)
            d_gate = (wide_grad * up * (sigmoid * (1.0 + gate * (1.0 - sigmoid)))).astype(BF16)
            pre_grads[0] = d_gate
            pre_grads[1] = d_up
            lat_grad = keep_low(
                select,
                jnp.concatenate(
                    [nn(d_gate, weight[:hidden, width:]), nn(d_up, weight[hidden:, width:])], 1
                ),
            )
            latent_grad[...] = lat_grad
            dx_ref[at, :] = (
                nn(d_gate, weight[:hidden, :width])
                + nn(d_up, weight[hidden:, :width])
                + nt(lat_grad, lower[...])
            ).astype(BF16)


def ffn(meta, first, xs, grads, weight, down_weight, lower, down_upper_t):
    rows, width = xs[0].shape
    hidden = down_weight.shape[0]
    total = 2 * rows
    block = lambda columns: pl.BlockSpec((BLOCK, columns), lambda s, *_: (s, 0))
    return pl.pallas_call(
        functools.partial(ffn_kernel, first),
        grid_spec=pltpu.PrefetchScalarGridSpec(
            num_scalar_prefetch=1,
            grid=(total // BLOCK,),
            in_specs=[
                whole(*v.shape)
                for v in (*xs, *grads, weight, down_weight, lower, down_upper_t)
            ],
            out_specs=[whole(rows, width)] * 2
            + [
                block(hidden),
                pl.BlockSpec((2, BLOCK, hidden), lambda s, *_: (0, s, 0)),
                block(2 * LANES),
                block(2 * LANES),
                block(LANES),
            ],
        ),
        out_shape=[jax.ShapeDtypeStruct((rows, width), BF16)] * 2
        + [
            jax.ShapeDtypeStruct((total, hidden), BF16),
            jax.ShapeDtypeStruct((2, total, hidden), BF16),
            jax.ShapeDtypeStruct((total, 2 * LANES), BF16),
            jax.ShapeDtypeStruct((total, 2 * LANES), BF16),
            jax.ShapeDtypeStruct((total, LANES), BF16),
        ],
        compiler_params=params(28),
        cost_estimate=cost(2 * total * width * hidden * 6.0, 14e6),
        name="ffn",
    )(meta, *xs, *grads, weight, down_weight, lower, down_upper_t)


def ffn_rest_kernel(steps, meta, *refs):
    xs, grads, refs = refs[:4], refs[4:8], refs[8:]
    near, far, refs = refs[:5], refs[5:10], refs[10:]
    weight, upper_t = refs[:2]
    branches, refs = refs[2:6], refs[6:]
    full_out, own_out, x_sum, gate_sum, up_sum, down_sum, branch_sum, turned = refs
    step = pl.program_id(0)
    hidden, rows = weight.shape[0], xs[0].shape[0]
    width = xs[0].shape[1]

    @pl.when(step == 0)
    def _():
        for total in (x_sum, gate_sum, up_sum, down_sum, branch_sum):
            total[...] = jnp.zeros_like(total)

    for k in range(4):

        @pl.when(step == k)
        def _(k=k):
            swiglu, pre_grads, latent, latent_grad, down_latent_grad = near if k < 2 else far
            at = slice((k % 2) * rows, (k % 2 + 1) * rows)
            wide = swiglu[at, :]
            select = adapter_select(meta, (meta[7] ^ k) * rows, rows, 1)
            lat = keep_low(select, nn(wide, weight[:, width:]))
            branches[k][...] = (nn(wide, weight[:, :width]) + nt(lat, upper_t[...])).astype(BF16)
            x_sum[...] += tn(latent_grad[at, :], xs[k][...])
            gate_sum[:, :hidden] += tn(latent[at, :LANES], pre_grads[0, at, :])
            up_sum[:, :hidden] += tn(latent[at, LANES:], pre_grads[1, at, :])
            down_sum[:, :hidden] += tn(down_latent_grad[at, :], wide)
            branch_sum[...] += tn(lat, grads[k][...])

    @pl.when(step == steps - 1)
    def _():
        for lanes, total in ((slice(0, 2 * LANES), x_sum), (slice(2 * LANES, 3 * LANES), branch_sum)):
            turned[:, lanes] = total[...].T.astype(BF16)
        spread_shares(meta, turned, full_out, slice(None))
        for n, total in enumerate((gate_sum, up_sum, down_sum)):
            own_out[n] = total[...].T[:hidden].astype(BF16)


def ffn_rest(meta, xs, grads, near, far, weight, upper_t):
    rows, width = xs[0].shape
    hidden = weight.shape[0]
    padded = -(-hidden // LANES) * LANES
    operands = (*xs, *grads, *near, *far, weight, upper_t)
    return pl.pallas_call(
        functools.partial(ffn_rest_kernel, 4),
        grid_spec=pltpu.PrefetchScalarGridSpec(
            num_scalar_prefetch=1,
            grid=(4,),
            in_specs=[whole(*v.shape) for v in operands],
            out_specs=[whole(rows, width)] * 4
            + [whole(4, width // 4, 3 * LANES), whole(3, hidden, LANES)],
            scratch_shapes=[
                pltpu.VMEM((2 * LANES, width), F32),
                pltpu.VMEM((LANES, padded), F32),
                pltpu.VMEM((LANES, padded), F32),
                pltpu.VMEM((LANES, padded), F32),
                pltpu.VMEM((LANES, width), F32),
                pltpu.VMEM((width, 3 * LANES), BF16),
            ],
        ),
        out_shape=[jax.ShapeDtypeStruct((rows, width), BF16)] * 4
        + [
            jax.ShapeDtypeStruct((4, width // 4, 3 * LANES), BF16),
            jax.ShapeDtypeStruct((3, hidden, LANES), BF16),
        ],
        compiler_params=params(36),
        cost_estimate=cost(8 * rows * width * hidden * 2.3, 30e6),
        name="ffn_rest",
    )(meta, *operands)


def qkv_backward_kernel(first, meta, grads0, grads1, weight, lower, upper_t, dx0, dx1):
    rows = dx0.shape[0]
    for k, (grads, dx) in enumerate(((grads0, dx0), (grads1, dx1))):
        select = adapter_select(meta, (meta[7] ^ (first + k)) * rows, rows, 3)
        lat = keep_low(
            select, jnp.concatenate([nn(grads[m], upper_t[m]) for m in range(3)], 1)
        )
        total = nt(lat, lower[...])
        for m in range(3):
            total += nt(grads[m], weight[m])
        dx[...] = total.astype(BF16)


def qkv_backward(meta, first, rows, grads, weight, lower, upper_t):
    own = grads.shape[2]
    width = lower.shape[0]
    piece = lambda k: pl.BlockSpec((3, rows, own), lambda s, meta: (0, meta[7] ^ (first + k), 0))
    return pl.pallas_call(
        functools.partial(qkv_backward_kernel, first),
        grid_spec=pltpu.PrefetchScalarGridSpec(
            num_scalar_prefetch=1,
            grid=(1,),
            in_specs=[
                piece(0),
                piece(1),
                whole(*weight.shape),
                whole(*lower.shape),
                whole(*upper_t.shape),
            ],
            out_specs=[whole(rows, width)] * 2,
        ),
        out_shape=[jax.ShapeDtypeStruct((rows, width), BF16)] * 2,
        compiler_params=params(16),
        cost_estimate=cost(4 * rows * width * 50, 4e5),
        name="qkv_backward",
    )(meta, grads, grads, weight, lower, upper_t)


def qkv_pairs_kernel(steps, meta, normed, latent, grads, upper_t, lower_out, upper_out, low_sum, up_sum, turned):
    step = pl.program_id(0)
    rows = normed.shape[0]
    select = adapter_select(meta, step * rows, rows, 3)
    lat = keep_low(
        select, jnp.concatenate([nn(grads[m], upper_t[m]) for m in range(3)], 1)
    )

    @pl.when(step == 0)
    def _():
        low_sum[...] = jnp.zeros_like(low_sum)
        up_sum[...] = jnp.zeros_like(up_sum)

    low_sum[...] += tn(lat, normed[...])
    for m in range(3):
        up_sum[m] += tn(latent[:, m * LANES : (m + 1) * LANES], grads[m])

    @pl.when(step == steps - 1)
    def _():
        turned[...] = low_sum[...].T.astype(BF16)
        spread_shares(meta, turned, lower_out, slice(None))
        for m in range(3):
            upper_out[m] = up_sum[m].T.astype(BF16)


def qkv_pairs(meta, normed, latent, grads, upper_t):
    total, width = normed.shape
    own = grads.shape[2]
    rows = 1024
    steps = total // rows
    return pl.pallas_call(
        functools.partial(qkv_pairs_kernel, steps),
        grid_spec=pltpu.PrefetchScalarGridSpec(
            num_scalar_prefetch=1,
            grid=(steps,),
            in_specs=[
                pl.BlockSpec((rows, width), lambda s, *_: (s, 0)),
                pl.BlockSpec((rows, 3 * LANES), lambda s, *_: (s, 0)),
                pl.BlockSpec((3, rows, own), lambda s, *_: (0, s, 0)),
                whole(*upper_t.shape),
            ],
            out_specs=[whole(4, width // 4, 3 * LANES), whole(3, own, LANES)],
            scratch_shapes=[
                pltpu.VMEM((3 * LANES, width), F32),
                pltpu.VMEM((3, LANES, own), F32),
                pltpu.VMEM((width, 3 * LANES), BF16),
            ],
        ),
        out_shape=[
            jax.ShapeDtypeStruct((4, width // 4, 3 * LANES), BF16),
            jax.ShapeDtypeStruct((3, own, LANES), BF16),
        ],
        compiler_params=params(20),
        cost_estimate=cost(2 * total * width * 20, 4e5),
        name="qkv_pairs",
    )(meta, normed, latent, grads, upper_t)


def join_norm_kernel(stream, own, got, gain, hidden, normed):
    values = stream[...].astype(F32) + (own[...].astype(F32) + got[...].astype(F32))
    hidden[...] = values
    scale = lax.rsqrt(jnp.mean(values * values, -1, keepdims=True) + EPSILON)
    normed[...] = (values * scale * gain[...]).astype(BF16)


def join_norm(stream, own, got, gain):
    rows, width = stream.shape
    return pl.pallas_call(
        join_norm_kernel,
        grid=(1,),
        in_specs=[whole(*v.shape) for v in (stream, own, got, gain)],
        out_specs=[whole(rows, width)] * 2,
        out_shape=[
            jax.ShapeDtypeStruct((rows, width), F32),
            jax.ShapeDtypeStruct((rows, width), BF16),
        ],
        compiler_params=params(12),
        cost_estimate=cost(1e6, 6e6),
        name="join_norm",
    )(stream, own, got, gain)


def norm_gradient_kernel(straight, values, own, near, far, gain, *outs):
    x = values[...].astype(F32)
    grad = own[...].astype(F32) + near[...].astype(F32) + far[...].astype(F32)
    inverse = lax.rsqrt(jnp.mean(x * x, -1, keepdims=True) + EPSILON)
    scaled = gain[...] * grad
    inner = jnp.mean(scaled * x, -1, keepdims=True)
    result = straight[...].astype(F32) + (
        inverse * scaled - x * (inverse * inverse * inverse * inner)
    )
    for out in outs:
        out[...] = result.astype(out.dtype)


def norm_gradient(straight, values, own, near, far, gain, kinds):
    rows, width = values.shape
    operands = (straight, values, own, near, far, gain)
    return pl.pallas_call(
        norm_gradient_kernel,
        grid=(1,),
        in_specs=[whole(*v.shape) for v in operands],
        out_specs=[whole(rows, width)] * len(kinds),
        out_shape=[jax.ShapeDtypeStruct((rows, width), kind) for kind in kinds],
        compiler_params=params(16),
        cost_estimate=cost(1e6, 9e6),
        name="norm_gradient",
    )(*operands)


def swap(values, bit):
    size = lax.axis_size("tensor")
    return lax.ppermute(values, "tensor", [(i, i ^ bit) for i in range(size)])


def swap_dp(values, bits):
    size = lax.axis_size("dp")
    return lax.ppermute(values, "dp", [(i, i ^ bits) for i in range(size)])


def gather_tensor(values):
    far = swap(values, 2)
    return [values, swap(values, 1), far, swap(far, 1)]


def tensor_order(pieces, place):
    stacked = jnp.stack(pieces)
    for bit in (1, 2):
        moved = stacked.reshape((2, 2) + pieces[0].shape)[:, ::-1] if bit == 1 else (
            stacked.reshape((2, 2) + pieces[0].shape)[::-1]
        )
        stacked = jnp.where((place & bit) != 0, moved.reshape(stacked.shape), stacked)
    return stacked


def gather_slabs(values):
    near = [values] + [swap_dp(values, 2 * k) for k in (1, 2, 3)]
    result = []
    for piece in near:
        result += [piece, swap_dp(piece, 1)]
    return result


def pieces_dp(values):
    size = lax.axis_size("dp")
    if size != SLABS:
        exchanged = exchange_dp(values)
        return [exchanged[k] for k in range(size)]
    place = lax.axis_index("dp")
    sent = [lax.dynamic_index_in_dim(values, place ^ k, 0, keepdims=False) for k in range(size)]
    return sent[:1] + [swap_dp(sent[k], k) for k in range(1, size)]


def exchange_dp(values):
    return lax.all_to_all(values, "dp", split_axis=0, concat_axis=0, tiled=True)


def after(values, *earlier):
    return lax.optimization_barrier((values,) + earlier)[0]


def together(*values):
    return lax.optimization_barrier(values)


def per_device(
    tokens,
    cotangent,
    attention_gain,
    feedforward_gain,
    query_key_value_matrix,
    output_matrix,
    feedforward_matrix,
    down_matrix,
    memory_retention,
    memory_step_size,
    sequence_length,
    sequence_permutation,
    sequence_adapter,
    head_span_window,
    query_key_value_lower,
    query_key_value_upper,
    output_adapter_lower,
    output_adapter_upper,
    feedforward_adapter_lower,
    feedforward_adapter_upper,
    down_adapter_lower,
    down_adapter_upper,
):
    groups = lax.axis_size("dp")
    group = lax.axis_index("dp")
    place = lax.axis_index("tensor")
    quarter, width = tokens.shape
    slot = quarter // groups
    heads_own = query_key_value_matrix.shape[2]
    hidden = feedforward_matrix.shape[2]

    members = lax.dynamic_slice_in_dim(sequence_permutation, group * SEQ_G, SEQ_G)
    hits = members[:, None] == jnp.arange(sequence_length.shape[0], dtype=jnp.int32)[None, :]
    lengths = jnp.sum(jnp.where(hits, sequence_length[None, :], 0), 1)
    adapters = jnp.sum(jnp.where(hits, sequence_adapter[None, :], 0), 1)
    head_at = place * 2
    windows = lax.dynamic_slice_in_dim(head_span_window, head_at, 2)
    meta = jnp.concatenate(
        [
            jnp.stack([lengths[0], lengths[0] + lengths[1]]),
            adapters,
            windows,
            jnp.stack([place, group if groups == SLABS else jnp.zeros_like(group)]),
        ]
    ).astype(jnp.int32)
    fmeta = jnp.concatenate(
        [
            lax.dynamic_slice_in_dim(memory_retention, head_at, 2),
            lax.dynamic_slice_in_dim(memory_step_size, head_at, 2) / STRETCH,
        ]
    )
    spans = (2, 3, 4, 5)
    axes = ("dp", "tensor")
    tensors = lax.axis_size("tensor")
    to_user = [(j, (j % groups) * tensors + j // groups) for j in range(groups * tensors)]
    to_owner = [(b, a) for a, b in to_user]
    share = query_key_value_lower.shape[1]
    up_share = feedforward_adapter_upper.shape[2]
    turn = lambda values: jnp.swapaxes(values, -1, -2)

    def flat(*parts):
        return jnp.concatenate([v.reshape(-1, LANES) for v in parts], 0)

    arrived = exchange_dp(tokens.reshape(groups, slot, width)).reshape(quarter, width)
    token_pieces = gather_tensor(arrived)
    if groups == SLABS:
        halves = jnp.moveaxis(
            query_key_value_matrix.reshape(3, width // groups, heads_own // LANES, LANES), 2, 0
        )
        pack = flat(halves, lax.ppermute(turn(query_key_value_upper), axes, to_user), query_key_value_lower)
        slabs = gather_slabs(after(pack, arrived))
        lower_rows = pack.shape[0] - 3 * share
        mates = gather_tensor(jnp.stack([v[lower_rows:] for v in slabs]))[1:]
    else:
        halves = lax.all_gather(query_key_value_matrix, "dp", axis=1, tiled=True)
        halves = jnp.moveaxis(halves.reshape(3, SLABS, LANES, heads_own // LANES, LANES), (1, 3), (0, 1))
        upper = lax.all_gather(lax.ppermute(turn(query_key_value_upper), axes, to_user), "dp", axis=1, tiled=True)
        upper = jnp.swapaxes(upper.reshape(3, SLABS, heads_own // SLABS, LANES), 0, 1)
        lower = lax.all_gather(query_key_value_lower, axes, axis=1, tiled=True)
        lower = jnp.moveaxis(lower.reshape(3, SLABS, 4, LANES // 4, LANES), (2, 1), (0, 1))
        lower = lower.reshape(4, SLABS, 3 * LANES // 4, LANES)
        at = lambda k: lax.dynamic_index_in_dim(lower, place ^ k, 0, keepdims=False)
        pack = jnp.concatenate(
            [v.reshape(SLABS, -1, LANES) for v in (halves, upper, at(0))], 1
        )
        slabs = [pack[k] for k in range(SLABS)]
        mates = [at(k) for k in (1, 2, 3)]

    cot_arrived = exchange_dp(
        after(cotangent, slabs[SLABS - 1]).reshape(groups, slot, width)
    ).reshape(quarter, width)
    wide = (turn(feedforward_matrix), down_matrix, output_matrix, swap(output_matrix, 2))
    fulls = (feedforward_adapter_lower, turn(output_adapter_upper), turn(down_adapter_upper))
    out_lower_used, *users = [
        lax.ppermute(v, axes, to_user)
        for v in (output_adapter_lower, turn(feedforward_adapter_upper), down_adapter_lower)
    ]
    out_used = (out_lower_used, swap(out_lower_used, 2))
    if groups == SLABS:
        pack = after(flat(*wide, *fulls, *out_used, *users), arrived)
        pack = lax.all_gather(pack, "dp", axis=0, tiled=False)

    gain_one = attention_gain.reshape(1, width)
    gain_two = feedforward_gain.reshape(1, width)
    normed, qkv, qkv_latent, qkv_w, qkv_a, qkv_b = project_qkv(
        meta, token_pieces, gain_one, slabs, mates, heads_own
    )
    attended, log_total = attend_forward(meta, qkv, spans)
    attended, cot_arrived = together(attended, cot_arrived)
    grad_mate, grad_far = swap(cot_arrived, 1), swap(cot_arrived, 2)
    heads_near, heads_sent, states = memory_forward(meta, fmeta, qkv, attended)
    heads_sent, grad_far = together(heads_sent, grad_far)
    heads_far = swap(heads_sent, 2)
    grad_pieces = [cot_arrived, grad_mate, grad_far, swap(grad_far, 1)]
    if groups == SLABS:
        pack = after(pack, heads_near)
        at = 3 * hidden + 2 * heads_own
        full_pieces = gather_tensor(pack[:, at : at + 4 * share])
        used = pack[:, at + 6 * share :].reshape(SLABS, 3, up_share, LANES)
        used = jnp.swapaxes(used, 0, 1).reshape(3, hidden, LANES)
        ffn_w, down_w, out_w, ffn_a, out_b, down_b, out_a = unpack(
            meta, pack, full_pieces, used, hidden, heads_own
        )
    else:
        gathered = [lax.all_gather(v, "dp", axis=v.ndim - 1, tiled=True) for v in wide]
        ffn_a, out_b, down_b = [
            lax.all_gather(v, axes, axis=v.ndim - 2, tiled=True) for v in fulls
        ]
        ffn_a = jnp.concatenate([ffn_a[0], ffn_a[1]], 1)
        ffn_b, down_a, *out_a = [
            lax.all_gather(v, "dp", axis=v.ndim - 2, tiled=True) for v in (*users, *out_used)
        ]
        out_a = jnp.concatenate(out_a, 0)
        ffn_w = jnp.concatenate([gathered[0], ffn_b], 2).reshape(2 * hidden, width + LANES)
        down_w = jnp.concatenate([gathered[1], down_a], 1)
        out_w = jnp.concatenate(gathered[2:], 0)
    branch_own, branch_mate, out_latent, heads = out_forward(
        meta, heads_near, heads_far, out_w, out_a, out_b
    )
    branch_got = swap(branch_mate, 1)
    hidden_one, normed_two = join_norm(arrived, branch_own, branch_got, gain_two)
    two = [normed_two, swap(normed_two, 1)]
    two_far = swap(normed_two, 2)

    near = ffn(meta, 0, two, grad_pieces[:2], ffn_w, down_w, ffn_a, down_b)
    two_far = after(two_far, near[0])
    two = two + [two_far, swap(two_far, 1)]
    far = ffn(meta, 2, two[2:], grad_pieces[2:], ffn_w, down_w, ffn_a, down_b)

    def first_step(far_mate, across):
        return (far_mate.astype(F32) + swap(across, 1).astype(F32)).astype(BF16)

    def second_step(own, mate, onward):
        return own.astype(F32) + swap(mate, 1).astype(F32) + swap(onward, 2).astype(F32)

    def scatter(own, mate, far_mate, across):
        return second_step(own, mate, first_step(far_mate, across))

    onward = first_step(far[0], far[1])
    onward, *far = together(onward, *far[2:])
    onward_far = swap(onward, 2)
    *branch, ffn_full, ffn_own = ffn_rest(meta, two, grad_pieces, near[2:], far, down_w, down_b)
    onward_far, *branch = together(onward_far, *branch)
    grad_one, grad_one_low = norm_gradient(
        cot_arrived, hidden_one, near[0], swap(near[1], 1), onward_far, gain_two, (F32, BF16)
    )

    grad_mate = swap(grad_one_low, 1)
    head_grads, head_grads_sent, out_latent_grad = out_backward(
        meta, grad_one_low, grad_mate, out_w, out_a, out_b
    )
    head_grads_far = swap(head_grads_sent, 2)
    out_own, out_full = out_pairs(
        meta, heads, after(out_latent_grad, head_grads_sent), out_latent, grad_one_low, grad_mate
    )
    def reduce_pack(full_terms, own_terms):
        parts = scatter(*[full_terms[k] for k in range(4)]).astype(BF16)
        parts = parts.reshape(groups, share, full_terms.shape[2])
        parts = [
            parts[:, :, i * LANES : (i + 1) * LANES]
            for i in range(full_terms.shape[2] // LANES)
        ]
        return jnp.concatenate(parts + own_terms, 1)

    def reduced(exchanged, parts):
        summed = sum(v.astype(F32) for v in exchanged)
        cut = share * parts
        own = lax.ppermute(summed[cut:], axes, to_owner)
        return summed[:cut].reshape(parts, share, LANES), own

    def by_owner(values):
        return values.reshape(groups, values.shape[0] // groups, LANES)

    def regroup(values):
        if groups == SLABS:
            return values
        rows = values.reshape(4, SLABS, LANES // 4, values.shape[2])
        ordered = tensor_order([rows[k] for k in range(4)], place)
        ordered = jnp.swapaxes(ordered, 0, 1).reshape(groups, tensors, share, values.shape[2])
        at = lambda k: lax.dynamic_index_in_dim(ordered, place ^ k, 1, keepdims=False)
        return jnp.stack([at(k).reshape(groups * share, values.shape[2]) for k in range(4)])

    ffn_pack = reduce_pack(regroup(ffn_full), [by_owner(ffn_own[n]) for n in range(3)])
    head_grads_far, ffn_pack, out_own, out_full, *branch = together(
        head_grads_far, ffn_pack, out_own, out_full, *branch
    )
    ffn_exchanged = exchange_dp(ffn_pack)
    branch_onward = first_step(branch[2], branch[3])
    branch_far = swap(branch_onward, 2)
    branch_near = branch[0].astype(F32) + swap(branch[1], 1).astype(F32)
    qkv_grads = mixer_backward(
        meta, fmeta, qkv, head_grads, head_grads_far, attended, log_total, states, spans
    )
    qkv_grads, branch_far, ffn_exchanged = together(qkv_grads, branch_far, ffn_exchanged)

    far_terms = qkv_backward(meta, 2, quarter, qkv_grads, qkv_w, qkv_a, qkv_b)
    onward = first_step(*far_terms)
    branch_far = after(branch_far, far_terms[0])
    mixed_rows = (hidden_one + (branch_near + branch_far.astype(F32))).astype(BF16)
    mixed = exchange_dp(mixed_rows.reshape(groups, slot, width)).reshape(quarter, width)
    qkv_grads = after(qkv_grads, onward)
    onward_far = swap(onward, 2)
    near_terms = qkv_backward(meta, 0, quarter, qkv_grads, qkv_w, qkv_a, qkv_b)
    near_got = swap(near_terms[1], 1)
    qkv_full, qkv_own = qkv_pairs(
        meta, normed, qkv_latent, after(qkv_grads, near_terms[0]), qkv_b
    )
    onward_far, mixed = together(onward_far, mixed)
    [grad_input] = norm_gradient(
        grad_one, arrived, near_terms[0], near_got, onward_far, gain_one, (BF16,)
    )
    token_grad = exchange_dp(grad_input.reshape(groups, slot, width)).reshape(quarter, width)
    qkv_full, qkv_own, out_own, out_full, _ = together(qkv_full, qkv_own, out_own, out_full, grad_input)
    out_mine, out_other = by_owner(out_own[:heads_own]), by_owner(out_own[heads_own:])
    out_mine = (out_mine.astype(F32) + swap(out_other, 2).astype(F32)).astype(BF16)
    qkv_pack = reduce_pack(
        regroup(jnp.concatenate([qkv_full, out_full], 2)),
        [by_owner(qkv_own[m]) for m in range(3)] + [out_mine],
    )
    qkv_full, qkv_own = reduced(pieces_dp(qkv_pack), 4)
    ffn_full, ffn_own = reduced([ffn_exchanged[k] for k in range(groups)], 3)
    ffn_own_parts = [ffn_own[i * up_share : (i + 1) * up_share] for i in range(3)]
    return (
        mixed,
        token_grad,
        qkv_full[:3],
        turn(qkv_own[: 3 * share].reshape(3, share, LANES)),
        qkv_own[3 * share :],
        qkv_full[3].T,
        ffn_full[:2],
        jnp.stack([ffn_own_parts[0].T, ffn_own_parts[1].T]),
        ffn_own_parts[2],
        ffn_full[2].T,
    )


def solution(mesh):
    both = ("dp", "tensor")
    rows = P(both, None)
    lower = P(None, both, None)
    upper = P(None, None, both)
    return jax.shard_map(
        per_device,
        mesh=mesh,
        in_specs=(
            rows,
            rows,
            P(),
            P(),
            P(None, "dp", "tensor"),
            P("tensor", "dp"),
            P(None, "dp", "tensor"),
            P("tensor", "dp"),
            P(),
            P(),
            P(),
            P(),
            P(),
            P(),
            lower,
            upper,
            rows,
            P(None, both),
            lower,
            upper,
            rows,
            P(None, both),
        ),
        out_specs=(
            rows,
            rows,
            lower,
            upper,
            rows,
            P(None, both),
            lower,
            upper,
            rows,
            P(None, both),
        ),
        check_vma=False,
    )
```

```python
import functools

import jax
import jax.numpy as jnp
from jax import lax
from jax.experimental import pallas as pl
from jax.experimental.pallas import tpu as pltpu
from jax.sharding import PartitionSpec as P

HEAD_DIM = 128
ADAPTER_RANK = 16
STRETCH = 64
SEQ_G = 3
LANES = 128
BLOCK = 256
MEMORY_GAIN = 32.0
EPSILON = 1e-06
LOG2E = 1.4426950408889634
BF16 = jnp.bfloat16
F32 = jnp.float32
SLABS = 8


def nn(left, right):
    return jnp.dot(left, right, preferred_element_type=F32)


def nt(left, right, precision=None):
    return lax.dot_general(
        left, right, (((1,), (1,)), ((), ())), precision=precision, preferred_element_type=F32
    )


def tn(left, right):
    return lax.dot_general(left, right, (((0,), (0,)), ((), ())), preferred_element_type=F32)


def params(mebibytes):
    return pltpu.CompilerParams(
        dimension_semantics=("arbitrary",), vmem_limit_bytes=mebibytes * 1024 * 1024
    )


def cost(flops, moved):
    return pl.CostEstimate(flops=int(flops), bytes_accessed=int(moved), transcendentals=0)


def in_hbm(values):
    return [pltpu.with_memory_space_constraint(v, pltpu.HBM) for v in values]


def whole(*shape):
    return pl.BlockSpec(shape, lambda *_: (0,) * len(shape), pipeline_mode=pl.Buffered(1))


def adapter_select(meta, first_row, rows, copies):
    row = first_row + lax.broadcasted_iota(jnp.int32, (rows, 1), 0)
    adapter = jnp.where(row >= meta[1], meta[4], jnp.where(row >= meta[0], meta[3], meta[2]))
    column = lax.broadcasted_iota(jnp.int32, (rows, copies * LANES), 1)
    return (column % LANES) // ADAPTER_RANK == adapter


def keep_low(select, values):
    return jnp.where(select, values, 0.0).astype(BF16)


def qkv_kernel(meta, *refs):
    pieces, slabs, mates = refs[:4], refs[4 : 4 + SLABS], refs[4 + SLABS : 8 + SLABS]
    gain, normed, qkv, latent, weight_out, lower_out, upper_out, *refs = refs[8 + SLABS :]
    x_all, slab_all, mate_all, x_sems, slab_sems, mate_sems = refs
    step = pl.program_id(0)
    rows = x_all.shape[1]
    kept = slab_all.shape[1]
    x_copies = [
        pltpu.make_async_copy(ref, x_all.at[k], x_sems.at[k]) for k, ref in enumerate(pieces)
    ]
    slab_copies = [
        pltpu.make_async_copy(ref.at[pl.ds(0, kept)], slab_all.at[k], slab_sems.at[k])
        for k, ref in enumerate(slabs)
    ]
    mate_copies = [
        pltpu.make_async_copy(ref, mate_all.at[k], mate_sems.at[k])
        for k, ref in enumerate(mates)
    ]
    slab, share = LANES, LANES // 4
    halves = weight_out.shape[2] // LANES
    upper_at = halves * 3 * slab

    @pl.when(step == 0)
    def _():
        for copy in slab_copies + mate_copies + x_copies:
            copy.start()
        for copy in mate_copies:
            copy.wait()
        for k in range(SLABS):
            slab_copies[k].wait()
            place = meta[8] ^ k
            wide = pl.ds(pl.multiple_of(place * slab, slab), slab)
            thin = pl.ds(pl.multiple_of(place * share, share), share)
            for m in range(3):
                for half in range(halves):
                    at = (half * 3 + m) * slab
                    weight_out[m, wide, half * LANES : (half + 1) * LANES] = slab_all[
                        k, at : at + slab, :
                    ]
                upper_out[m, thin, :] = slab_all[
                    k, upper_at + m * share : upper_at + (m + 1) * share, :
                ]
                lanes = slice(m * LANES, (m + 1) * LANES)
                for mate in range(4):
                    to = pl.multiple_of(place * slab + (meta[7] ^ mate) * share, share)
                    lower_out[pl.ds(to, share), lanes] = mate_all[
                        mate, k, m * share : (m + 1) * share, :
                    ]

    for k in range(4):

        @pl.when(step == k)
        def _(k=k):
            x_copies[k].wait()

    values = x_all[step].astype(F32)
    scale = lax.rsqrt(jnp.mean(values * values, -1, keepdims=True) + EPSILON)
    low = (values * scale * gain[...]).astype(BF16)
    normed[...] = low
    select = adapter_select(meta, (meta[7] ^ step) * rows, rows, 3)
    lat = keep_low(select, nn(low, lower_out[...]))
    latent[...] = lat
    for m in range(3):
        qkv[m] = (
            nn(low, weight_out[m]) + nt(lat[:, m * LANES : (m + 1) * LANES], upper_out[m])
        ).astype(BF16)


def project_qkv(meta, pieces, gain, slabs, mates, own):
    rows, width = pieces[0].shape
    total = rows * 4
    place = lambda step, meta: (meta[7] ^ step, 0)
    return pl.pallas_call(
        qkv_kernel,
        grid_spec=pltpu.PrefetchScalarGridSpec(
            num_scalar_prefetch=1,
            grid=(4,),
            in_specs=[pl.BlockSpec(memory_space=pltpu.HBM)] * len(pieces + slabs + mates)
            + [whole(1, width)],
            out_specs=[
                pl.BlockSpec((rows, width), place),
                pl.BlockSpec((3, rows, own), lambda step, meta: (0, meta[7] ^ step, 0)),
                pl.BlockSpec((rows, 3 * LANES), place),
                whole(3, width, own),
                whole(width, 3 * LANES),
                whole(3, own, LANES),
            ],
            scratch_shapes=[
                pltpu.VMEM((4, rows, width), BF16),
                pltpu.VMEM((SLABS, slabs[0].shape[0] - mates[0].shape[1], LANES), BF16),
                pltpu.VMEM((4,) + mates[0].shape, BF16),
                pltpu.SemaphoreType.DMA((4,)),
                pltpu.SemaphoreType.DMA((SLABS,)),
                pltpu.SemaphoreType.DMA((4,)),
            ],
        ),
        out_shape=[
            pltpu.HBM((total, width), BF16),
            pltpu.HBM((3, total, own), BF16),
            pltpu.HBM((total, 3 * LANES), BF16),
            pltpu.HBM((3, width, own), BF16),
            pltpu.HBM((width, 3 * LANES), BF16),
            pltpu.HBM((3, own, LANES), BF16),
        ],
        compiler_params=params(30),
        cost_estimate=cost(2 * total * width * (3 * own + 600), 4 * total * width),
        name="project_qkv",
    )(meta, *in_hbm(pieces + slabs + mates), gain)


def span_variants(count, spans, run):
    for n, blocks in enumerate(spans):
        if n == 0:
            condition = count <= blocks
        else:
            condition = count == blocks
        pl.when(condition)(functools.partial(run, blocks * BLOCK))


def stretch_columns(low, total_stretches):
    stretch = lax.broadcasted_iota(jnp.int32, low.shape, 0) // STRETCH
    zero = jnp.zeros_like(low)
    return jnp.concatenate(
        [jnp.where(stretch == n, low, zero) for n in range(total_stretches)], 1
    )


def unit_rows(values):
    inverse = lax.rsqrt(jnp.sum(values * values, -1, keepdims=True) + EPSILON)
    return values * inverse, inverse


def attend_forward_kernel(spans, meta, rows_in, attended, log_total, qkv, sems):
    block = pl.program_id(0)
    first_row = block * BLOCK

    def copy_of(b):
        rows = pl.ds(b * BLOCK, BLOCK)
        return pltpu.make_async_copy(rows_in.at[:, rows], qkv.at[:, rows], sems.at[b])

    @pl.when(block == 0)
    def _():
        for b in range(qkv.shape[1] // BLOCK):
            copy_of(b).start()

    for b in range(qkv.shape[1] // BLOCK):

        @pl.when(block == (0 if b == 1 else b))
        def _(b=b):
            copy_of(b).wait()

    start_two, start_three = meta[0], meta[1]
    row = first_row + lax.broadcasted_iota(jnp.int32, (BLOCK, 1), 0)
    begin = jnp.where(row >= start_three, start_three, jnp.where(row >= start_two, start_two, 0))
    first_begin = jnp.where(
        first_row >= start_three, start_three, jnp.where(first_row >= start_two, start_two, 0)
    )
    factor = HEAD_DIM ** (-0.5) * LOG2E
    here = pl.ds(pl.multiple_of(first_row, BLOCK), BLOCK)
    windows = meta[5], meta[6]
    low_keys = [jnp.maximum(row - window + 1, begin) for window in windows]
    first_key = jnp.maximum(first_row - jnp.maximum(*windows) + 1, first_begin)

    def attend(span):
        start = pl.multiple_of(jnp.maximum(first_row + BLOCK - span, 0), BLOCK)
        there = pl.ds(start, span)
        position = start + lax.broadcasted_iota(jnp.int32, (BLOCK, span), 1)
        heads = [slice(h * HEAD_DIM, (h + 1) * HEAD_DIM) for h in range(2)]
        scores = [nt(qkv[0, here, cols], qkv[1, there, cols]) for cols in heads]
        for h, cols in enumerate(heads):
            allowed = (position >= low_keys[h]) & (position <= row)
            score = jnp.where(allowed, scores[h], -1e30)
            top = jnp.max(score, -1, keepdims=True)
            weight = jnp.exp2((score - top) * factor).astype(BF16)
            value = qkv[2, there, cols]
            both = nn(weight, jnp.concatenate([value, jnp.ones_like(value)], 1))
            total = both[:, HEAD_DIM : HEAD_DIM + 1]
            attended[:, cols] = (both[:, :HEAD_DIM] / both[:, HEAD_DIM:]).astype(BF16)
            logs = jnp.broadcast_to(top * factor + jnp.log2(total), (BLOCK, LANES))
            pick = jnp.where(lax.broadcasted_iota(jnp.int32, (8, LANES), 1) == 0, 1.0, 0.0)
            log_total[0, h : h + 1, :] = nt(pick, logs, lax.Precision.HIGHEST)[0:1]

    span_variants(block - first_key // BLOCK + 1, spans, attend)


def attend_forward(meta, qkv, spans):
    total, own = qkv.shape[1:]
    blocks = total // BLOCK
    return pl.pallas_call(
        functools.partial(attend_forward_kernel, spans),
        grid_spec=pltpu.PrefetchScalarGridSpec(
            num_scalar_prefetch=1,
            grid=(blocks,),
            in_specs=[pl.BlockSpec(memory_space=pltpu.HBM)],
            out_specs=[
                pl.BlockSpec((BLOCK, own), lambda b, *_: (b, 0)),
                pl.BlockSpec((1, 8, BLOCK), lambda b, *_: (b, 0, 0)),
            ],
            scratch_shapes=[
                pltpu.VMEM(qkv.shape, BF16),
                pltpu.SemaphoreType.DMA((blocks,)),
            ],
        ),
        out_shape=[
            jax.ShapeDtypeStruct((total, own), BF16),
            jax.ShapeDtypeStruct((blocks, 8, BLOCK), F32),
        ],
        compiler_params=params(18),
        cost_estimate=cost(4e9, 12e6),
        name="attend_forward",
    )(meta, *in_hbm([qkv]))


def memory_forward_kernel(meta, fmeta, qkv, attended, near, far, states, heads, state_scr):
    block = pl.program_id(0)
    first_row = block * BLOCK
    start_two, start_three = meta[0], meta[1]
    stretches = BLOCK // STRETCH

    @pl.when(block == 0)
    def _():
        state_scr[...] = jnp.zeros_like(state_scr)

    columns = [slice(h * HEAD_DIM, (h + 1) * HEAD_DIM) for h in range(2)]
    queries, grams, writtens = [], [], []
    for h, cols in enumerate(columns):
        query_unit, _ = unit_rows(qkv[0, :, cols].astype(F32))
        key_unit, _ = unit_rows(qkv[1, :, cols].astype(F32))
        by_stretch = stretch_columns(key_unit.astype(BF16), stretches)
        step_size = fmeta[2 + h]
        queries.append(query_unit.astype(BF16))
        grams.append((nn(key_unit.T.astype(BF16), by_stretch) * step_size).astype(BF16))
        turned = qkv[2, :, cols].astype(F32).T.astype(BF16)
        writtens.append(nn(turned, by_stretch) * step_size)
    carried = [state_scr[h] for h in range(2)]
    for n in range(stretches):
        row_at = first_row + n * STRETCH
        keep = jnp.where((row_at == start_two) | (row_at == start_three), 0.0, 1.0)
        lanes = slice(n * HEAD_DIM, (n + 1) * HEAD_DIM)
        for h in range(2):
            state = carried[h] * keep
            low = state.astype(BF16)
            states[n, h] = low
            carried[h] = fmeta[h] * state - nn(low, grams[h][:, lanes]) + writtens[h][:, lanes]
    for h, cols in enumerate(columns):
        state_scr[h] = carried[h]
        for n in range(stretches):
            rows = slice(n * STRETCH, (n + 1) * STRETCH)
            read = nt(queries[h][rows], states[n, h])
            heads[rows, cols] = (attended[rows, cols].astype(F32) + MEMORY_GAIN * read).astype(BF16)

    half_blocks = near.shape[0] // BLOCK
    at = pl.ds(pl.multiple_of((block % half_blocks) * BLOCK, BLOCK), BLOCK)
    own_chip = block // half_blocks == meta[7] // 2

    @pl.when(own_chip)
    def _():
        near[at, :] = heads[...]

    @pl.when(jnp.logical_not(own_chip))
    def _():
        far[at, :] = heads[...]


def memory_forward(meta, fmeta, qkv, attended):
    total, own = qkv.shape[1:]
    blocks = total // BLOCK
    stretches = BLOCK // STRETCH
    return pl.pallas_call(
        memory_forward_kernel,
        grid_spec=pltpu.PrefetchScalarGridSpec(
            num_scalar_prefetch=2,
            grid=(blocks,),
            in_specs=[
                pl.BlockSpec((3, BLOCK, own), lambda b, *_: (0, b, 0)),
                pl.BlockSpec((BLOCK, own), lambda b, *_: (b, 0)),
            ],
            out_specs=[
                whole(total // 2, own),
                whole(total // 2, own),
                pl.BlockSpec(
                    (stretches, 2, HEAD_DIM, HEAD_DIM), lambda b, *_: (b, 0, 0, 0)
                ),
            ],
            scratch_shapes=[
                pltpu.VMEM((BLOCK, own), BF16),
                pltpu.VMEM((2, HEAD_DIM, HEAD_DIM), F32),
            ],
        ),
        out_shape=[
            jax.ShapeDtypeStruct((total // 2, own), BF16),
            jax.ShapeDtypeStruct((total // 2, own), BF16),
            pltpu.HBM((blocks * stretches, 2, HEAD_DIM, HEAD_DIM), BF16),
        ],
        compiler_params=params(10),
        cost_estimate=cost(1e5, 1e5),
        name="memory_forward",
    )(meta, fmeta, *in_hbm([qkv, attended]))


def mixer_backward_kernel(
    spans,
    blocks,
    meta,
    fmeta,
    qkv,
    grad_near,
    grad_far,
    attended,
    log_total,
    states,
    grads,
    grad_out,
    key_t,
    key_sum,
    value_sum,
    query_t,
    state_grad,
):
    block = blocks - 1 - pl.program_id(0)
    first_row = block * BLOCK
    start_two, start_three = meta[0], meta[1]
    row = first_row + lax.broadcasted_iota(jnp.int32, (1, BLOCK), 1)
    begin = jnp.where(row >= start_three, start_three, jnp.where(row >= start_two, start_two, 0))
    first_begin = jnp.where(
        first_row >= start_three, start_three, jnp.where(first_row >= start_two, start_two, 0)
    )
    scale = HEAD_DIM ** (-0.5)
    factor = scale * LOG2E
    stretches = BLOCK // STRETCH
    here = pl.ds(pl.multiple_of(first_row, BLOCK), BLOCK)
    per_piece = grad_near.shape[0] // 2 // BLOCK
    piece = (block // per_piece) ^ meta[7]
    at = pl.ds(
        pl.multiple_of(((piece % 2) * per_piece + block % per_piece) * BLOCK, BLOCK), BLOCK
    )

    @pl.when(piece < 2)
    def _():
        grad_out[...] = grad_near[at, :]

    @pl.when(piece >= 2)
    def _():
        grad_out[...] = grad_far[at, :]

    @pl.when(pl.program_id(0) == 0)
    def _():
        key_sum[...] = jnp.zeros_like(key_sum)
        value_sum[...] = jnp.zeros_like(value_sum)
        state_grad[...] = jnp.zeros_like(state_grad)
        for h in range(2):
            for b in range(blocks):
                rows = slice(b * BLOCK, (b + 1) * BLOCK)
                key = qkv[1, rows, h * HEAD_DIM : (h + 1) * HEAD_DIM]
                key_t[h, :, rows] = key.astype(F32).T.astype(BF16)

    windows = meta[5], meta[6]
    low_keys = [jnp.maximum(row - window + 1, begin) for window in windows]
    first_key = jnp.maximum(first_row - jnp.maximum(*windows) + 1, first_begin)
    heads = [slice(h * HEAD_DIM, (h + 1) * HEAD_DIM) for h in range(2)]
    ones = jnp.ones((8, HEAD_DIM), F32)
    inners = [
        nt(ones, grad_out[:, cols].astype(F32) * attended[:, cols].astype(F32), lax.Precision.HIGHEST)[0:1]
        for cols in heads
    ]

    def attend(span):
        start = pl.multiple_of(jnp.maximum(first_row + BLOCK - span, 0), BLOCK)
        there = pl.ds(start, span)
        position = start + lax.broadcasted_iota(jnp.int32, (span, BLOCK), 0)
        scores = [nt(qkv[1, there, cols], qkv[0, here, cols]) for cols in heads]
        grad_weights = [nt(qkv[2, there, cols], grad_out[:, cols]) for cols in heads]
        for h, cols in enumerate(heads):
            allowed = (position >= low_keys[h]) & (position <= row)
            weight = jnp.where(
                allowed, jnp.exp2(scores[h] * factor - log_total[0, h : h + 1, :]), 0.0
            )
            grad_score = (weight * (grad_weights[h] - inners[h])).astype(BF16)
            value_sum[h, there, :] += nn(weight.astype(BF16), grad_out[:, cols])
            key_sum[h, there, :] += nn(grad_score, qkv[0, here, cols])
            query_t[h] = nn(key_t[h, :, there], grad_score)

    def remember():
        for h in range(2):
            cols = slice(h * HEAD_DIM, (h + 1) * HEAD_DIM)
            query_unit, query_inverse = unit_rows(qkv[0, here, cols].astype(F32))
            key_unit, key_inverse = unit_rows(qkv[1, here, cols].astype(F32))
            value = qkv[2, here, cols].astype(F32)
            key_low = key_unit.astype(BF16)
            grad = grad_out[:, cols]
            retention, step_size = fmeta[h], fmeta[2 + h]
            gram = (
                nn(key_unit.T.astype(BF16), stretch_columns(key_low, stretches)) * step_size
            ).astype(BF16)
            read_grad = MEMORY_GAIN * nn(
                grad.astype(F32).T.astype(BF16),
                stretch_columns(query_unit.astype(BF16), stretches),
            )
            carried = state_grad[h]
            query_grads, key_grads, value_grads = [], [], []
            for n in reversed(range(stretches)):
                row_at = first_row + n * STRETCH
                keep = jnp.where((row_at == start_two) | (row_at == start_three), 0.0, 1.0)
                rows = slice(n * STRETCH, (n + 1) * STRETCH)
                lanes = slice(n * HEAD_DIM, (n + 1) * HEAD_DIM)
                carried_low = carried.astype(BF16)
                state = states[n, h]
                key_rows = key_low[rows]
                pulled = nt(key_rows, carried_low)
                error = nt(key_rows, state) - value[rows]
                value_grads.append(step_size * pulled)
                key_grads.append(
                    -step_size
                    * (nn(pulled.astype(BF16), state) + nn(error.astype(BF16), carried_low))
                )
                query_grads.append(MEMORY_GAIN * nn(grad[rows], state))
                carried = keep * (
                    read_grad[:, lanes] + retention * carried - nn(carried_low, gram[:, lanes])
                )
            state_grad[h] = carried
            query_unit_grad = jnp.concatenate(query_grads[::-1], 0)
            key_unit_grad = jnp.concatenate(key_grads[::-1], 0)
            value_grad = jnp.concatenate(value_grads[::-1], 0)
            query_memory = query_inverse * (
                query_unit_grad
                - query_unit * jnp.sum(query_unit * query_unit_grad, -1, keepdims=True)
            )
            key_memory = key_inverse * (
                key_unit_grad - key_unit * jnp.sum(key_unit * key_unit_grad, -1, keepdims=True)
            )
            grads[0, :, cols] = (scale * query_t[h].T + query_memory).astype(BF16)
            grads[1, :, cols] = (scale * key_sum[h, here, :] + key_memory).astype(BF16)
            grads[2, :, cols] = (value_sum[h, here, :] + value_grad).astype(BF16)

    def both(span):
        attend(span)
        remember()

    span_variants(block - first_key // BLOCK + 1, spans, both)


def mixer_backward(meta, fmeta, qkv, grad_near, grad_far, attended, log_total, states, spans):
    total, own = qkv.shape[1:]
    blocks = total // BLOCK
    stretches = BLOCK // STRETCH
    row_block = pl.BlockSpec((BLOCK, own), lambda s, *_: (blocks - 1 - s, 0))
    return pl.pallas_call(
        functools.partial(mixer_backward_kernel, spans, blocks),
        grid_spec=pltpu.PrefetchScalarGridSpec(
            num_scalar_prefetch=2,
            grid=(blocks,),
            in_specs=[
                whole(*qkv.shape),
                whole(*grad_near.shape),
                whole(*grad_far.shape),
                row_block,
                pl.BlockSpec((1, 8, BLOCK), lambda s, *_: (blocks - 1 - s, 0, 0)),
                pl.BlockSpec(
                    (stretches, 2, HEAD_DIM, HEAD_DIM), lambda s, *_: (blocks - 1 - s, 0, 0, 0)
                ),
            ],
            out_specs=pl.BlockSpec((3, BLOCK, own), lambda s, *_: (0, blocks - 1 - s, 0)),
            scratch_shapes=[
                pltpu.VMEM((BLOCK, own), BF16),
                pltpu.VMEM((2, HEAD_DIM, total), BF16),
                pltpu.VMEM((2, total, HEAD_DIM), F32),
                pltpu.VMEM((2, total, HEAD_DIM), F32),
                pltpu.VMEM((2, HEAD_DIM, BLOCK), F32),
                pltpu.VMEM((2, HEAD_DIM, HEAD_DIM), F32),
            ],
        ),
        out_shape=jax.ShapeDtypeStruct(qkv.shape, BF16),
        compiler_params=params(20),
        cost_estimate=cost(10e9, 16e6),
        name="mixer_backward",
    )(meta, fmeta, qkv, grad_near, grad_far, attended, log_total, states)


def unpack_kernel(meta, pack, f0, f1, f2, f3, used, wide, down, out, lower, out_upper, down_upper, out_lower):
    hidden = down.shape[0]
    width = out.shape[1]
    heads = out.shape[0] // 2
    share = LANES // 4
    first_out, first_lower = 3 * hidden, 3 * hidden + 2 * heads
    skip = f0.shape[1] - 4 * share
    for p in range(SLABS):
        lanes = slice(p * LANES, (p + 1) * LANES)
        wide[:, lanes] = pack[p, : 2 * hidden, :]
        down[:, lanes] = pack[p, 2 * hidden : 3 * hidden, :]
        out[:, lanes] = pack[p, first_out : first_out + 2 * heads, :]
        for n in range(2):
            at = first_lower + n * share
            to = n * heads + p * share
            out_lower[to : to + share, :] = pack[p, at : at + share, :]
        for k, ref in enumerate((f0, f1, f2, f3)):
            place = (meta[8] ^ p) * LANES + (meta[7] ^ k) * share
            to = pl.ds(pl.multiple_of(place, share), share)
            part = lambda n, ref=ref: ref[p, skip + n * share : skip + (n + 1) * share, :]
            lower[to, :LANES] = part(0)
            lower[to, LANES:] = part(1)
            out_upper[to, :] = part(2)
            down_upper[to, :] = part(3)
    wide[:hidden, width:] = used[0]
    wide[hidden:, width:] = used[1]
    down[:, width:] = used[2]


def unpack(meta, pack, fulls, used, hidden, heads):
    width = SLABS * LANES
    shapes = [
        (2 * hidden, width + LANES),
        (hidden, width + LANES),
        (2 * heads, width),
        (width, 2 * LANES),
        (width, LANES),
        (width, LANES),
        (2 * heads, LANES),
    ]
    return pl.pallas_call(
        unpack_kernel,
        grid_spec=pltpu.PrefetchScalarGridSpec(
            num_scalar_prefetch=1,
            grid=(1,),
            in_specs=[whole(*v.shape) for v in (pack, *fulls, used)],
            out_specs=[whole(*v) for v in shapes],
        ),
        out_shape=[jax.ShapeDtypeStruct(v, BF16) for v in shapes],
        compiler_params=params(20),
        cost_estimate=cost(1e5, 1e5),
        name="unpack",
    )(meta, pack, *fulls, used)


def out_forward_kernel(meta, near, far, weight, lower, upper_t, own, mate, latent, heads):
    rows, columns = own.shape[0], near.shape[1]
    for k, out in enumerate((own, mate)):
        at = pl.ds(pl.multiple_of(((meta[7] % 2) ^ k) * rows, rows), rows)
        both = jnp.concatenate([near[at, :], far[at, :]], 1)
        here = slice(k * rows, (k + 1) * rows)
        heads[here, :] = both
        select = adapter_select(meta, (meta[7] ^ k) * rows, rows, 1)
        lat = keep_low(select, nn(both, lower[...]))
        latent[here, :] = lat
        out[...] = (nn(both, weight[...]) + nt(lat, upper_t[...])).astype(BF16)


def out_forward(meta, near, far, weight, lower, upper_t):
    rows, columns = near.shape[0] // 2, near.shape[1]
    width = upper_t.shape[0]
    return pl.pallas_call(
        out_forward_kernel,
        grid_spec=pltpu.PrefetchScalarGridSpec(
            num_scalar_prefetch=1,
            grid=(1,),
            in_specs=[whole(*v.shape) for v in (near, far, weight, lower, upper_t)],
            out_specs=[
                whole(rows, width),
                whole(rows, width),
                whole(2 * rows, LANES),
                whole(2 * rows, 2 * columns),
            ],
        ),
        out_shape=[
            jax.ShapeDtypeStruct((rows, width), BF16),
            jax.ShapeDtypeStruct((rows, width), BF16),
            jax.ShapeDtypeStruct((2 * rows, LANES), BF16),
            jax.ShapeDtypeStruct((2 * rows, 2 * columns), BF16),
        ],
        compiler_params=params(14),
        cost_estimate=cost(1e5, 1e5),
        name="out_forward",
    )(meta, near, far, weight, lower, upper_t)


def out_backward_kernel(meta, grad_own, grad_mate, weight, lower, upper_t, mine, other, latent):
    rows, columns = grad_own.shape[0], mine.shape[1]
    for k, grad in enumerate((grad_own, grad_mate)):
        here = slice(k * rows, (k + 1) * rows)
        select = adapter_select(meta, (meta[7] ^ k) * rows, rows, 1)
        lat = keep_low(select, nn(grad[...], upper_t[...]))
        latent[here, :] = lat
        both = (nt(grad[...], weight[...]) + nt(lat, lower[...])).astype(BF16)
        mine[here, :] = both[:, :columns]
        other[here, :] = both[:, columns:]


def out_backward(meta, grad_own, grad_mate, weight, lower, upper_t):
    rows, width = grad_own.shape
    columns = lower.shape[0] // 2
    return pl.pallas_call(
        out_backward_kernel,
        grid_spec=pltpu.PrefetchScalarGridSpec(
            num_scalar_prefetch=1,
            grid=(1,),
            in_specs=[whole(*v.shape) for v in (grad_own, grad_mate, weight, lower, upper_t)],
            out_specs=[
                whole(2 * rows, columns),
                whole(2 * rows, columns),
                whole(2 * rows, LANES),
            ],
        ),
        out_shape=[
            jax.ShapeDtypeStruct((2 * rows, columns), BF16),
            jax.ShapeDtypeStruct((2 * rows, columns), BF16),
            jax.ShapeDtypeStruct((2 * rows, LANES), BF16),
        ],
        compiler_params=params(14),
        cost_estimate=cost(4 * rows * width * 640, 8e6),
        name="out_backward",
    )(meta, grad_own, grad_mate, weight, lower, upper_t)


def spread_shares(meta, turned, out, lanes):
    share = LANES // 4
    for mate in range(4):
        for p in range(SLABS):
            at = pl.multiple_of(p * LANES + (meta[7] ^ mate) * share, share)
            out[mate, p * share : (p + 1) * share, lanes] = turned[pl.ds(at, share), :]


def out_pairs_kernel(meta, heads, latent_grad, latent, grad_own, grad_mate, lower_out, upper_out, turned):
    rows = grad_own.shape[0]
    lower_out[...] = tn(latent_grad[...], heads[...]).T.astype(BF16)
    turned[...] = (
        (tn(latent[:rows], grad_own[...]) + tn(latent[rows:], grad_mate[...])).T
    ).astype(BF16)
    spread_shares(meta, turned, upper_out, slice(None))


def out_pairs(meta, heads, latent_grad, latent, grad_own, grad_mate):
    rows, width = grad_own.shape
    columns = heads.shape[1]
    return pl.pallas_call(
        out_pairs_kernel,
        grid_spec=pltpu.PrefetchScalarGridSpec(
            num_scalar_prefetch=1,
            grid=(1,),
            in_specs=[whole(*v.shape) for v in (heads, latent_grad, latent, grad_own, grad_mate)],
            out_specs=[whole(columns, LANES), whole(4, width // 4, LANES)],
            scratch_shapes=[pltpu.VMEM((width, LANES), BF16)],
        ),
        out_shape=[
            jax.ShapeDtypeStruct((columns, LANES), BF16),
            jax.ShapeDtypeStruct((4, width // 4, LANES), BF16),
        ],
        compiler_params=params(12),
        cost_estimate=cost(4 * rows * LANES * (columns + width), 5e6),
        name="out_pairs",
    )(meta, heads, latent_grad, latent, grad_own, grad_mate)


def ffn_kernel(
    first,
    meta,
    x0,
    x1,
    g0,
    g1,
    weight,
    down_weight,
    lower,
    down_upper_t,
    dx0,
    dx1,
    swiglu,
    pre_grads,
    latent,
    latent_grad,
    down_latent_grad,
):
    step = pl.program_id(0)
    rows = swiglu.shape[0]
    parts = x0.shape[0] // rows
    width, hidden = x0.shape[1], swiglu.shape[1]

    for k, (x_ref, g_ref, dx_ref) in enumerate(((x0, g0, dx0), (x1, g1, dx1))):

        @pl.when(step // parts == k)
        def _(k=k, x_ref=x_ref, g_ref=g_ref, dx_ref=dx_ref):
            part = step % parts
            at = pl.ds(pl.multiple_of(part * rows, rows), rows)
            first_row = (meta[7] ^ (first + k)) * (rows * parts) + part * rows
            select = adapter_select(meta, first_row, rows, 2)
            x = x_ref[at, :]
            grad = g_ref[at, :]
            lat = keep_low(select, nn(x, lower[...]))
            latent[...] = lat
            gate = nt(jnp.concatenate([x, lat[:, :LANES]], 1), weight[:hidden])
            up = nt(jnp.concatenate([x, lat[:, LANES:]], 1), weight[hidden:])
            down_lat = keep_low(select[:, :LANES], nn(grad, down_upper_t[...]))
            down_latent_grad[...] = down_lat
            wide_grad = nt(jnp.concatenate([grad, down_lat], 1), down_weight[...])
            sigmoid = 1.0 / (1.0 + jnp.exp(-gate))
            silu = gate * sigmoid
            swiglu[...] = (silu * up).astype(BF16)
            d_up = (wide_grad * silu).astype(BF16)
            d_gate = (wide_grad * up * (sigmoid * (1.0 + gate * (1.0 - sigmoid)))).astype(BF16)
            pre_grads[0] = d_gate
            pre_grads[1] = d_up
            lat_grad = keep_low(
                select,
                jnp.concatenate(
                    [nn(d_gate, weight[:hidden, width:]), nn(d_up, weight[hidden:, width:])], 1
                ),
            )
            latent_grad[...] = lat_grad
            dx_ref[at, :] = (
                nn(d_gate, weight[:hidden, :width])
                + nn(d_up, weight[hidden:, :width])
                + nt(lat_grad, lower[...])
            ).astype(BF16)


def ffn(meta, first, xs, grads, weight, down_weight, lower, down_upper_t):
    rows, width = xs[0].shape
    hidden = down_weight.shape[0]
    total = 2 * rows
    block = lambda columns: pl.BlockSpec((BLOCK, columns), lambda s, *_: (s, 0))
    return pl.pallas_call(
        functools.partial(ffn_kernel, first),
        grid_spec=pltpu.PrefetchScalarGridSpec(
            num_scalar_prefetch=1,
            grid=(total // BLOCK,),
            in_specs=[
                whole(*v.shape)
                for v in (*xs, *grads, weight, down_weight, lower, down_upper_t)
            ],
            out_specs=[whole(rows, width)] * 2
            + [
                block(hidden),
                pl.BlockSpec((2, BLOCK, hidden), lambda s, *_: (0, s, 0)),
                block(2 * LANES),
                block(2 * LANES),
                block(LANES),
            ],
        ),
        out_shape=[jax.ShapeDtypeStruct((rows, width), BF16)] * 2
        + [
            pltpu.HBM((total, hidden), BF16),
            pltpu.HBM((2, total, hidden), BF16),
            jax.ShapeDtypeStruct((total, 2 * LANES), BF16),
            jax.ShapeDtypeStruct((total, 2 * LANES), BF16),
            jax.ShapeDtypeStruct((total, LANES), BF16),
        ],
        compiler_params=params(28),
        cost_estimate=cost(2 * total * width * hidden * 6.0, 14e6),
        name="ffn",
    )(meta, *xs, *grads, weight, down_weight, lower, down_upper_t)


def ffn_rest_kernel(steps, meta, *refs):
    xs, grads, refs = refs[:4], refs[4:8], refs[8:]
    near, far, refs = refs[:5], refs[5:10], refs[10:]
    weight, upper_t = refs[:2]
    branches, refs = refs[2:6], refs[6:]
    sums_out, x_sum, gate_sum, up_sum, down_sum, branch_sum, turned = refs
    step = pl.program_id(0)
    hidden, rows = weight.shape[0], xs[0].shape[0]
    width = xs[0].shape[1]

    @pl.when(step == 0)
    def _():
        for total in (x_sum, gate_sum, up_sum, down_sum, branch_sum):
            total[...] = jnp.zeros_like(total)

    for k in range(4):

        @pl.when(step == k)
        def _(k=k):
            swiglu, pre_grads, latent, latent_grad, down_latent_grad = near if k < 2 else far
            wide = swiglu[...]
            select = adapter_select(meta, (meta[7] ^ k) * rows, rows, 1)
            lat = keep_low(select, nn(wide, weight[:, width:]))
            branches[k][...] = (nn(wide, weight[:, :width]) + nt(lat, upper_t[...])).astype(BF16)
            x_sum[...] += tn(latent_grad[...], xs[k][...])
            gate_sum[:, :hidden] += tn(latent[:, :LANES], pre_grads[0])
            up_sum[:, :hidden] += tn(latent[:, LANES:], pre_grads[1])
            down_sum[:, :hidden] += tn(down_latent_grad[...], wide)
            branch_sum[...] += tn(lat, grads[k][...])

    @pl.when(step == steps - 1)
    def _():
        turned[:, : 2 * LANES] = x_sum[...].T
        turned[:, 2 * LANES :] = branch_sum[...].T
        share, used = LANES // 4, hidden // SLABS
        for p in range(SLABS):
            for mate in range(4):
                at = pl.multiple_of(p * LANES + (meta[7] ^ mate) * share, share)
                for n in range(3):
                    to = (mate * 3 + n) * share
                    sums_out[p, to : to + share, :] = turned[
                        pl.ds(at, share), n * LANES : (n + 1) * LANES
                    ]
        for n, total in enumerate((gate_sum, up_sum, down_sum)):
            values = total[...].T
            for p in range(SLABS):
                to = 12 * share + n * used
                sums_out[p, to : to + used, :] = values[p * used : (p + 1) * used]


def ffn_rest(meta, xs, grads, near, far, weight, upper_t):
    rows, width = xs[0].shape
    hidden = weight.shape[0]
    padded = -(-hidden // LANES) * LANES
    operands = (*xs, *grads, *near, *far, weight, upper_t)

    def kept(values, first):
        step_of = lambda s: jnp.clip(s - first, 0, 1)
        if values.ndim == 3:
            return pl.BlockSpec((2, rows, hidden), lambda s, *_: (0, step_of(s), 0))
        return pl.BlockSpec((rows, values.shape[1]), lambda s, *_: (step_of(s), 0))

    return pl.pallas_call(
        functools.partial(ffn_rest_kernel, 4),
        grid_spec=pltpu.PrefetchScalarGridSpec(
            num_scalar_prefetch=1,
            grid=(4,),
            in_specs=[whole(*v.shape) for v in (*xs, *grads)]
            + [kept(v, 0) for v in near]
            + [kept(v, 2) for v in far]
            + [whole(*v.shape) for v in (weight, upper_t)],
            out_specs=[whole(rows, width)] * 4
            + [whole(SLABS, 3 * LANES + 3 * hidden // SLABS, LANES)],
            scratch_shapes=[
                pltpu.VMEM((2 * LANES, width), F32),
                pltpu.VMEM((LANES, padded), F32),
                pltpu.VMEM((LANES, padded), F32),
                pltpu.VMEM((LANES, padded), F32),
                pltpu.VMEM((LANES, width), F32),
                pltpu.VMEM((width, 3 * LANES), F32),
            ],
        ),
        out_shape=[jax.ShapeDtypeStruct((rows, width), BF16)] * 4
        + [jax.ShapeDtypeStruct((SLABS, 3 * LANES + 3 * hidden // SLABS, LANES), F32)],
        compiler_params=params(36),
        cost_estimate=cost(8 * rows * width * hidden * 2.3, 30e6),
        name="ffn_rest",
    )(meta, *operands)


def qkv_backward_kernel(first, meta, grads0, grads1, weight, lower, upper_t, dx0, dx1):
    rows = dx0.shape[0]
    for k, (grads, dx) in enumerate(((grads0, dx0), (grads1, dx1))):
        select = adapter_select(meta, (meta[7] ^ (first + k)) * rows, rows, 3)
        lat = keep_low(
            select, jnp.concatenate([nn(grads[m], upper_t[m]) for m in range(3)], 1)
        )
        total = nt(lat, lower[...])
        for m in range(3):
            total += nt(grads[m], weight[m])
        dx[...] = total.astype(BF16)


def qkv_backward(meta, first, rows, grads, weight, lower, upper_t):
    own = grads.shape[2]
    width = lower.shape[0]
    piece = lambda k: pl.BlockSpec((3, rows, own), lambda s, meta: (0, meta[7] ^ (first + k), 0))
    return pl.pallas_call(
        functools.partial(qkv_backward_kernel, first),
        grid_spec=pltpu.PrefetchScalarGridSpec(
            num_scalar_prefetch=1,
            grid=(1,),
            in_specs=[
                piece(0),
                piece(1),
                whole(*weight.shape),
                whole(*lower.shape),
                whole(*upper_t.shape),
            ],
            out_specs=[whole(rows, width)] * 2,
        ),
        out_shape=[jax.ShapeDtypeStruct((rows, width), BF16)] * 2,
        compiler_params=params(16),
        cost_estimate=cost(4 * rows * width * 50, 4e5),
        name="qkv_backward",
    )(meta, grads, grads, weight, lower, upper_t)


def qkv_pairs_kernel(steps, meta, normed, latent, grads, upper_t, lower_out, upper_out, low_sum, up_sum, turned):
    step = pl.program_id(0)
    rows = normed.shape[0]
    select = adapter_select(meta, step * rows, rows, 3)
    lat = keep_low(
        select, jnp.concatenate([nn(grads[m], upper_t[m]) for m in range(3)], 1)
    )

    @pl.when(step == 0)
    def _():
        low_sum[...] = jnp.zeros_like(low_sum)
        up_sum[...] = jnp.zeros_like(up_sum)

    low_sum[...] += tn(lat, normed[...])
    for m in range(3):
        up_sum[m] += tn(latent[:, m * LANES : (m + 1) * LANES], grads[m])

    @pl.when(step == steps - 1)
    def _():
        turned[...] = low_sum[...].T.astype(BF16)
        spread_shares(meta, turned, lower_out, slice(None))
        for m in range(3):
            upper_out[m] = up_sum[m].T.astype(BF16)


def qkv_pairs(meta, normed, latent, grads, upper_t):
    total, width = normed.shape
    own = grads.shape[2]
    rows = 1024
    steps = total // rows
    return pl.pallas_call(
        functools.partial(qkv_pairs_kernel, steps),
        grid_spec=pltpu.PrefetchScalarGridSpec(
            num_scalar_prefetch=1,
            grid=(steps,),
            in_specs=[
                pl.BlockSpec((rows, width), lambda s, *_: (s, 0)),
                pl.BlockSpec((rows, 3 * LANES), lambda s, *_: (s, 0)),
                pl.BlockSpec((3, rows, own), lambda s, *_: (0, s, 0)),
                whole(*upper_t.shape),
            ],
            out_specs=[whole(4, width // 4, 3 * LANES), whole(3, own, LANES)],
            scratch_shapes=[
                pltpu.VMEM((3 * LANES, width), F32),
                pltpu.VMEM((3, LANES, own), F32),
                pltpu.VMEM((width, 3 * LANES), BF16),
            ],
        ),
        out_shape=[
            jax.ShapeDtypeStruct((4, width // 4, 3 * LANES), BF16),
            jax.ShapeDtypeStruct((3, own, LANES), BF16),
        ],
        compiler_params=params(20),
        cost_estimate=cost(2 * total * width * 20, 4e5),
        name="qkv_pairs",
    )(meta, normed, latent, grads, upper_t)


def join_norm_kernel(stream, own, got, gain, hidden, normed):
    values = stream[...].astype(F32) + (own[...].astype(F32) + got[...].astype(F32))
    hidden[...] = values.astype(BF16)
    scale = lax.rsqrt(jnp.mean(values * values, -1, keepdims=True) + EPSILON)
    normed[...] = (values * scale * gain[...]).astype(BF16)


def join_norm(stream, own, got, gain):
    rows, width = stream.shape
    return pl.pallas_call(
        join_norm_kernel,
        grid=(1,),
        in_specs=[whole(*v.shape) for v in (stream, own, got, gain)],
        out_specs=[whole(rows, width)] * 2,
        out_shape=[
            jax.ShapeDtypeStruct((rows, width), BF16),
            jax.ShapeDtypeStruct((rows, width), BF16),
        ],
        compiler_params=params(12),
        cost_estimate=cost(1e5, 1e5),
        name="join_norm",
    )(stream, own, got, gain)


def norm_gradient_kernel(*refs):
    operands, (gain, out), (held, sems) = refs[:5], refs[5:7], refs[7:]
    copies = [
        pltpu.make_async_copy(ref, held.at[k], sems.at[k]) for k, ref in enumerate(operands)
    ]
    for copy in copies:
        copy.start()
    for copy in copies:
        copy.wait()
    straight, values, own, near, far = [held[k].astype(F32) for k in range(5)]
    grad = own + near + far
    inverse = lax.rsqrt(jnp.mean(values * values, -1, keepdims=True) + EPSILON)
    scaled = gain[...] * grad
    inner = jnp.mean(scaled * values, -1, keepdims=True)
    out[...] = (
        straight + (inverse * scaled - values * (inverse * inverse * inverse * inner))
    ).astype(BF16)


def norm_gradient(straight, values, own, near, far, gain, stay=False):
    rows, width = values.shape
    operands = [straight, values, own, near, far]
    operands = in_hbm(operands) if stay else operands
    place = pltpu.HBM if stay else pl.ANY
    return pl.pallas_call(
        norm_gradient_kernel,
        grid=(1,),
        in_specs=[pl.BlockSpec(memory_space=place)] * 5 + [whole(1, width)],
        out_specs=whole(rows, width),
        out_shape=jax.ShapeDtypeStruct((rows, width), BF16),
        scratch_shapes=[pltpu.VMEM((5, rows, width), BF16), pltpu.SemaphoreType.DMA((5,))],
        compiler_params=params(20),
        cost_estimate=cost(1e6, 9e6),
        name="norm_gradient",
    )(*operands, gain)


def swap(values, bit):
    size = lax.axis_size("tensor")
    return lax.ppermute(values, "tensor", [(i, i ^ bit) for i in range(size)])


def swap_dp(values, bits):
    size = lax.axis_size("dp")
    return lax.ppermute(values, "dp", [(i, i ^ bits) for i in range(size)])


def gather_tensor(values):
    far = swap(values, 2)
    return [values, swap(values, 1), far, swap(far, 1)]


def tensor_order(pieces, place):
    stacked = jnp.stack(pieces)
    for bit in (1, 2):
        moved = stacked.reshape((2, 2) + pieces[0].shape)[:, ::-1] if bit == 1 else (
            stacked.reshape((2, 2) + pieces[0].shape)[::-1]
        )
        stacked = jnp.where((place & bit) != 0, moved.reshape(stacked.shape), stacked)
    return stacked


def gather_slabs(values):
    near = [values] + [swap_dp(values, 2 * k) for k in (1, 2, 3)]
    result = []
    for piece in near:
        result += [piece, swap_dp(piece, 1)]
    return result


def pieces_dp(values):
    size = lax.axis_size("dp")
    if size != SLABS:
        exchanged = exchange_dp(values)
        return [exchanged[k] for k in range(size)]
    place = lax.axis_index("dp")
    sent = [lax.dynamic_index_in_dim(values, place ^ k, 0, keepdims=False) for k in range(size)]
    return sent[:1] + [swap_dp(sent[k], k) for k in range(1, size)]


def exchange_dp(values):
    return lax.all_to_all(values, "dp", split_axis=0, concat_axis=0, tiled=True)


def after(values, *earlier):
    return lax.optimization_barrier((values,) + earlier)[0]


def together(*values):
    return lax.optimization_barrier(values)


def per_device(
    tokens,
    cotangent,
    attention_gain,
    feedforward_gain,
    query_key_value_matrix,
    output_matrix,
    feedforward_matrix,
    down_matrix,
    memory_retention,
    memory_step_size,
    sequence_length,
    sequence_permutation,
    sequence_adapter,
    head_span_window,
    query_key_value_lower,
    query_key_value_upper,
    output_adapter_lower,
    output_adapter_upper,
    feedforward_adapter_lower,
    feedforward_adapter_upper,
    down_adapter_lower,
    down_adapter_upper,
):
    groups = lax.axis_size("dp")
    group = lax.axis_index("dp")
    place = lax.axis_index("tensor")
    quarter, width = tokens.shape
    slot = quarter // groups
    heads_own = query_key_value_matrix.shape[2]
    hidden = feedforward_matrix.shape[2]

    members = lax.dynamic_slice_in_dim(sequence_permutation, group * SEQ_G, SEQ_G)
    hits = members[:, None] == jnp.arange(sequence_length.shape[0], dtype=jnp.int32)[None, :]
    lengths = jnp.sum(jnp.where(hits, sequence_length[None, :], 0), 1)
    adapters = jnp.sum(jnp.where(hits, sequence_adapter[None, :], 0), 1)
    head_at = place * 2
    windows = lax.dynamic_slice_in_dim(head_span_window, head_at, 2)
    meta = jnp.concatenate(
        [
            jnp.stack([lengths[0], lengths[0] + lengths[1]]),
            adapters,
            windows,
            jnp.stack([place, group if groups == SLABS else jnp.zeros_like(group)]),
        ]
    ).astype(jnp.int32)
    fmeta = jnp.concatenate(
        [
            lax.dynamic_slice_in_dim(memory_retention, head_at, 2),
            lax.dynamic_slice_in_dim(memory_step_size, head_at, 2) / STRETCH,
        ]
    )
    spans = (2, 3, 4, 5)
    axes = ("dp", "tensor")
    tensors = lax.axis_size("tensor")
    to_user = [(j, (j % groups) * tensors + j // groups) for j in range(groups * tensors)]
    to_owner = [(b, a) for a, b in to_user]
    share = query_key_value_lower.shape[1]
    up_share = feedforward_adapter_upper.shape[2]
    turn = lambda values: jnp.swapaxes(values, -1, -2)

    def flat(*parts):
        return jnp.concatenate([v.reshape(-1, LANES) for v in parts], 0)

    fulls = (feedforward_adapter_lower, turn(output_adapter_upper), turn(down_adapter_upper))

    arrived = exchange_dp(tokens.reshape(groups, slot, width)).reshape(quarter, width)
    token_pieces = gather_tensor(arrived)
    if groups == SLABS:
        halves = jnp.moveaxis(
            query_key_value_matrix.reshape(3, width // groups, heads_own // LANES, LANES), 2, 0
        )
        pack = flat(
            halves,
            lax.ppermute(turn(query_key_value_upper), axes, to_user),
            query_key_value_lower,
            *fulls,
        )
        slabs = gather_slabs(after(pack, arrived))
        lower_rows = pack.shape[0] - 7 * share
        mates = gather_tensor(jnp.stack([v[lower_rows:] for v in slabs]))
    else:
        halves = lax.all_gather(query_key_value_matrix, "dp", axis=1, tiled=True)
        halves = jnp.moveaxis(halves.reshape(3, SLABS, LANES, heads_own // LANES, LANES), (1, 3), (0, 1))
        upper = lax.all_gather(lax.ppermute(turn(query_key_value_upper), axes, to_user), "dp", axis=1, tiled=True)
        upper = jnp.swapaxes(upper.reshape(3, SLABS, heads_own // SLABS, LANES), 0, 1)
        lower = lax.all_gather(query_key_value_lower, axes, axis=1, tiled=True)
        lower = jnp.moveaxis(lower.reshape(3, SLABS, 4, LANES // 4, LANES), (2, 1), (0, 1))
        lower = lower.reshape(4, SLABS, 3 * LANES // 4, LANES)
        at = lambda k: lax.dynamic_index_in_dim(lower, place ^ k, 0, keepdims=False)
        pack = jnp.concatenate(
            [v.reshape(SLABS, -1, LANES) for v in (halves, upper, at(0))], 1
        )
        slabs = [pack[k] for k in range(SLABS)]
        mates = [at(k) for k in range(4)]

    cot_arrived = exchange_dp(
        after(cotangent, mates[3]).reshape(groups, slot, width)
    ).reshape(quarter, width)
    wide = (turn(feedforward_matrix), down_matrix, output_matrix, swap(output_matrix, 2))
    out_lower_used, *users = [
        lax.ppermute(v, axes, to_user)
        for v in (output_adapter_lower, turn(feedforward_adapter_upper), down_adapter_lower)
    ]
    out_used = (out_lower_used, swap(out_lower_used, 2))
    if groups == SLABS:
        pack = after(flat(*wide, *out_used, *users), slabs[6])
        pack = lax.all_gather(pack, "dp", axis=0, tiled=False)

    gain_one = attention_gain.reshape(1, width)
    gain_two = feedforward_gain.reshape(1, width)
    normed, qkv, qkv_latent, qkv_w, qkv_a, qkv_b = project_qkv(
        meta, token_pieces, gain_one, slabs, mates, heads_own
    )
    attended, log_total = attend_forward(meta, qkv, spans)
    heads_near, heads_sent, states = memory_forward(meta, fmeta, qkv, attended)
    heads_far = swap(heads_sent, 2)
    cot_arrived = after(cot_arrived, heads_far)
    grad_mate, grad_far = swap(cot_arrived, 1), swap(cot_arrived, 2)
    grad_pieces = [cot_arrived, grad_mate, grad_far]
    if groups == SLABS:
        pack = after(pack, heads_near, cot_arrived)
        at = 3 * hidden + 2 * heads_own
        used = pack[:, at + 2 * share :].reshape(SLABS, 3, up_share, LANES)
        used = jnp.swapaxes(used, 0, 1).reshape(3, hidden, LANES)
        ffn_w, down_w, out_w, ffn_a, out_b, down_b, out_a = unpack(
            meta, pack, mates, used, hidden, heads_own
        )
    else:
        gathered = [lax.all_gather(v, "dp", axis=v.ndim - 1, tiled=True) for v in wide]
        ffn_a, out_b, down_b = [
            lax.all_gather(v, axes, axis=v.ndim - 2, tiled=True) for v in fulls
        ]
        ffn_a = jnp.concatenate([ffn_a[0], ffn_a[1]], 1)
        ffn_b, down_a, *out_a = [
            lax.all_gather(v, "dp", axis=v.ndim - 2, tiled=True) for v in (*users, *out_used)
        ]
        out_a = jnp.concatenate(out_a, 0)
        ffn_w = jnp.concatenate([gathered[0], ffn_b], 2).reshape(2 * hidden, width + LANES)
        down_w = jnp.concatenate([gathered[1], down_a], 1)
        out_w = jnp.concatenate(gathered[2:], 0)
    heads_far, grad_pieces[2] = together(heads_far, grad_pieces[2])
    branch_own, branch_mate, out_latent, heads = out_forward(
        meta, heads_near, heads_far, out_w, out_a, out_b
    )
    branch_got = swap(branch_mate, 1)
    hidden_one, normed_two = join_norm(arrived, branch_own, branch_got, gain_two)
    two = [normed_two, swap(normed_two, 1)]
    two_far = swap(normed_two, 2)

    two[0], grad_pieces[2] = together(two[0], grad_pieces[2])
    near = ffn(meta, 0, two, grad_pieces[:2], ffn_w, down_w, ffn_a, down_b)
    two_far = after(two_far, near[0])
    grad_pieces = grad_pieces + [swap(grad_pieces[2], 1)]
    two = two + [two_far, swap(two_far, 1)]
    far = ffn(meta, 2, two[2:], grad_pieces[2:], ffn_w, down_w, ffn_a, down_b)

    def first_step(far_mate, across):
        return (far_mate.astype(F32) + swap(across, 1).astype(F32)).astype(BF16)

    def second_step(own, mate, onward):
        return own.astype(F32) + swap(mate, 1).astype(F32) + swap(onward, 2).astype(F32)

    def scatter(own, mate, far_mate, across):
        return second_step(own, mate, first_step(far_mate, across))

    onward = first_step(far[0], far[1])
    onward, *far = together(onward, *far[2:])
    onward_far = swap(onward, 2)
    *branch, ffn_sums = ffn_rest(meta, two, grad_pieces, near[2:], far, down_w, down_b)
    onward_far, *branch = together(onward_far, *branch)
    grad_one = norm_gradient(
        cot_arrived, hidden_one, near[0], swap(near[1], 1), onward_far, gain_two
    )

    grad_mate = swap(grad_one, 1)
    head_grads, head_grads_sent, out_latent_grad = out_backward(
        meta, grad_one, grad_mate, out_w, out_a, out_b
    )
    head_grads_far = swap(head_grads_sent, 2)
    out_own, out_full = out_pairs(
        meta, heads, after(out_latent_grad, head_grads_sent), out_latent, grad_one, grad_mate
    )
    def reduce_pack(full_terms, own_terms):
        parts = scatter(*[full_terms[k] for k in range(4)]).astype(BF16)
        parts = parts.reshape(groups, share, full_terms.shape[2])
        parts = [
            parts[:, :, i * LANES : (i + 1) * LANES]
            for i in range(full_terms.shape[2] // LANES)
        ]
        return jnp.concatenate(parts + own_terms, 1)

    def reduced(exchanged, parts):
        summed = sum(v.astype(F32) for v in exchanged)
        cut = share * parts
        own = lax.ppermute(summed[cut:], axes, to_owner)
        return summed[:cut].reshape(parts, share, LANES), own

    def by_owner(values):
        return values.reshape(groups, values.shape[0] // groups, LANES)

    def regroup(values):
        if groups == SLABS:
            return values
        rows = values.reshape(4, SLABS, LANES // 4, values.shape[2])
        ordered = tensor_order([rows[k] for k in range(4)], place)
        ordered = jnp.swapaxes(ordered, 0, 1).reshape(groups, tensors, share, values.shape[2])
        at = lambda k: lax.dynamic_index_in_dim(ordered, place ^ k, 1, keepdims=False)
        return jnp.stack([at(k).reshape(groups * share, values.shape[2]) for k in range(4)])

    def by_dp(sums):
        if groups == SLABS:
            return sums
        parts = sums[:, : 3 * LANES].reshape(SLABS, 4, 3, LANES // 4, LANES)
        parts = tensor_order([parts[:, k] for k in range(4)], place)
        parts = jnp.moveaxis(parts, (1, 0, 3), (0, 1, 2)).reshape(groups, tensors, share, 3, LANES)
        at = lambda k: lax.dynamic_index_in_dim(parts, place ^ k, 1, keepdims=False)
        parts = [jnp.swapaxes(at(k), 1, 2).reshape(groups, -1, LANES) for k in range(4)]
        own = sums[:, 3 * LANES :].reshape(SLABS, 3, hidden // SLABS, LANES)
        own = jnp.swapaxes(own, 0, 1).reshape(3, groups, up_share, LANES)
        return jnp.concatenate(parts + [own[n] for n in range(3)], 1)

    ffn_sums = lax.psum_scatter(by_dp(ffn_sums), "dp", scatter_dimension=0, tiled=False)
    branch_onward = first_step(branch[2], branch[3])
    head_grads_far, branch_onward, out_own, out_full = together(
        head_grads_far, branch_onward, out_own, out_full
    )
    branch_far = swap(branch_onward, 2)
    branch_near = branch[0].astype(F32) + swap(branch[1], 1).astype(F32)
    qkv_grads = mixer_backward(
        meta, fmeta, qkv, head_grads, head_grads_far, attended, log_total, states, spans
    )
    qkv_grads, branch_far = together(qkv_grads, branch_far)

    far_terms = qkv_backward(meta, 2, quarter, qkv_grads, qkv_w, qkv_a, qkv_b)
    onward = first_step(*far_terms)
    branch_far = after(branch_far, far_terms[0])
    mixed_rows = (hidden_one.astype(F32) + (branch_near + branch_far.astype(F32))).astype(BF16)
    mixed_rows = after(mixed_rows, onward)
    mixed = exchange_dp(mixed_rows.reshape(groups, slot, width)).reshape(quarter, width)
    qkv_grads = after(qkv_grads, onward)
    onward_far = swap(onward, 2)
    near_terms = qkv_backward(meta, 0, quarter, qkv_grads, qkv_w, qkv_a, qkv_b)
    near_got = swap(near_terms[1], 1)
    qkv_full, qkv_own = qkv_pairs(
        meta, normed, qkv_latent, after(qkv_grads, near_terms[0]), qkv_b
    )
    onward_far, mixed = together(onward_far, mixed)
    grad_input = norm_gradient(
        grad_one, arrived, near_terms[0], near_got, onward_far, gain_one, True
    )
    token_grad = exchange_dp(grad_input.reshape(groups, slot, width)).reshape(quarter, width)
    qkv_full, qkv_own, out_own, out_full, _ = together(
        qkv_full, qkv_own, out_own, out_full, onward_far
    )
    out_mine, out_other = by_owner(out_own[:heads_own]), by_owner(out_own[heads_own:])
    out_mine = (out_mine.astype(F32) + swap(out_other, 2).astype(F32)).astype(BF16)
    qkv_pack = reduce_pack(
        regroup(jnp.concatenate([qkv_full, out_full], 2)),
        [by_owner(qkv_own[m]) for m in range(3)] + [out_mine],
    )
    qkv_full, qkv_own = reduced(pieces_dp(qkv_pack), 4)
    ffn_sums = after(ffn_sums, grad_input)
    ffn_parts = [ffn_sums[k * 3 * share : (k + 1) * 3 * share] for k in range(4)]
    ffn_onward = ffn_parts[2] + swap(ffn_parts[3], 1)
    ffn_full = ffn_parts[0] + swap(ffn_parts[1], 1) + swap(ffn_onward, 2)
    ffn_full = ffn_full.reshape(3, share, LANES)
    ffn_own = lax.ppermute(ffn_sums[12 * share :], axes, to_owner)
    ffn_own_parts = [ffn_own[i * up_share : (i + 1) * up_share] for i in range(3)]
    return (
        mixed,
        token_grad,
        qkv_full[:3],
        turn(qkv_own[: 3 * share].reshape(3, share, LANES)),
        qkv_own[3 * share :],
        qkv_full[3].T,
        ffn_full[:2],
        jnp.stack([ffn_own_parts[0].T, ffn_own_parts[1].T]),
        ffn_own_parts[2],
        ffn_full[2].T,
    )


def solution(mesh):
    both = ("dp", "tensor")
    rows = P(both, None)
    lower = P(None, both, None)
    upper = P(None, None, both)
    return jax.shard_map(
        per_device,
        mesh=mesh,
        in_specs=(
            rows,
            rows,
            P(),
            P(),
            P(None, "dp", "tensor"),
            P("tensor", "dp"),
            P(None, "dp", "tensor"),
            P("tensor", "dp"),
            P(),
            P(),
            P(),
            P(),
            P(),
            P(),
            lower,
            upper,
            rows,
            P(None, both),
            lower,
            upper,
            rows,
            P(None, both),
        ),
        out_specs=(
            rows,
            rows,
            lower,
            upper,
            rows,
            P(None, both),
            lower,
            upper,
            rows,
            P(None, both),
        ),
        check_vma=False,
    )
```

```python
import functools

import jax
import jax.numpy as jnp
from jax import lax
from jax.experimental import pallas as pl
from jax.experimental.pallas import tpu as pltpu
from jax.sharding import PartitionSpec as P

HEAD_DIM = 128
ADAPTER_RANK = 16
STRETCH = 64
SEQ_G = 3
LANES = 128
BLOCK = 256
MEMORY_GAIN = 32.0
EPSILON = 1e-06
LOG2E = 1.4426950408889634
BF16 = jnp.bfloat16
F32 = jnp.float32
SLABS = 8


def nn(left, right):
    return jnp.dot(left, right, preferred_element_type=F32)


def nt(left, right, precision=None):
    return lax.dot_general(
        left, right, (((1,), (1,)), ((), ())), precision=precision, preferred_element_type=F32
    )


def tn(left, right):
    return lax.dot_general(left, right, (((0,), (0,)), ((), ())), preferred_element_type=F32)


def params(mebibytes):
    return pltpu.CompilerParams(
        dimension_semantics=("arbitrary",), vmem_limit_bytes=mebibytes * 1024 * 1024
    )


def cost(flops, moved):
    return pl.CostEstimate(flops=int(flops), bytes_accessed=int(moved), transcendentals=0)


def in_hbm(values):
    return [pltpu.with_memory_space_constraint(v, pltpu.HBM) for v in values]


def whole(*shape):
    return pl.BlockSpec(shape, lambda *_: (0,) * len(shape), pipeline_mode=pl.Buffered(1))


def adapter_select(meta, first_row, rows, copies):
    row = first_row + lax.broadcasted_iota(jnp.int32, (rows, 1), 0)
    adapter = jnp.where(row >= meta[1], meta[4], jnp.where(row >= meta[0], meta[3], meta[2]))
    column = lax.broadcasted_iota(jnp.int32, (rows, copies * LANES), 1)
    return (column % LANES) // ADAPTER_RANK == adapter


def keep_low(select, values):
    return jnp.where(select, values, 0.0).astype(BF16)


def qkv_kernel(meta, *refs):
    pieces, slabs, mates = refs[:4], refs[4 : 4 + SLABS], refs[4 + SLABS : 8 + SLABS]
    gain, normed, qkv, latent, weight_out, lower_out, upper_out, *refs = refs[8 + SLABS :]
    x_all, slab_all, mate_all, x_sems, slab_sems, mate_sems = refs
    step = pl.program_id(0)
    rows = x_all.shape[1]
    kept = slab_all.shape[1]
    x_copies = [
        pltpu.make_async_copy(ref, x_all.at[k], x_sems.at[k]) for k, ref in enumerate(pieces)
    ]
    slab_copies = [
        pltpu.make_async_copy(ref.at[pl.ds(0, kept)], slab_all.at[k], slab_sems.at[k])
        for k, ref in enumerate(slabs)
    ]
    mate_copies = [
        pltpu.make_async_copy(ref, mate_all.at[k], mate_sems.at[k])
        for k, ref in enumerate(mates)
    ]
    slab, share = LANES, LANES // 4
    halves = weight_out.shape[2] // LANES
    upper_at = halves * 3 * slab

    @pl.when(step == 0)
    def _():
        for copy in slab_copies + mate_copies + x_copies:
            copy.start()
        for copy in mate_copies:
            copy.wait()
        for k in range(SLABS):
            slab_copies[k].wait()
            place = meta[8] ^ k
            wide = pl.ds(pl.multiple_of(place * slab, slab), slab)
            thin = pl.ds(pl.multiple_of(place * share, share), share)
            for m in range(3):
                for half in range(halves):
                    at = (half * 3 + m) * slab
                    weight_out[m, wide, half * LANES : (half + 1) * LANES] = slab_all[
                        k, at : at + slab, :
                    ]
                upper_out[m, thin, :] = slab_all[
                    k, upper_at + m * share : upper_at + (m + 1) * share, :
                ]
                lanes = slice(m * LANES, (m + 1) * LANES)
                for mate in range(4):
                    to = pl.multiple_of(place * slab + (meta[7] ^ mate) * share, share)
                    lower_out[pl.ds(to, share), lanes] = mate_all[
                        mate, k, m * share : (m + 1) * share, :
                    ]

    for k in range(4):

        @pl.when(step == k)
        def _(k=k):
            x_copies[k].wait()

    values = x_all[step].astype(F32)
    scale = lax.rsqrt(jnp.mean(values * values, -1, keepdims=True) + EPSILON)
    low = (values * scale * gain[...]).astype(BF16)
    normed[...] = low
    select = adapter_select(meta, (meta[7] ^ step) * rows, rows, 3)
    lat = keep_low(select, nn(low, lower_out[...]))
    latent[...] = lat
    for m in range(3):
        qkv[m] = (
            nn(low, weight_out[m]) + nt(lat[:, m * LANES : (m + 1) * LANES], upper_out[m])
        ).astype(BF16)


def project_qkv(meta, pieces, gain, slabs, mates, own):
    rows, width = pieces[0].shape
    total = rows * 4
    place = lambda step, meta: (meta[7] ^ step, 0)
    return pl.pallas_call(
        qkv_kernel,
        grid_spec=pltpu.PrefetchScalarGridSpec(
            num_scalar_prefetch=1,
            grid=(4,),
            in_specs=[pl.BlockSpec(memory_space=pltpu.HBM)] * len(pieces + slabs + mates)
            + [whole(1, width)],
            out_specs=[
                pl.BlockSpec((rows, width), place),
                pl.BlockSpec((3, rows, own), lambda step, meta: (0, meta[7] ^ step, 0)),
                pl.BlockSpec((rows, 3 * LANES), place),
                whole(3, width, own),
                whole(width, 3 * LANES),
                whole(3, own, LANES),
            ],
            scratch_shapes=[
                pltpu.VMEM((4, rows, width), BF16),
                pltpu.VMEM((SLABS, slabs[0].shape[0] - mates[0].shape[1], LANES), BF16),
                pltpu.VMEM((4,) + mates[0].shape, BF16),
                pltpu.SemaphoreType.DMA((4,)),
                pltpu.SemaphoreType.DMA((SLABS,)),
                pltpu.SemaphoreType.DMA((4,)),
            ],
        ),
        out_shape=[
            pltpu.HBM((total, width), BF16),
            pltpu.HBM((3, total, own), BF16),
            pltpu.HBM((total, 3 * LANES), BF16),
            pltpu.HBM((3, width, own), BF16),
            pltpu.HBM((width, 3 * LANES), BF16),
            pltpu.HBM((3, own, LANES), BF16),
        ],
        compiler_params=params(30),
        cost_estimate=cost(2 * total * width * (3 * own + 600), 4 * total * width),
        name="project_qkv",
    )(meta, *in_hbm(pieces + slabs + mates), gain)


def span_variants(count, spans, run):
    for n, blocks in enumerate(spans):
        if n == 0:
            condition = count <= blocks
        else:
            condition = count == blocks
        pl.when(condition)(functools.partial(run, blocks * BLOCK))


def stretch_columns(low, total_stretches):
    stretch = lax.broadcasted_iota(jnp.int32, low.shape, 0) // STRETCH
    zero = jnp.zeros_like(low)
    return jnp.concatenate(
        [jnp.where(stretch == n, low, zero) for n in range(total_stretches)], 1
    )


def unit_rows(values):
    inverse = lax.rsqrt(jnp.sum(values * values, -1, keepdims=True) + EPSILON)
    return values * inverse, inverse


def attend_forward_kernel(spans, meta, rows_in, attended, log_total, qkv, sems):
    block = pl.program_id(0)
    first_row = block * BLOCK

    def copy_of(b):
        rows = pl.ds(b * BLOCK, BLOCK)
        return pltpu.make_async_copy(rows_in.at[:, rows], qkv.at[:, rows], sems.at[b])

    @pl.when(block == 0)
    def _():
        for b in range(qkv.shape[1] // BLOCK):
            copy_of(b).start()

    for b in range(qkv.shape[1] // BLOCK):

        @pl.when(block == (0 if b == 1 else b))
        def _(b=b):
            copy_of(b).wait()

    start_two, start_three = meta[0], meta[1]
    row = first_row + lax.broadcasted_iota(jnp.int32, (BLOCK, 1), 0)
    begin = jnp.where(row >= start_three, start_three, jnp.where(row >= start_two, start_two, 0))
    first_begin = jnp.where(
        first_row >= start_three, start_three, jnp.where(first_row >= start_two, start_two, 0)
    )
    factor = HEAD_DIM ** (-0.5) * LOG2E
    here = pl.ds(pl.multiple_of(first_row, BLOCK), BLOCK)
    windows = meta[5], meta[6]
    low_keys = [jnp.maximum(row - window + 1, begin) for window in windows]
    first_key = jnp.maximum(first_row - jnp.maximum(*windows) + 1, first_begin)

    def attend(span):
        start = pl.multiple_of(jnp.maximum(first_row + BLOCK - span, 0), BLOCK)
        there = pl.ds(start, span)
        position = start + lax.broadcasted_iota(jnp.int32, (BLOCK, span), 1)
        heads = [slice(h * HEAD_DIM, (h + 1) * HEAD_DIM) for h in range(2)]
        scores = [nt(qkv[0, here, cols], qkv[1, there, cols]) for cols in heads]
        for h, cols in enumerate(heads):
            allowed = (position >= low_keys[h]) & (position <= row)
            score = jnp.where(allowed, scores[h], -1e30)
            top = jnp.max(score, -1, keepdims=True)
            weight = jnp.exp2((score - top) * factor).astype(BF16)
            value = qkv[2, there, cols]
            both = nn(weight, jnp.concatenate([value, jnp.ones_like(value)], 1))
            total = both[:, HEAD_DIM : HEAD_DIM + 1]
            attended[:, cols] = (both[:, :HEAD_DIM] / both[:, HEAD_DIM:]).astype(BF16)
            logs = jnp.broadcast_to(top * factor + jnp.log2(total), (BLOCK, LANES))
            pick = jnp.where(lax.broadcasted_iota(jnp.int32, (8, LANES), 1) == 0, 1.0, 0.0)
            log_total[0, h : h + 1, :] = nt(pick, logs, lax.Precision.HIGHEST)[0:1]

    span_variants(block - first_key // BLOCK + 1, spans, attend)


def attend_forward(meta, qkv, spans):
    total, own = qkv.shape[1:]
    blocks = total // BLOCK
    return pl.pallas_call(
        functools.partial(attend_forward_kernel, spans),
        grid_spec=pltpu.PrefetchScalarGridSpec(
            num_scalar_prefetch=1,
            grid=(blocks,),
            in_specs=[pl.BlockSpec(memory_space=pltpu.HBM)],
            out_specs=[
                pl.BlockSpec((BLOCK, own), lambda b, *_: (b, 0)),
                pl.BlockSpec((1, 8, BLOCK), lambda b, *_: (b, 0, 0)),
            ],
            scratch_shapes=[
                pltpu.VMEM(qkv.shape, BF16),
                pltpu.SemaphoreType.DMA((blocks,)),
            ],
        ),
        out_shape=[
            jax.ShapeDtypeStruct((total, own), BF16),
            jax.ShapeDtypeStruct((blocks, 8, BLOCK), F32),
        ],
        compiler_params=params(18),
        cost_estimate=cost(4e9, 12e6),
        name="attend_forward",
    )(meta, *in_hbm([qkv]))


def memory_forward_kernel(meta, fmeta, qkv, attended, near, far, states, heads, state_scr):
    block = pl.program_id(0)
    first_row = block * BLOCK
    start_two, start_three = meta[0], meta[1]
    stretches = BLOCK // STRETCH

    @pl.when(block == 0)
    def _():
        state_scr[...] = jnp.zeros_like(state_scr)

    columns = [slice(h * HEAD_DIM, (h + 1) * HEAD_DIM) for h in range(2)]
    queries, grams, writtens = [], [], []
    for h, cols in enumerate(columns):
        query_unit, _ = unit_rows(qkv[0, :, cols].astype(F32))
        key_unit, _ = unit_rows(qkv[1, :, cols].astype(F32))
        by_stretch = stretch_columns(key_unit.astype(BF16), stretches)
        step_size = fmeta[2 + h]
        queries.append(query_unit.astype(BF16))
        grams.append((nn(key_unit.T.astype(BF16), by_stretch) * step_size).astype(BF16))
        turned = qkv[2, :, cols].astype(F32).T.astype(BF16)
        writtens.append(nn(turned, by_stretch) * step_size)
    carried = [state_scr[h] for h in range(2)]
    for n in range(stretches):
        row_at = first_row + n * STRETCH
        keep = jnp.where((row_at == start_two) | (row_at == start_three), 0.0, 1.0)
        lanes = slice(n * HEAD_DIM, (n + 1) * HEAD_DIM)
        for h in range(2):
            state = carried[h] * keep
            low = state.astype(BF16)
            states[n, h] = low
            carried[h] = fmeta[h] * state - nn(low, grams[h][:, lanes]) + writtens[h][:, lanes]
    for h, cols in enumerate(columns):
        state_scr[h] = carried[h]
        for n in range(stretches):
            rows = slice(n * STRETCH, (n + 1) * STRETCH)
            read = nt(queries[h][rows], states[n, h])
            heads[rows, cols] = (attended[rows, cols].astype(F32) + MEMORY_GAIN * read).astype(BF16)

    half_blocks = near.shape[0] // BLOCK
    at = pl.ds(pl.multiple_of((block % half_blocks) * BLOCK, BLOCK), BLOCK)
    own_chip = block // half_blocks == meta[7] // 2

    @pl.when(own_chip)
    def _():
        near[at, :] = heads[...]

    @pl.when(jnp.logical_not(own_chip))
    def _():
        far[at, :] = heads[...]


def memory_forward(meta, fmeta, qkv, attended):
    total, own = qkv.shape[1:]
    blocks = total // BLOCK
    stretches = BLOCK // STRETCH
    return pl.pallas_call(
        memory_forward_kernel,
        grid_spec=pltpu.PrefetchScalarGridSpec(
            num_scalar_prefetch=2,
            grid=(blocks,),
            in_specs=[
                pl.BlockSpec((3, BLOCK, own), lambda b, *_: (0, b, 0)),
                pl.BlockSpec((BLOCK, own), lambda b, *_: (b, 0)),
            ],
            out_specs=[
                whole(total // 2, own),
                whole(total // 2, own),
                pl.BlockSpec(
                    (stretches, 2, HEAD_DIM, HEAD_DIM), lambda b, *_: (b, 0, 0, 0)
                ),
            ],
            scratch_shapes=[
                pltpu.VMEM((BLOCK, own), BF16),
                pltpu.VMEM((2, HEAD_DIM, HEAD_DIM), F32),
            ],
        ),
        out_shape=[
            jax.ShapeDtypeStruct((total // 2, own), BF16),
            jax.ShapeDtypeStruct((total // 2, own), BF16),
            pltpu.HBM((blocks * stretches, 2, HEAD_DIM, HEAD_DIM), BF16),
        ],
        compiler_params=params(10),
        cost_estimate=cost(1e5, 1e5),
        name="memory_forward",
    )(meta, fmeta, *in_hbm([qkv, attended]))


def mixer_backward_kernel(
    spans,
    blocks,
    meta,
    fmeta,
    qkv,
    grad_near,
    grad_far,
    attended,
    log_total,
    states,
    grads,
    grad_out,
    key_t,
    key_sum,
    value_sum,
    query_t,
    state_grad,
):
    block = blocks - 1 - pl.program_id(0)
    first_row = block * BLOCK
    start_two, start_three = meta[0], meta[1]
    row = first_row + lax.broadcasted_iota(jnp.int32, (1, BLOCK), 1)
    begin = jnp.where(row >= start_three, start_three, jnp.where(row >= start_two, start_two, 0))
    first_begin = jnp.where(
        first_row >= start_three, start_three, jnp.where(first_row >= start_two, start_two, 0)
    )
    scale = HEAD_DIM ** (-0.5)
    factor = scale * LOG2E
    stretches = BLOCK // STRETCH
    here = pl.ds(pl.multiple_of(first_row, BLOCK), BLOCK)
    per_piece = grad_near.shape[0] // 2 // BLOCK
    piece = (block // per_piece) ^ meta[7]
    at = pl.ds(
        pl.multiple_of(((piece % 2) * per_piece + block % per_piece) * BLOCK, BLOCK), BLOCK
    )

    @pl.when(piece < 2)
    def _():
        grad_out[...] = grad_near[at, :]

    @pl.when(piece >= 2)
    def _():
        grad_out[...] = grad_far[at, :]

    @pl.when(pl.program_id(0) == 0)
    def _():
        key_sum[...] = jnp.zeros_like(key_sum)
        value_sum[...] = jnp.zeros_like(value_sum)
        state_grad[...] = jnp.zeros_like(state_grad)
        for h in range(2):
            for b in range(blocks):
                rows = slice(b * BLOCK, (b + 1) * BLOCK)
                key = qkv[1, rows, h * HEAD_DIM : (h + 1) * HEAD_DIM]
                key_t[h, :, rows] = key.astype(F32).T.astype(BF16)

    windows = meta[5], meta[6]
    low_keys = [jnp.maximum(row - window + 1, begin) for window in windows]
    first_key = jnp.maximum(first_row - jnp.maximum(*windows) + 1, first_begin)
    heads = [slice(h * HEAD_DIM, (h + 1) * HEAD_DIM) for h in range(2)]
    ones = jnp.ones((8, HEAD_DIM), F32)
    inners = [
        nt(ones, grad_out[:, cols].astype(F32) * attended[:, cols].astype(F32), lax.Precision.HIGHEST)[0:1]
        for cols in heads
    ]

    def attend(span):
        start = pl.multiple_of(jnp.maximum(first_row + BLOCK - span, 0), BLOCK)
        there = pl.ds(start, span)
        position = start + lax.broadcasted_iota(jnp.int32, (span, BLOCK), 0)
        scores = [nt(qkv[1, there, cols], qkv[0, here, cols]) for cols in heads]
        grad_weights = [nt(qkv[2, there, cols], grad_out[:, cols]) for cols in heads]
        for h, cols in enumerate(heads):
            allowed = (position >= low_keys[h]) & (position <= row)
            weight = jnp.where(
                allowed, jnp.exp2(scores[h] * factor - log_total[0, h : h + 1, :]), 0.0
            )
            grad_score = (weight * (grad_weights[h] - inners[h])).astype(BF16)
            value_sum[h, there, :] += nn(weight.astype(BF16), grad_out[:, cols])
            key_sum[h, there, :] += nn(grad_score, qkv[0, here, cols])
            query_t[h] = nn(key_t[h, :, there], grad_score)

    def remember():
        for h in range(2):
            cols = slice(h * HEAD_DIM, (h + 1) * HEAD_DIM)
            query_unit, query_inverse = unit_rows(qkv[0, here, cols].astype(F32))
            key_unit, key_inverse = unit_rows(qkv[1, here, cols].astype(F32))
            value = qkv[2, here, cols].astype(F32)
            key_low = key_unit.astype(BF16)
            grad = grad_out[:, cols]
            retention, step_size = fmeta[h], fmeta[2 + h]
            gram = (
                nn(key_unit.T.astype(BF16), stretch_columns(key_low, stretches)) * step_size
            ).astype(BF16)
            read_grad = MEMORY_GAIN * nn(
                grad.astype(F32).T.astype(BF16),
                stretch_columns(query_unit.astype(BF16), stretches),
            )
            carried = state_grad[h]
            query_grads, key_grads, value_grads = [], [], []
            for n in reversed(range(stretches)):
                row_at = first_row + n * STRETCH
                keep = jnp.where((row_at == start_two) | (row_at == start_three), 0.0, 1.0)
                rows = slice(n * STRETCH, (n + 1) * STRETCH)
                lanes = slice(n * HEAD_DIM, (n + 1) * HEAD_DIM)
                carried_low = carried.astype(BF16)
                state = states[n, h]
                key_rows = key_low[rows]
                pulled = nt(key_rows, carried_low)
                error = nt(key_rows, state) - value[rows]
                value_grads.append(step_size * pulled)
                key_grads.append(
                    -step_size
                    * (nn(pulled.astype(BF16), state) + nn(error.astype(BF16), carried_low))
                )
                query_grads.append(MEMORY_GAIN * nn(grad[rows], state))
                carried = keep * (
                    read_grad[:, lanes] + retention * carried - nn(carried_low, gram[:, lanes])
                )
            state_grad[h] = carried
            query_unit_grad = jnp.concatenate(query_grads[::-1], 0)
            key_unit_grad = jnp.concatenate(key_grads[::-1], 0)
            value_grad = jnp.concatenate(value_grads[::-1], 0)
            query_memory = query_inverse * (
                query_unit_grad
                - query_unit * jnp.sum(query_unit * query_unit_grad, -1, keepdims=True)
            )
            key_memory = key_inverse * (
                key_unit_grad - key_unit * jnp.sum(key_unit * key_unit_grad, -1, keepdims=True)
            )
            grads[0, :, cols] = (scale * query_t[h].T + query_memory).astype(BF16)
            grads[1, :, cols] = (scale * key_sum[h, here, :] + key_memory).astype(BF16)
            grads[2, :, cols] = (value_sum[h, here, :] + value_grad).astype(BF16)

    def both(span):
        attend(span)
        remember()

    span_variants(block - first_key // BLOCK + 1, spans, both)


def mixer_backward(meta, fmeta, qkv, grad_near, grad_far, attended, log_total, states, spans):
    total, own = qkv.shape[1:]
    blocks = total // BLOCK
    stretches = BLOCK // STRETCH
    row_block = pl.BlockSpec((BLOCK, own), lambda s, *_: (blocks - 1 - s, 0))
    return pl.pallas_call(
        functools.partial(mixer_backward_kernel, spans, blocks),
        grid_spec=pltpu.PrefetchScalarGridSpec(
            num_scalar_prefetch=2,
            grid=(blocks,),
            in_specs=[
                whole(*qkv.shape),
                whole(*grad_near.shape),
                whole(*grad_far.shape),
                row_block,
                pl.BlockSpec((1, 8, BLOCK), lambda s, *_: (blocks - 1 - s, 0, 0)),
                pl.BlockSpec(
                    (stretches, 2, HEAD_DIM, HEAD_DIM), lambda s, *_: (blocks - 1 - s, 0, 0, 0)
                ),
            ],
            out_specs=pl.BlockSpec((3, BLOCK, own), lambda s, *_: (0, blocks - 1 - s, 0)),
            scratch_shapes=[
                pltpu.VMEM((BLOCK, own), BF16),
                pltpu.VMEM((2, HEAD_DIM, total), BF16),
                pltpu.VMEM((2, total, HEAD_DIM), F32),
                pltpu.VMEM((2, total, HEAD_DIM), F32),
                pltpu.VMEM((2, HEAD_DIM, BLOCK), F32),
                pltpu.VMEM((2, HEAD_DIM, HEAD_DIM), F32),
            ],
        ),
        out_shape=jax.ShapeDtypeStruct(qkv.shape, BF16),
        compiler_params=params(20),
        cost_estimate=cost(10e9, 16e6),
        name="mixer_backward",
    )(meta, fmeta, qkv, grad_near, grad_far, attended, log_total, states)


def unpack_kernel(meta, pack, f0, f1, f2, f3, used, wide, down, out, lower, out_upper, down_upper, out_lower):
    hidden = down.shape[0]
    width = out.shape[1]
    heads = out.shape[0] // 2
    share = LANES // 4
    first_out, first_lower = 3 * hidden, 3 * hidden + 2 * heads
    skip = f0.shape[1] - 4 * share
    for p in range(SLABS):
        lanes = slice(p * LANES, (p + 1) * LANES)
        wide[:, lanes] = pack[p, : 2 * hidden, :]
        down[:, lanes] = pack[p, 2 * hidden : 3 * hidden, :]
        out[:, lanes] = pack[p, first_out : first_out + 2 * heads, :]
        for n in range(2):
            at = first_lower + n * share
            to = n * heads + p * share
            out_lower[to : to + share, :] = pack[p, at : at + share, :]
        for k, ref in enumerate((f0, f1, f2, f3)):
            place = (meta[8] ^ p) * LANES + (meta[7] ^ k) * share
            to = pl.ds(pl.multiple_of(place, share), share)
            part = lambda n, ref=ref: ref[p, skip + n * share : skip + (n + 1) * share, :]
            lower[to, :LANES] = part(0)
            lower[to, LANES:] = part(1)
            out_upper[to, :] = part(2)
            down_upper[to, :] = part(3)
    wide[:hidden, width:] = used[0]
    wide[hidden:, width:] = used[1]
    down[:, width:] = used[2]


def unpack(meta, pack, fulls, used, hidden, heads):
    width = SLABS * LANES
    shapes = [
        (2 * hidden, width + LANES),
        (hidden, width + LANES),
        (2 * heads, width),
        (width, 2 * LANES),
        (width, LANES),
        (width, LANES),
        (2 * heads, LANES),
    ]
    return pl.pallas_call(
        unpack_kernel,
        grid_spec=pltpu.PrefetchScalarGridSpec(
            num_scalar_prefetch=1,
            grid=(1,),
            in_specs=[whole(*v.shape) for v in (pack, *fulls, used)],
            out_specs=[whole(*v) for v in shapes],
        ),
        out_shape=[jax.ShapeDtypeStruct(v, BF16) for v in shapes],
        compiler_params=params(20),
        cost_estimate=cost(1e5, 1e5),
        name="unpack",
    )(meta, pack, *fulls, used)


def out_forward_kernel(meta, near, far, weight, lower, upper_t, own, mate, latent, heads):
    rows, columns = own.shape[0], near.shape[1]
    for k, out in enumerate((own, mate)):
        at = pl.ds(pl.multiple_of(((meta[7] % 2) ^ k) * rows, rows), rows)
        both = jnp.concatenate([near[at, :], far[at, :]], 1)
        here = slice(k * rows, (k + 1) * rows)
        heads[here, :] = both
        select = adapter_select(meta, (meta[7] ^ k) * rows, rows, 1)
        lat = keep_low(select, nn(both, lower[...]))
        latent[here, :] = lat
        out[...] = (nn(both, weight[...]) + nt(lat, upper_t[...])).astype(BF16)


def out_forward(meta, near, far, weight, lower, upper_t):
    rows, columns = near.shape[0] // 2, near.shape[1]
    width = upper_t.shape[0]
    return pl.pallas_call(
        out_forward_kernel,
        grid_spec=pltpu.PrefetchScalarGridSpec(
            num_scalar_prefetch=1,
            grid=(1,),
            in_specs=[whole(*v.shape) for v in (near, far, weight, lower, upper_t)],
            out_specs=[
                whole(rows, width),
                whole(rows, width),
                whole(2 * rows, LANES),
                whole(2 * rows, 2 * columns),
            ],
        ),
        out_shape=[
            jax.ShapeDtypeStruct((rows, width), BF16),
            jax.ShapeDtypeStruct((rows, width), BF16),
            jax.ShapeDtypeStruct((2 * rows, LANES), BF16),
            jax.ShapeDtypeStruct((2 * rows, 2 * columns), BF16),
        ],
        compiler_params=params(14),
        cost_estimate=cost(1e5, 1e5),
        name="out_forward",
    )(meta, near, far, weight, lower, upper_t)


def out_backward_kernel(meta, grad_own, grad_mate, weight, lower, upper_t, mine, other, latent):
    rows, columns = grad_own.shape[0], mine.shape[1]
    for k, grad in enumerate((grad_own, grad_mate)):
        here = slice(k * rows, (k + 1) * rows)
        select = adapter_select(meta, (meta[7] ^ k) * rows, rows, 1)
        lat = keep_low(select, nn(grad[...], upper_t[...]))
        latent[here, :] = lat
        both = (nt(grad[...], weight[...]) + nt(lat, lower[...])).astype(BF16)
        mine[here, :] = both[:, :columns]
        other[here, :] = both[:, columns:]


def out_backward(meta, grad_own, grad_mate, weight, lower, upper_t):
    rows, width = grad_own.shape
    columns = lower.shape[0] // 2
    return pl.pallas_call(
        out_backward_kernel,
        grid_spec=pltpu.PrefetchScalarGridSpec(
            num_scalar_prefetch=1,
            grid=(1,),
            in_specs=[whole(*v.shape) for v in (grad_own, grad_mate, weight, lower, upper_t)],
            out_specs=[
                whole(2 * rows, columns),
                whole(2 * rows, columns),
                whole(2 * rows, LANES),
            ],
        ),
        out_shape=[
            jax.ShapeDtypeStruct((2 * rows, columns), BF16),
            jax.ShapeDtypeStruct((2 * rows, columns), BF16),
            jax.ShapeDtypeStruct((2 * rows, LANES), BF16),
        ],
        compiler_params=params(14),
        cost_estimate=cost(4 * rows * width * 640, 8e6),
        name="out_backward",
    )(meta, grad_own, grad_mate, weight, lower, upper_t)


def spread_shares(meta, turned, out, lanes):
    share = LANES // 4
    for mate in range(4):
        for p in range(SLABS):
            at = pl.multiple_of(p * LANES + (meta[7] ^ mate) * share, share)
            out[mate, p * share : (p + 1) * share, lanes] = turned[pl.ds(at, share), :]


def out_pairs_kernel(meta, heads, latent_grad, latent, grad_own, grad_mate, lower_out, upper_out, turned):
    rows = grad_own.shape[0]
    lower_out[...] = tn(latent_grad[...], heads[...]).T.astype(BF16)
    turned[...] = (
        (tn(latent[:rows], grad_own[...]) + tn(latent[rows:], grad_mate[...])).T
    ).astype(BF16)
    spread_shares(meta, turned, upper_out, slice(None))


def out_pairs(meta, heads, latent_grad, latent, grad_own, grad_mate):
    rows, width = grad_own.shape
    columns = heads.shape[1]
    return pl.pallas_call(
        out_pairs_kernel,
        grid_spec=pltpu.PrefetchScalarGridSpec(
            num_scalar_prefetch=1,
            grid=(1,),
            in_specs=[whole(*v.shape) for v in (heads, latent_grad, latent, grad_own, grad_mate)],
            out_specs=[whole(columns, LANES), whole(4, width // 4, LANES)],
            scratch_shapes=[pltpu.VMEM((width, LANES), BF16)],
        ),
        out_shape=[
            jax.ShapeDtypeStruct((columns, LANES), BF16),
            jax.ShapeDtypeStruct((4, width // 4, LANES), BF16),
        ],
        compiler_params=params(12),
        cost_estimate=cost(4 * rows * LANES * (columns + width), 5e6),
        name="out_pairs",
    )(meta, heads, latent_grad, latent, grad_own, grad_mate)


def ffn_kernel(
    first,
    meta,
    x0,
    x1,
    g0,
    g1,
    weight,
    down_weight,
    lower,
    down_upper_t,
    dx0,
    dx1,
    swiglu,
    pre_grads,
    latent,
    latent_grad,
    down_latent_grad,
):
    step = pl.program_id(0)
    rows = swiglu.shape[0]
    parts = x0.shape[0] // rows
    width, hidden = x0.shape[1], swiglu.shape[1]

    for k, (x_ref, g_ref, dx_ref) in enumerate(((x0, g0, dx0), (x1, g1, dx1))):

        @pl.when(step // parts == k)
        def _(k=k, x_ref=x_ref, g_ref=g_ref, dx_ref=dx_ref):
            part = step % parts
            at = pl.ds(pl.multiple_of(part * rows, rows), rows)
            first_row = (meta[7] ^ (first + k)) * (rows * parts) + part * rows
            select = adapter_select(meta, first_row, rows, 2)
            x = x_ref[at, :]
            grad = g_ref[at, :]
            lat = keep_low(select, nn(x, lower[...]))
            latent[...] = lat
            gate = nt(jnp.concatenate([x, lat[:, :LANES]], 1), weight[:hidden])
            up = nt(jnp.concatenate([x, lat[:, LANES:]], 1), weight[hidden:])
            down_lat = keep_low(select[:, :LANES], nn(grad, down_upper_t[...]))
            down_latent_grad[...] = down_lat
            wide_grad = nt(jnp.concatenate([grad, down_lat], 1), down_weight[...])
            sigmoid = 1.0 / (1.0 + jnp.exp(-gate))
            silu = gate * sigmoid
            swiglu[...] = (silu * up).astype(BF16)
            d_up = (wide_grad * silu).astype(BF16)
            d_gate = (wide_grad * up * (sigmoid * (1.0 + gate * (1.0 - sigmoid)))).astype(BF16)
            pre_grads[0] = d_gate
            pre_grads[1] = d_up
            lat_grad = keep_low(
                select,
                jnp.concatenate(
                    [nn(d_gate, weight[:hidden, width:]), nn(d_up, weight[hidden:, width:])], 1
                ),
            )
            latent_grad[...] = lat_grad
            dx_ref[at, :] = (
                nn(d_gate, weight[:hidden, :width])
                + nn(d_up, weight[hidden:, :width])
                + nt(lat_grad, lower[...])
            ).astype(BF16)


def ffn(meta, first, xs, grads, weight, down_weight, lower, down_upper_t):
    rows, width = xs[0].shape
    hidden = down_weight.shape[0]
    total = 2 * rows
    block = lambda columns: pl.BlockSpec((BLOCK, columns), lambda s, *_: (s, 0))
    return pl.pallas_call(
        functools.partial(ffn_kernel, first),
        grid_spec=pltpu.PrefetchScalarGridSpec(
            num_scalar_prefetch=1,
            grid=(total // BLOCK,),
            in_specs=[
                whole(*v.shape)
                for v in (*xs, *grads, weight, down_weight, lower, down_upper_t)
            ],
            out_specs=[whole(rows, width)] * 2
            + [
                block(hidden),
                pl.BlockSpec((2, BLOCK, hidden), lambda s, *_: (0, s, 0)),
                block(2 * LANES),
                block(2 * LANES),
                block(LANES),
            ],
        ),
        out_shape=[jax.ShapeDtypeStruct((rows, width), BF16)] * 2
        + [
            pltpu.HBM((total, hidden), BF16),
            pltpu.HBM((2, total, hidden), BF16),
            jax.ShapeDtypeStruct((total, 2 * LANES), BF16),
            jax.ShapeDtypeStruct((total, 2 * LANES), BF16),
            jax.ShapeDtypeStruct((total, LANES), BF16),
        ],
        compiler_params=params(28),
        cost_estimate=cost(2 * total * width * hidden * 6.0, 14e6),
        name="ffn",
    )(meta, *xs, *grads, weight, down_weight, lower, down_upper_t)


def ffn_rest_kernel(steps, meta, *refs):
    xs, grads, refs = refs[:4], refs[4:8], refs[8:]
    near, far, refs = refs[:5], refs[5:10], refs[10:]
    weight, upper_t = refs[:2]
    branches, refs = refs[2:6], refs[6:]
    sums_out, x_sum, gate_sum, up_sum, down_sum, branch_sum, turned = refs
    step = pl.program_id(0)
    hidden, rows = weight.shape[0], xs[0].shape[0]
    width = xs[0].shape[1]

    @pl.when(step == 0)
    def _():
        for total in (x_sum, gate_sum, up_sum, down_sum, branch_sum):
            total[...] = jnp.zeros_like(total)

    for k in range(4):

        @pl.when(step == k)
        def _(k=k):
            swiglu, pre_grads, latent, latent_grad, down_latent_grad = near if k < 2 else far
            wide = swiglu[...]
            select = adapter_select(meta, (meta[7] ^ k) * rows, rows, 1)
            lat = keep_low(select, nn(wide, weight[:, width:]))
            branches[k][...] = (nn(wide, weight[:, :width]) + nt(lat, upper_t[...])).astype(BF16)
            x_sum[...] += tn(latent_grad[...], xs[k][...])
            gate_sum[:, :hidden] += tn(latent[:, :LANES], pre_grads[0])
            up_sum[:, :hidden] += tn(latent[:, LANES:], pre_grads[1])
            down_sum[:, :hidden] += tn(down_latent_grad[...], wide)
            branch_sum[...] += tn(lat, grads[k][...])

    @pl.when(step == steps - 1)
    def _():
        turned[:, : 2 * LANES] = x_sum[...].T
        turned[:, 2 * LANES :] = branch_sum[...].T
        share, used = LANES // 4, hidden // SLABS
        for p in range(SLABS):
            for mate in range(4):
                at = pl.multiple_of(p * LANES + (meta[7] ^ mate) * share, share)
                for n in range(3):
                    to = (mate * 3 + n) * share
                    sums_out[p, to : to + share, :] = turned[
                        pl.ds(at, share), n * LANES : (n + 1) * LANES
                    ]
        for n, total in enumerate((gate_sum, up_sum, down_sum)):
            values = total[...].T
            for p in range(SLABS):
                to = 12 * share + n * used
                sums_out[p, to : to + used, :] = values[p * used : (p + 1) * used]


def ffn_rest(meta, xs, grads, near, far, weight, upper_t):
    rows, width = xs[0].shape
    hidden = weight.shape[0]
    padded = -(-hidden // LANES) * LANES
    operands = (*xs, *grads, *near, *far, weight, upper_t)

    def kept(values, first):
        step_of = lambda s: jnp.clip(s - first, 0, 1)
        if values.ndim == 3:
            return pl.BlockSpec((2, rows, hidden), lambda s, *_: (0, step_of(s), 0))
        return pl.BlockSpec((rows, values.shape[1]), lambda s, *_: (step_of(s), 0))

    return pl.pallas_call(
        functools.partial(ffn_rest_kernel, 4),
        grid_spec=pltpu.PrefetchScalarGridSpec(
            num_scalar_prefetch=1,
            grid=(4,),
            in_specs=[whole(*v.shape) for v in (*xs, *grads)]
            + [kept(v, 0) for v in near]
            + [kept(v, 2) for v in far]
            + [whole(*v.shape) for v in (weight, upper_t)],
            out_specs=[whole(rows, width)] * 4
            + [whole(SLABS, 3 * LANES + 3 * hidden // SLABS, LANES)],
            scratch_shapes=[
                pltpu.VMEM((2 * LANES, width), F32),
                pltpu.VMEM((LANES, padded), F32),
                pltpu.VMEM((LANES, padded), F32),
                pltpu.VMEM((LANES, padded), F32),
                pltpu.VMEM((LANES, width), F32),
                pltpu.VMEM((width, 3 * LANES), F32),
            ],
        ),
        out_shape=[jax.ShapeDtypeStruct((rows, width), BF16)] * 4
        + [jax.ShapeDtypeStruct((SLABS, 3 * LANES + 3 * hidden // SLABS, LANES), F32)],
        compiler_params=params(36),
        cost_estimate=cost(8 * rows * width * hidden * 2.3, 30e6),
        name="ffn_rest",
    )(meta, *operands)


def qkv_backward_kernel(first, meta, grads0, grads1, weight, lower, upper_t, dx0, dx1):
    rows = dx0.shape[0]
    for k, (grads, dx) in enumerate(((grads0, dx0), (grads1, dx1))):
        select = adapter_select(meta, (meta[7] ^ (first + k)) * rows, rows, 3)
        lat = keep_low(
            select, jnp.concatenate([nn(grads[m], upper_t[m]) for m in range(3)], 1)
        )
        total = nt(lat, lower[...])
        for m in range(3):
            total += nt(grads[m], weight[m])
        dx[...] = total.astype(BF16)


def qkv_backward(meta, first, rows, grads, weight, lower, upper_t):
    own = grads.shape[2]
    width = lower.shape[0]
    piece = lambda k: pl.BlockSpec((3, rows, own), lambda s, meta: (0, meta[7] ^ (first + k), 0))
    return pl.pallas_call(
        functools.partial(qkv_backward_kernel, first),
        grid_spec=pltpu.PrefetchScalarGridSpec(
            num_scalar_prefetch=1,
            grid=(1,),
            in_specs=[
                piece(0),
                piece(1),
                whole(*weight.shape),
                whole(*lower.shape),
                whole(*upper_t.shape),
            ],
            out_specs=[whole(rows, width)] * 2,
        ),
        out_shape=[jax.ShapeDtypeStruct((rows, width), BF16)] * 2,
        compiler_params=params(16),
        cost_estimate=cost(4 * rows * width * 50, 4e5),
        name="qkv_backward",
    )(meta, grads, grads, weight, lower, upper_t)


def qkv_pairs_kernel(steps, meta, normed, latent, grads, upper_t, lower_out, upper_out, low_sum, up_sum, turned):
    step = pl.program_id(0)
    rows = normed.shape[0]
    select = adapter_select(meta, step * rows, rows, 3)
    lat = keep_low(
        select, jnp.concatenate([nn(grads[m], upper_t[m]) for m in range(3)], 1)
    )

    @pl.when(step == 0)
    def _():
        low_sum[...] = jnp.zeros_like(low_sum)
        up_sum[...] = jnp.zeros_like(up_sum)

    low_sum[...] += tn(lat, normed[...])
    for m in range(3):
        up_sum[m] += tn(latent[:, m * LANES : (m + 1) * LANES], grads[m])

    @pl.when(step == steps - 1)
    def _():
        turned[...] = low_sum[...].T.astype(BF16)
        spread_shares(meta, turned, lower_out, slice(None))
        for m in range(3):
            upper_out[m] = up_sum[m].T.astype(BF16)


def qkv_pairs(meta, normed, latent, grads, upper_t):
    total, width = normed.shape
    own = grads.shape[2]
    rows = 1024
    steps = total // rows
    return pl.pallas_call(
        functools.partial(qkv_pairs_kernel, steps),
        grid_spec=pltpu.PrefetchScalarGridSpec(
            num_scalar_prefetch=1,
            grid=(steps,),
            in_specs=[
                pl.BlockSpec((rows, width), lambda s, *_: (s, 0)),
                pl.BlockSpec((rows, 3 * LANES), lambda s, *_: (s, 0)),
                pl.BlockSpec((3, rows, own), lambda s, *_: (0, s, 0)),
                whole(*upper_t.shape),
            ],
            out_specs=[whole(4, width // 4, 3 * LANES), whole(3, own, LANES)],
            scratch_shapes=[
                pltpu.VMEM((3 * LANES, width), F32),
                pltpu.VMEM((3, LANES, own), F32),
                pltpu.VMEM((width, 3 * LANES), BF16),
            ],
        ),
        out_shape=[
            jax.ShapeDtypeStruct((4, width // 4, 3 * LANES), BF16),
            jax.ShapeDtypeStruct((3, own, LANES), BF16),
        ],
        compiler_params=params(20),
        cost_estimate=cost(2 * total * width * 20, 4e5),
        name="qkv_pairs",
    )(meta, normed, latent, grads, upper_t)


def join_norm_kernel(stream, own, got, gain, hidden, normed):
    values = stream[...].astype(F32) + (own[...].astype(F32) + got[...].astype(F32))
    hidden[...] = values.astype(BF16)
    scale = lax.rsqrt(jnp.mean(values * values, -1, keepdims=True) + EPSILON)
    normed[...] = (values * scale * gain[...]).astype(BF16)


def join_norm(stream, own, got, gain):
    rows, width = stream.shape
    return pl.pallas_call(
        join_norm_kernel,
        grid=(1,),
        in_specs=[whole(*v.shape) for v in (stream, own, got, gain)],
        out_specs=[whole(rows, width)] * 2,
        out_shape=[
            jax.ShapeDtypeStruct((rows, width), BF16),
            jax.ShapeDtypeStruct((rows, width), BF16),
        ],
        compiler_params=params(12),
        cost_estimate=cost(1e5, 1e5),
        name="join_norm",
    )(stream, own, got, gain)


def norm_gradient_kernel(*refs):
    operands, (gain, out), (held, sems) = refs[:5], refs[5:7], refs[7:]
    copies = [
        pltpu.make_async_copy(ref, held.at[k], sems.at[k]) for k, ref in enumerate(operands)
    ]
    for copy in copies:
        copy.start()
    for copy in copies:
        copy.wait()
    straight, values, own, near, far = [held[k].astype(F32) for k in range(5)]
    grad = own + near + far
    inverse = lax.rsqrt(jnp.mean(values * values, -1, keepdims=True) + EPSILON)
    scaled = gain[...] * grad
    inner = jnp.mean(scaled * values, -1, keepdims=True)
    out[...] = (
        straight + (inverse * scaled - values * (inverse * inverse * inverse * inner))
    ).astype(BF16)


def norm_gradient(straight, values, own, near, far, gain, stay=False):
    rows, width = values.shape
    operands = [straight, values, own, near, far]
    operands = in_hbm(operands) if stay else operands
    place = pltpu.HBM if stay else pl.ANY
    return pl.pallas_call(
        norm_gradient_kernel,
        grid=(1,),
        in_specs=[pl.BlockSpec(memory_space=place)] * 5 + [whole(1, width)],
        out_specs=whole(rows, width),
        out_shape=jax.ShapeDtypeStruct((rows, width), BF16),
        scratch_shapes=[pltpu.VMEM((5, rows, width), BF16), pltpu.SemaphoreType.DMA((5,))],
        compiler_params=params(20),
        cost_estimate=cost(1e6, 9e6),
        name="norm_gradient",
    )(*operands, gain)


def swap(values, bit):
    size = lax.axis_size("tensor")
    return lax.ppermute(values, "tensor", [(i, i ^ bit) for i in range(size)])


def swap_dp(values, bits):
    size = lax.axis_size("dp")
    return lax.ppermute(values, "dp", [(i, i ^ bits) for i in range(size)])


def gather_tensor(values):
    far = swap(values, 2)
    return [values, swap(values, 1), far, swap(far, 1)]


def tensor_order(pieces, place):
    stacked = jnp.stack(pieces)
    for bit in (1, 2):
        moved = stacked.reshape((2, 2) + pieces[0].shape)[:, ::-1] if bit == 1 else (
            stacked.reshape((2, 2) + pieces[0].shape)[::-1]
        )
        stacked = jnp.where((place & bit) != 0, moved.reshape(stacked.shape), stacked)
    return stacked


def gather_slabs(values):
    near = [values] + [swap_dp(values, 2 * k) for k in (1, 2, 3)]
    result = []
    for piece in near:
        result += [piece, swap_dp(piece, 1)]
    return result


def pieces_dp(values):
    size = lax.axis_size("dp")
    if size != SLABS:
        exchanged = exchange_dp(values)
        return [exchanged[k] for k in range(size)]
    place = lax.axis_index("dp")
    sent = [lax.dynamic_index_in_dim(values, place ^ k, 0, keepdims=False) for k in range(size)]
    return sent[:1] + [swap_dp(sent[k], k) for k in range(1, size)]


def exchange_dp(values):
    return lax.all_to_all(values, "dp", split_axis=0, concat_axis=0, tiled=True)


def after(values, *earlier):
    return lax.optimization_barrier((values,) + earlier)[0]


def together(*values):
    return lax.optimization_barrier(values)


def per_device(
    tokens,
    cotangent,
    attention_gain,
    feedforward_gain,
    query_key_value_matrix,
    output_matrix,
    feedforward_matrix,
    down_matrix,
    memory_retention,
    memory_step_size,
    sequence_length,
    sequence_permutation,
    sequence_adapter,
    head_span_window,
    query_key_value_lower,
    query_key_value_upper,
    output_adapter_lower,
    output_adapter_upper,
    feedforward_adapter_lower,
    feedforward_adapter_upper,
    down_adapter_lower,
    down_adapter_upper,
):
    groups = lax.axis_size("dp")
    group = lax.axis_index("dp")
    place = lax.axis_index("tensor")
    quarter, width = tokens.shape
    slot = quarter // groups
    heads_own = query_key_value_matrix.shape[2]
    hidden = feedforward_matrix.shape[2]

    members = lax.dynamic_slice_in_dim(sequence_permutation, group * SEQ_G, SEQ_G)
    hits = members[:, None] == jnp.arange(sequence_length.shape[0], dtype=jnp.int32)[None, :]
    lengths = jnp.sum(jnp.where(hits, sequence_length[None, :], 0), 1)
    adapters = jnp.sum(jnp.where(hits, sequence_adapter[None, :], 0), 1)
    head_at = place * 2
    windows = lax.dynamic_slice_in_dim(head_span_window, head_at, 2)
    meta = jnp.concatenate(
        [
            jnp.stack([lengths[0], lengths[0] + lengths[1]]),
            adapters,
            windows,
            jnp.stack([place, group if groups == SLABS else jnp.zeros_like(group)]),
        ]
    ).astype(jnp.int32)
    fmeta = jnp.concatenate(
        [
            lax.dynamic_slice_in_dim(memory_retention, head_at, 2),
            lax.dynamic_slice_in_dim(memory_step_size, head_at, 2) / STRETCH,
        ]
    )
    spans = (2, 3, 4, 5)
    axes = ("dp", "tensor")
    tensors = lax.axis_size("tensor")
    to_user = [(j, (j % groups) * tensors + j // groups) for j in range(groups * tensors)]
    to_owner = [(b, a) for a, b in to_user]
    share = query_key_value_lower.shape[1]
    up_share = feedforward_adapter_upper.shape[2]
    turn = lambda values: jnp.swapaxes(values, -1, -2)

    def flat(*parts):
        return jnp.concatenate([v.reshape(-1, LANES) for v in parts], 0)

    fulls = (feedforward_adapter_lower, turn(output_adapter_upper), turn(down_adapter_upper))

    arrived = exchange_dp(tokens.reshape(groups, slot, width)).reshape(quarter, width)
    token_pieces = gather_tensor(arrived)
    if groups == SLABS:
        halves = jnp.moveaxis(
            query_key_value_matrix.reshape(3, width // groups, heads_own // LANES, LANES), 2, 0
        )
        pack = flat(
            halves,
            lax.ppermute(turn(query_key_value_upper), axes, to_user),
            query_key_value_lower,
            *fulls,
        )
        slabs = gather_slabs(pack)
        lower_rows = pack.shape[0] - 7 * share
        mates = gather_tensor(jnp.stack([v[lower_rows:] for v in slabs]))
    else:
        halves = lax.all_gather(query_key_value_matrix, "dp", axis=1, tiled=True)
        halves = jnp.moveaxis(halves.reshape(3, SLABS, LANES, heads_own // LANES, LANES), (1, 3), (0, 1))
        upper = lax.all_gather(lax.ppermute(turn(query_key_value_upper), axes, to_user), "dp", axis=1, tiled=True)
        upper = jnp.swapaxes(upper.reshape(3, SLABS, heads_own // SLABS, LANES), 0, 1)
        lower = lax.all_gather(query_key_value_lower, axes, axis=1, tiled=True)
        lower = jnp.moveaxis(lower.reshape(3, SLABS, 4, LANES // 4, LANES), (2, 1), (0, 1))
        lower = lower.reshape(4, SLABS, 3 * LANES // 4, LANES)
        at = lambda k: lax.dynamic_index_in_dim(lower, place ^ k, 0, keepdims=False)
        pack = jnp.concatenate(
            [v.reshape(SLABS, -1, LANES) for v in (halves, upper, at(0))], 1
        )
        slabs = [pack[k] for k in range(SLABS)]
        mates = [at(k) for k in range(4)]

    cot_arrived = exchange_dp(
        after(cotangent, mates[3]).reshape(groups, slot, width)
    ).reshape(quarter, width)
    wide = (turn(feedforward_matrix), down_matrix, output_matrix, swap(output_matrix, 2))
    out_lower_used, *users = [
        lax.ppermute(v, axes, to_user)
        for v in (output_adapter_lower, turn(feedforward_adapter_upper), down_adapter_lower)
    ]
    out_used = (out_lower_used, swap(out_lower_used, 2))
    if groups == SLABS:
        pack = after(flat(*wide, *out_used, *users), slabs[6])
        pack = lax.all_gather(pack, "dp", axis=0, tiled=False)

    gain_one = attention_gain.reshape(1, width)
    gain_two = feedforward_gain.reshape(1, width)
    normed, qkv, qkv_latent, qkv_w, qkv_a, qkv_b = project_qkv(
        meta, token_pieces, gain_one, slabs, mates, heads_own
    )
    attended, log_total = attend_forward(meta, qkv, spans)
    heads_near, heads_sent, states = memory_forward(meta, fmeta, qkv, attended)
    heads_far = swap(heads_sent, 2)
    cot_arrived = after(cot_arrived, heads_far)
    grad_mate, grad_far = swap(cot_arrived, 1), swap(cot_arrived, 2)
    grad_pieces = [cot_arrived, grad_mate, grad_far]
    if groups == SLABS:
        pack = after(pack, heads_near, cot_arrived)
        at = 3 * hidden + 2 * heads_own
        used = pack[:, at + 2 * share :].reshape(SLABS, 3, up_share, LANES)
        used = jnp.swapaxes(used, 0, 1).reshape(3, hidden, LANES)
        ffn_w, down_w, out_w, ffn_a, out_b, down_b, out_a = unpack(
            meta, pack, mates, used, hidden, heads_own
        )
    else:
        gathered = [lax.all_gather(v, "dp", axis=v.ndim - 1, tiled=True) for v in wide]
        ffn_a, out_b, down_b = [
            lax.all_gather(v, axes, axis=v.ndim - 2, tiled=True) for v in fulls
        ]
        ffn_a = jnp.concatenate([ffn_a[0], ffn_a[1]], 1)
        ffn_b, down_a, *out_a = [
            lax.all_gather(v, "dp", axis=v.ndim - 2, tiled=True) for v in (*users, *out_used)
        ]
        out_a = jnp.concatenate(out_a, 0)
        ffn_w = jnp.concatenate([gathered[0], ffn_b], 2).reshape(2 * hidden, width + LANES)
        down_w = jnp.concatenate([gathered[1], down_a], 1)
        out_w = jnp.concatenate(gathered[2:], 0)
    heads_far, grad_pieces[2] = together(heads_far, grad_pieces[2])
    branch_own, branch_mate, out_latent, heads = out_forward(
        meta, heads_near, heads_far, out_w, out_a, out_b
    )
    branch_got = swap(branch_mate, 1)
    hidden_one, normed_two = join_norm(arrived, branch_own, branch_got, gain_two)
    two = [normed_two, swap(normed_two, 1)]
    two_far = swap(normed_two, 2)

    two[0], grad_pieces[2] = together(two[0], grad_pieces[2])
    near = ffn(meta, 0, two, grad_pieces[:2], ffn_w, down_w, ffn_a, down_b)
    two_far = after(two_far, near[0])
    grad_pieces = grad_pieces + [swap(grad_pieces[2], 1)]
    two = two + [two_far, swap(two_far, 1)]
    far = ffn(meta, 2, two[2:], grad_pieces[2:], ffn_w, down_w, ffn_a, down_b)

    def first_step(far_mate, across):
        return (far_mate.astype(F32) + swap(across, 1).astype(F32)).astype(BF16)

    def second_step(own, mate, onward):
        return own.astype(F32) + swap(mate, 1).astype(F32) + swap(onward, 2).astype(F32)

    def scatter(own, mate, far_mate, across):
        return second_step(own, mate, first_step(far_mate, across))

    onward = first_step(far[0], far[1])
    onward, *far = together(onward, *far[2:])
    onward_far = swap(onward, 2)
    *branch, ffn_sums = ffn_rest(meta, two, grad_pieces, near[2:], far, down_w, down_b)
    onward_far, *branch = together(onward_far, *branch)
    grad_one = norm_gradient(
        cot_arrived, hidden_one, near[0], swap(near[1], 1), onward_far, gain_two
    )

    grad_mate = swap(grad_one, 1)
    head_grads, head_grads_sent, out_latent_grad = out_backward(
        meta, grad_one, grad_mate, out_w, out_a, out_b
    )
    head_grads_far = swap(head_grads_sent, 2)
    out_own, out_full = out_pairs(
        meta, heads, after(out_latent_grad, head_grads_sent), out_latent, grad_one, grad_mate
    )
    def reduce_pack(full_terms, own_terms):
        parts = scatter(*[full_terms[k] for k in range(4)]).astype(BF16)
        parts = parts.reshape(groups, share, full_terms.shape[2])
        parts = [
            parts[:, :, i * LANES : (i + 1) * LANES]
            for i in range(full_terms.shape[2] // LANES)
        ]
        return jnp.concatenate(parts + own_terms, 1)

    def reduced(exchanged, parts):
        summed = sum(v.astype(F32) for v in exchanged)
        cut = share * parts
        own = lax.ppermute(summed[cut:], axes, to_owner)
        return summed[:cut].reshape(parts, share, LANES), own

    def by_owner(values):
        return values.reshape(groups, values.shape[0] // groups, LANES)

    def regroup(values):
        if groups == SLABS:
            return values
        rows = values.reshape(4, SLABS, LANES // 4, values.shape[2])
        ordered = tensor_order([rows[k] for k in range(4)], place)
        ordered = jnp.swapaxes(ordered, 0, 1).reshape(groups, tensors, share, values.shape[2])
        at = lambda k: lax.dynamic_index_in_dim(ordered, place ^ k, 1, keepdims=False)
        return jnp.stack([at(k).reshape(groups * share, values.shape[2]) for k in range(4)])

    def by_dp(sums):
        if groups == SLABS:
            return sums
        parts = sums[:, : 3 * LANES].reshape(SLABS, 4, 3, LANES // 4, LANES)
        parts = tensor_order([parts[:, k] for k in range(4)], place)
        parts = jnp.moveaxis(parts, (1, 0, 3), (0, 1, 2)).reshape(groups, tensors, share, 3, LANES)
        at = lambda k: lax.dynamic_index_in_dim(parts, place ^ k, 1, keepdims=False)
        parts = [jnp.swapaxes(at(k), 1, 2).reshape(groups, -1, LANES) for k in range(4)]
        own = sums[:, 3 * LANES :].reshape(SLABS, 3, hidden // SLABS, LANES)
        own = jnp.swapaxes(own, 0, 1).reshape(3, groups, up_share, LANES)
        return jnp.concatenate(parts + [own[n] for n in range(3)], 1)

    ffn_sums = lax.psum_scatter(by_dp(ffn_sums), "dp", scatter_dimension=0, tiled=False)
    branch_onward = first_step(branch[2], branch[3])
    head_grads_far, branch_onward, out_own, out_full = together(
        head_grads_far, branch_onward, out_own, out_full
    )
    branch_far = swap(branch_onward, 2)
    branch_near = branch[0].astype(F32) + swap(branch[1], 1).astype(F32)
    qkv_grads = mixer_backward(
        meta, fmeta, qkv, head_grads, head_grads_far, attended, log_total, states, spans
    )
    qkv_grads, branch_far = together(qkv_grads, branch_far)

    far_terms = qkv_backward(meta, 2, quarter, qkv_grads, qkv_w, qkv_a, qkv_b)
    onward = first_step(*far_terms)
    branch_far = after(branch_far, far_terms[0])
    mixed_rows = (hidden_one.astype(F32) + (branch_near + branch_far.astype(F32))).astype(BF16)
    mixed_rows = after(mixed_rows, onward)
    mixed = exchange_dp(mixed_rows.reshape(groups, slot, width)).reshape(quarter, width)
    qkv_grads = after(qkv_grads, onward)
    onward_far = swap(onward, 2)
    near_terms = qkv_backward(meta, 0, quarter, qkv_grads, qkv_w, qkv_a, qkv_b)
    near_got = swap(near_terms[1], 1)
    qkv_full, qkv_own = qkv_pairs(
        meta, normed, qkv_latent, after(qkv_grads, near_terms[0]), qkv_b
    )
    onward_far, mixed = together(onward_far, mixed)
    grad_input = norm_gradient(
        grad_one, arrived, near_terms[0], near_got, onward_far, gain_one, True
    )
    token_grad = exchange_dp(grad_input.reshape(groups, slot, width)).reshape(quarter, width)
    qkv_full, qkv_own, out_own, out_full, _ = together(
        qkv_full, qkv_own, out_own, out_full, onward_far
    )
    out_mine, out_other = by_owner(out_own[:heads_own]), by_owner(out_own[heads_own:])
    out_mine = (out_mine.astype(F32) + swap(out_other, 2).astype(F32)).astype(BF16)
    qkv_pack = reduce_pack(
        regroup(jnp.concatenate([qkv_full, out_full], 2)),
        [by_owner(qkv_own[m]) for m in range(3)] + [out_mine],
    )
    qkv_full, qkv_own = reduced(pieces_dp(qkv_pack), 4)
    ffn_sums = after(ffn_sums, grad_input)
    ffn_parts = [ffn_sums[k * 3 * share : (k + 1) * 3 * share] for k in range(4)]
    ffn_onward = ffn_parts[2] + swap(ffn_parts[3], 1)
    ffn_full = ffn_parts[0] + swap(ffn_parts[1], 1) + swap(ffn_onward, 2)
    ffn_full = ffn_full.reshape(3, share, LANES)
    ffn_own = lax.ppermute(ffn_sums[12 * share :], axes, to_owner)
    ffn_own_parts = [ffn_own[i * up_share : (i + 1) * up_share] for i in range(3)]
    return (
        mixed,
        token_grad,
        qkv_full[:3],
        turn(qkv_own[: 3 * share].reshape(3, share, LANES)),
        qkv_own[3 * share :],
        qkv_full[3].T,
        ffn_full[:2],
        jnp.stack([ffn_own_parts[0].T, ffn_own_parts[1].T]),
        ffn_own_parts[2],
        ffn_full[2].T,
    )


def solution(mesh):
    both = ("dp", "tensor")
    rows = P(both, None)
    lower = P(None, both, None)
    upper = P(None, None, both)
    return jax.shard_map(
        per_device,
        mesh=mesh,
        in_specs=(
            rows,
            rows,
            P(),
            P(),
            P(None, "dp", "tensor"),
            P("tensor", "dp"),
            P(None, "dp", "tensor"),
            P("tensor", "dp"),
            P(),
            P(),
            P(),
            P(),
            P(),
            P(),
            lower,
            upper,
            rows,
            P(None, both),
            lower,
            upper,
            rows,
            P(None, both),
        ),
        out_specs=(
            rows,
            rows,
            lower,
            upper,
            rows,
            P(None, both),
            lower,
            upper,
            rows,
            P(None, both),
        ),
        check_vma=False,
    )
```
